32 devices in a mesh: fsdp: 8 (over z, core), seq: 4 (over y, x).
Axes of the slice: x: 2, y: 2, z: 4, core: 2. Of those that a mesh axis runs over, the one named last changes fastest.
Arguments:
- inputs: bfloat16 [8, 2048, 2048], P('fsdp', 'seq'), may hold values from -6 to 6
- cotangent: bfloat16 [8, 2048, 2048], P('fsdp', 'seq'), may hold values from -6 to 6
- segments: int32 [8, 2048], P('fsdp', 'seq'), may hold values from 0 to 10, as said below
- valid_mask: int32 [8, 2048], P('fsdp', 'seq'), may hold values from 0 to 1, as said below
- query_weight: bfloat16 [2048, 2048], P('fsdp'), may hold values from -0.125 to 0.125
- key_weight: bfloat16 [2048, 512], P('fsdp'), may hold values from -0.125 to 0.125
- value_weight: bfloat16 [2048, 512], P('fsdp'), may hold values from -0.125 to 0.125
- out_weight: bfloat16 [2048, 2048], P(None, 'fsdp'), may hold values from -2 to 2
- gate_weight: bfloat16 [2048, 8192], P('fsdp'), may hold values from -0.125 to 0.125
- up_weight: bfloat16 [2048, 8192], P('fsdp'), may hold values from -0.125 to 0.125
- down_weight: bfloat16 [8192, 2048], P(None, 'fsdp'), may hold values from -0.0625 to 0.0625
- attn_gain: bfloat16 [2048], P('fsdp'), may hold values from 0.5 to 1.5
- mlp_gain: bfloat16 [2048], P('fsdp'), may hold values from 0.5 to 1.5
Outputs:
- outputs: bfloat16 [8, 2048, 2048], P('fsdp', 'seq')
- input_grad: bfloat16 [8, 2048, 2048], P('fsdp', 'seq')
- query_grad: float32 [2048, 2048], P('fsdp')
- key_grad: float32 [2048, 512], P('fsdp')
- value_grad: float32 [2048, 512], P('fsdp')
- out_grad: float32 [2048, 2048], P(None, 'fsdp')
- gate_grad: float32 [2048, 8192], P('fsdp')
- up_grad: float32 [2048, 8192], P('fsdp')
- down_grad: float32 [8192, 2048], P(None, 'fsdp')
- attn_gain_grad: float32 [2048], P('fsdp')
- mlp_gain_grad: float32 [2048], P('fsdp')
- rms_stats: float32 [8, 5], P('fsdp')
The draws below stay inside these ranges and needn't reach their ends.
Inputs may be any that keep to these rules, and one draw needn't show every extreme that they name: `segments`: in each sequence the numbers start at 0, never fall and rise by one where a new document begins; every document but the last of its sequence holds 204 tokens or more. `valid_mask`: in each sequence the pads, if any, are its last tokens; most tokens are valid.
All inputs are finite; a program needn't handle non-finite values.
Results may differ from the reference program's by a relative error of at most 0.02.
Values may be sent and summed in bfloat16 or wider, within the bound.
No kernel may reach another device: no remote copies, remote signals or barrier semaphores. Data moves between devices by JAX's collectives and lax.ppermute only.
A program may use at most 704 MiB of HBM per device.

```python
import jax
import jax.numpy as jnp
from jax import lax

D = 2048
HEADS = 32
KV_HEADS = 8
HEAD_DIM = 64
FF = 8192
SEQ_LEN = 2048
ROWS = 512
SEQS = 8


def draw_segments(key, part):
    key = jax.random.fold_in(key, 11)
    class_key, length_key, pick_key = jax.random.split(key, 3)
    shortest = max(2, SEQ_LEN // 10)
    most_docs = SEQ_LEN // shortest + 1
    classes = jax.random.randint(class_key, (SEQS, most_docs), 1, 4)
    widest = shortest * jnp.left_shift(jnp.ones((SEQS, most_docs), jnp.int32), classes)
    lengths = jax.random.randint(length_key, (SEQS, most_docs), shortest, widest + 1)
    ends = jnp.cumsum(lengths, axis=1)
    places = jnp.arange(SEQ_LEN, dtype=jnp.int32)
    numbers = jnp.sum((ends[:, None, :] <= places[None, :, None]).astype(jnp.int32), axis=2)
    single = jax.random.randint(pick_key, (), 0, SEQS)
    finest = (single + 1) % SEQS
    rows = jnp.arange(SEQS, dtype=jnp.int32)[:, None]
    numbers = jnp.where(rows == finest, (places // shortest)[None, :], numbers)
    numbers = jnp.where(rows == single, 0, numbers)
    return numbers.astype(jnp.int32)


def draw_valid_mask(key, part):
    key = jax.random.fold_in(key, 23)
    padding = jax.random.randint(key, (SEQS, 1), 0, ROWS // 2)
    places = jnp.arange(SEQ_LEN, dtype=jnp.int32)[None, :]
    return jnp.where(places < SEQ_LEN - padding, 1, 0).astype(jnp.int32)


def levels(rng, extent, pieces, least, high):
    loudness = 1.0
    for axis_at, shards_of in pieces:
        heights = jax.random.uniform(jax.random.fold_in(jax.random.fold_in(rng, 6), axis_at), (shards_of,), jnp.float32, least / len(pieces), high / len(pieces))
        loudness = loudness * jnp.repeat(jnp.exp(heights), extent[axis_at] // shards_of).reshape((-1,) + (1,) * (len(extent) - 1 - axis_at))
    return loudness


def scatter_about(key, shape, deviation, reach, cuts=(), kind=jnp.bfloat16):
    result = deviation * jax.random.normal(key, shape, jnp.float32)
    if cuts:
        result = result * levels(key, shape, cuts, -0.22, 0.18)
    return jnp.clip(result, -reach, reach).astype(kind)


def setup_inputs(seed: int = 0) -> dict:
    key_of = jax.random.split(jax.random.key(seed), 14)
    return {
        "inputs": scatter_about(key_of[0], (SEQS, SEQ_LEN, D), 1.0, 6.0, ((0, 8), (1, 4))),
        "cotangent": scatter_about(key_of[1], (SEQS, SEQ_LEN, D), 1.0, 6.0, ((0, 8), (1, 4))),
        "segments": draw_segments(jax.random.fold_in(key_of[13], 71), 0),
        "valid_mask": draw_valid_mask(jax.random.fold_in(key_of[13], 71), 0),
        "query_weight": scatter_about(key_of[4], (D, HEADS * HEAD_DIM), D ** -0.5, 0.125, ((0, 8),)),
        "key_weight": scatter_about(key_of[5], (D, KV_HEADS * HEAD_DIM), D ** -0.5, 0.125, ((0, 8),)),
        "value_weight": scatter_about(key_of[6], (D, KV_HEADS * HEAD_DIM), D ** -0.5, 0.125, ((0, 8),)),
        "out_weight": scatter_about(key_of[7], (HEADS * HEAD_DIM, D), (max(1, D // 256)) ** -0.5, 2.0, ((1, 8),)),
        "gate_weight": scatter_about(key_of[8], (D, FF), D ** -0.5, 0.125, ((0, 8),)),
        "up_weight": scatter_about(key_of[9], (D, FF), D ** -0.5, 0.125, ((0, 8),)),
        "down_weight": scatter_about(key_of[10], (FF, D), FF ** -0.5, 0.0625, ((1, 8),)),
        "attn_gain": jnp.clip(1.0 + 0.1 * jax.random.normal(key_of[11], (D,), jnp.float32), 0.5, 1.5).astype(jnp.bfloat16),
        "mlp_gain": jnp.clip(1.0 + 0.1 * jax.random.normal(key_of[12], (D,), jnp.float32), 0.5, 1.5).astype(jnp.bfloat16),
    }


EPSILON = 1e-05
ROPE_BASE = 500000.0
NEGATIVE = -1e+30
HIGHEST_PRECISION = lax.Precision.HIGHEST

@jax.custom_vjp
def low(v):
    return lax.optimization_barrier(v.astype(jnp.bfloat16)).astype(jnp.float32)

@jax.custom_vjp
def low_back(v):
    return v

def low_keep(v):
    return (low(v), None)

def low_pass(kept, grad):
    return (grad,)

def back_keep(v):
    return (v, None)

def back_low(kept, grad):
    return (low(grad),)
low.defvjp(low_keep, low_pass)
low_back.defvjp(back_keep, back_low)

def matmul(left_side, right_side):
    return jnp.dot(left_side, right_side, precision=HIGHEST_PRECISION, preferred_element_type=jnp.float32)

def norm_scale(values):
    return lax.rsqrt(lax.optimization_barrier(jnp.mean(values * values, axis=-1, keepdims=True)) + EPSILON)

def doc_positions(segment_ids):
    length = segment_ids.shape[0]
    places = jnp.arange(length, dtype=jnp.int32)
    boundary = jnp.concatenate([jnp.ones((1,), jnp.bool_), segment_ids[1:] != segment_ids[:-1]])
    starts = lax.cummax(jnp.where(boundary, places, 0).astype(jnp.int32), axis=0)
    return places - starts

def rotate(values, places, head_count, direction):
    length = values.shape[0]
    half_dim = HEAD_DIM // 2
    per_head = values.reshape(length, head_count, HEAD_DIM)
    frequency = ROPE_BASE ** (-2.0 * jnp.arange(half_dim, dtype=jnp.float32) / HEAD_DIM)
    angles = places.astype(jnp.float32)[:, None] * frequency[None, :]
    cosine = jnp.cos(angles)[:, None, :]
    sine_part = direction * jnp.sin(angles)[:, None, :]
    first_half = per_head[..., :half_dim]
    second_half = per_head[..., half_dim:]
    turned = jnp.concatenate([first_half * cosine - second_half * sine_part, second_half * cosine + first_half * sine_part], axis=-1)
    return turned.reshape(length, head_count * HEAD_DIM)

def visible(block_start, block_rows, segment_ids, valid_ids):
    length = segment_ids.shape[0]
    query_pos = block_start + jnp.arange(block_rows, dtype=jnp.int32)
    key_pos = jnp.arange(length, dtype=jnp.int32)
    query_seg = lax.dynamic_slice_in_dim(segment_ids, block_start, block_rows, 0)
    query_valid = lax.dynamic_slice_in_dim(valid_ids, block_start, block_rows, 0)
    allowed = (query_seg[:, None] == segment_ids[None, :]) & (key_pos[None, :] <= query_pos[:, None]) & (query_valid[:, None] == 1)
    return allowed | (key_pos[None, :] == query_pos[:, None])

def attention(queries, keys, values, segment_ids, valid_ids):
    length = queries.shape[0]
    group = HEADS // KV_HEADS
    query_four = queries.reshape(length, KV_HEADS, group, HEAD_DIM)
    key_three = keys.reshape(length, KV_HEADS, HEAD_DIM)
    value_three = values.reshape(length, KV_HEADS, HEAD_DIM)
    block_rows = min(512, length)

    def one_block(index):
        block_start = (index * block_rows).astype(jnp.int32)
        query_block = lax.dynamic_slice_in_dim(query_four, block_start, block_rows, 0)
        scores = jnp.einsum('qkgd,skd->kgqs', query_block, key_three, precision=HIGHEST_PRECISION) * HEAD_DIM ** (-0.5)
        allowed = visible(block_start, block_rows, segment_ids, valid_ids)
        scores = low_back(jnp.where(allowed[None, None], scores, NEGATIVE))
        probs = low(jax.nn.softmax(scores, axis=-1))
        return jnp.einsum('kgqs,skd->qkgd', probs, value_three, precision=HIGHEST_PRECISION)
    outputs = lax.map(jax.checkpoint(one_block), jnp.arange(length // block_rows, dtype=jnp.int32))
    return outputs.reshape(length, HEADS * HEAD_DIM)

def layer(tokens, params, segment_ids, valid_ids):
    query_weight, key_weight, value_weight, out_weight, gate_weight, up_weight, down_weight, attn_gain, mlp_gain = params
    places = doc_positions(segment_ids)
    inv_one = norm_scale(tokens)
    normed_one = low(tokens * inv_one * attn_gain)
    query_lin = low_back(matmul(normed_one, query_weight))
    key_lin = low_back(matmul(normed_one, key_weight))
    value_lin = matmul(normed_one, value_weight)
    query_low = low(low_back(rotate(query_lin, places, HEADS, 1.0)))
    key_low = low(low_back(rotate(key_lin, places, KV_HEADS, 1.0)))
    value_low = low(low_back(value_lin))
    heads_out = low(low_back(attention(query_low, key_low, value_low, segment_ids, valid_ids)))
    attn_branch = low_back(matmul(heads_out, out_weight))
    middle = tokens + attn_branch
    inv_two = norm_scale(middle)
    normed_two = low(middle * inv_two * mlp_gain)
    gate_lin = low_back(matmul(normed_two, gate_weight))
    up_lin = low_back(matmul(normed_two, up_weight))
    activated = low(jax.nn.silu(gate_lin) * up_lin)
    mlp_branch = low_back(matmul(activated, down_weight))
    final = middle + mlp_branch
    return (final, (middle, attn_branch, mlp_branch))

def reference(inputs, cotangent, segments, valid_mask, query_weight, key_weight, value_weight, out_weight, gate_weight, up_weight, down_weight, attn_gain, mlp_gain):
    weights = tuple((weight.astype(jnp.float32) for weight in (query_weight, key_weight, value_weight, out_weight, gate_weight, up_weight, down_weight, attn_gain, mlp_gain)))
    zeros = tuple((jnp.zeros(weight.shape, jnp.float32) for weight in weights))

    def per_sequence(totals, items):
        token_rows, cotan_rows, segment_ids, valid_ids = items

        def forward(tokens, *param_list):
            return layer(tokens, param_list, segment_ids, valid_ids)
        tokens = token_rows.astype(jnp.float32)
        final, pullback, kept = jax.vjp(forward, tokens, *weights, has_aux=True)
        middle, attn_branch, mlp_branch = kept
        valid_rows = valid_ids.astype(jnp.float32)
        grads = pullback(cotan_rows.astype(jnp.float32) * valid_rows[:, None])
        totals = tuple((total + grad_part for total, grad_part in zip(totals, grads[1:])))
        count = jnp.sum(valid_rows)

        def root_mean(values):
            return jnp.sqrt(jnp.sum(valid_rows[:, None] * values * values) / (count * D))
        stats = jnp.stack([root_mean(tokens), root_mean(middle), root_mean(final), root_mean(attn_branch), root_mean(mlp_branch)])
        return (totals, (final.astype(jnp.bfloat16), grads[0].astype(jnp.bfloat16), stats))
    totals, results = lax.scan(per_sequence, zeros, (inputs, cotangent, segments, valid_mask))
    outputs, input_grad, rms_stats = results
    return (outputs, input_grad, totals[0], totals[1], totals[2], totals[3], totals[4], totals[5], totals[6], totals[7], totals[8], rms_stats)
```

```python
import functools

import jax
import jax.numpy as jnp
from jax import lax
from jax.experimental import pallas as pl
from jax.experimental.pallas import tpu as pltpu
from jax.sharding import PartitionSpec as P

D = 2048
HEADS = 32
KV_HEADS = 8
HEAD_DIM = 64
GROUP = HEADS // KV_HEADS
FF = 8192
EPSILON = 1e-05
ROPE_BASE = 500000.0
NEGATIVE = -1e30
SCALE = HEAD_DIM**-0.5
BF = jnp.bfloat16
F32 = jnp.float32
LANES = 128
VMEM_LIMIT = 60 * 1024 * 1024
NT = (((1,), (1,)), ((), ()))
NN = (((1,), (0,)), ((), ()))
TN = (((0,), (0,)), ((), ()))


def dot(left, right, dims=NN):
    return lax.dot_general(left, right, dims, preferred_element_type=F32)


def params(grid_rank):
    return pltpu.CompilerParams(
        dimension_semantics=("arbitrary",) * grid_rank, vmem_limit_bytes=VMEM_LIMIT
    )


def swap(values, bit):
    count = lax.axis_size("seq")
    return lax.ppermute(values, "seq", [(i, i ^ bit) for i in range(count)])


def bit_orders():
    bits = [1 << b for b in range(lax.axis_size("seq").bit_length() - 1)]
    return bits, bits[::-1]


def gather_stream(block, order):
    held, owners = block[None], [0]
    for bit in order:
        held = jnp.concatenate([held, swap(held, bit)], axis=0)
        owners = owners + [k ^ bit for k in owners]
    return [held[owners.index(k)] for k in range(len(owners))]


def gather_seq(block):
    half = block.shape[-1] // 2
    low_order, high_order = bit_orders()
    low = gather_stream(block[..., :half], low_order)
    high = gather_stream(block[..., half:], high_order)
    return [jnp.concatenate(pair, axis=-1) for pair in zip(low, high)]


def reduce_stream(blocks, order):
    held = {k: b for k, b in enumerate(blocks)}
    for bit in order:
        away = sorted(k for k in held if k & bit)
        sent = swap(jnp.stack([held[k].astype(BF) for k in away]), bit)
        held = {
            k: held[k].astype(F32) + sent[away.index(k ^ bit)].astype(F32)
            for k in held
            if not k & bit
        }
    return held[0]


def reduce_seq(blocks):
    half = blocks[0].shape[-1] // 2
    low_order, high_order = bit_orders()
    low = reduce_stream([b[..., :half] for b in blocks], low_order)
    high = reduce_stream([b[..., half:] for b in blocks], high_order)
    return jnp.concatenate([low, high], axis=-1)


def exchange_seq(blocks):
    return [b if k == 0 else swap(b, k) for k, b in enumerate(blocks)]


def gather_fsdp(shard):
    return lax.all_gather(shard, "fsdp", axis=0, tiled=True)


def scatter_fsdp(values):
    return lax.psum_scatter(values, "fsdp", scatter_dimension=0, tiled=True)


def turn(values, cosine, sine):
    lane = lax.broadcasted_iota(jnp.int32, values.shape, 1)
    half = HEAD_DIM // 2
    ahead = pltpu.roll(values, LANES - half, 1)
    behind = pltpu.roll(values, half, 1)
    return values * cosine + jnp.where(lane % HEAD_DIM < half, ahead, behind) * sine


def project_kernel(kv_local, x_ref, gain_ref, w_ref, cos_ref, sin_ref, normed_ref, q_ref, k_ref, v_ref):
    x = x_ref[...].astype(F32)
    inv = lax.rsqrt(jnp.mean(x * x, axis=-1, keepdims=True) + EPSILON)
    normed = (x * inv * gain_ref[...]).astype(BF)
    normed_ref[...] = normed
    q_width = kv_local * GROUP * HEAD_DIM
    kv_width = kv_local * HEAD_DIM
    lin = dot(normed, w_ref[:, : q_width + 2 * kv_width])
    cosine, sine = cos_ref[...], sin_ref[...]
    for start in range(0, q_width, LANES):
        part = turn(lin[:, start : start + LANES], cosine, sine) * SCALE
        q_ref[:, start : start + LANES] = part.astype(BF)
    for start in range(0, kv_width, LANES):
        part = turn(lin[:, q_width + start : q_width + start + LANES], cosine, sine)
        for at in range(0, min(LANES, kv_width - start), HEAD_DIM):
            k_ref[(start + at) // HEAD_DIM] = part[:, at : at + HEAD_DIM].astype(BF)
    for head in range(kv_local):
        start = q_width + kv_width + head * HEAD_DIM
        v_ref[head] = lin[:, start : start + HEAD_DIM].astype(BF)


def project(x, gain_row, weight, cosine, sine, kv_local):
    rows = x.shape[0]
    block = 256
    q_width = kv_local * GROUP * HEAD_DIM
    by_row = lambda i: (i, 0)
    whole = lambda i: (0, 0)
    by_head = lambda i: (0, i, 0)
    return pl.pallas_call(
        functools.partial(project_kernel, kv_local),
        grid=(rows // block,),
        in_specs=[
            pl.BlockSpec((block, D), by_row),
            pl.BlockSpec((1, D), whole),
            pl.BlockSpec(weight.shape, whole),
            pl.BlockSpec((block, LANES), by_row),
            pl.BlockSpec((block, LANES), by_row),
        ],
        out_specs=[
            pl.BlockSpec((block, D), by_row),
            pl.BlockSpec((block, q_width), by_row),
            pl.BlockSpec((kv_local, block, HEAD_DIM), by_head),
            pl.BlockSpec((kv_local, block, HEAD_DIM), by_head),
        ],
        out_shape=[
            jax.ShapeDtypeStruct((rows, D), BF),
            jax.ShapeDtypeStruct((rows, q_width), BF),
            jax.ShapeDtypeStruct((kv_local, rows, HEAD_DIM), BF),
            jax.ShapeDtypeStruct((kv_local, rows, HEAD_DIM), BF),
        ],
        compiler_params=params(1),
        cost_estimate=pl.CostEstimate(
            flops=2 * rows * D * weight.shape[1], bytes_accessed=rows * D * 6, transcendentals=0
        ),
        name="project",
    )(x, gain_row, weight, cosine, sine)


def pair_bias(rows, query_index, key_index, query_row, key_col):
    key_pos = key_index * rows + lax.broadcasted_iota(jnp.int32, (rows, rows), 0)
    query_pos = query_index * rows + lax.broadcasted_iota(jnp.int32, (rows, rows), 1)
    allowed = ((key_col == query_row) & (key_pos <= query_pos)) | (key_pos == query_pos)
    return jnp.where(allowed, 0.0, NEGATIVE)


def attend_kernel(rows, me_ref, q_ref, k_ref, v_ref, query_row_ref, key_col_ref, out_ref, total_ref, v_t, peak, total, acc):
    index = pl.program_id(1)
    me = me_ref[0]

    @pl.when(index == 0)
    def _():
        v_t[...] = v_ref[0].astype(F32).T.astype(BF)

    peak[...] = jnp.full(peak.shape, NEGATIVE, F32)
    total[...] = jnp.zeros(total.shape, F32)
    acc[...] = jnp.zeros(acc.shape, F32)

    def step(j, _):
        at = pl.multiple_of((j ^ me) * rows, rows)
        keys = k_ref[0, pl.ds(at, rows), :]
        values_t = v_t[:, pl.ds(at, rows)]
        bias = pair_bias(rows, index, j, query_row_ref[...], key_col_ref[pl.ds(at, rows), :])
        for head in range(GROUP):
            query = q_ref[:, head * HEAD_DIM : (head + 1) * HEAD_DIM]
            scores = dot(keys, query, NT) + bias
            old = peak[head : head + 1, :]
            new = jnp.maximum(old, jnp.max(scores, axis=0, keepdims=True))
            expo = jnp.exp(scores - new)
            fade = jnp.exp(old - new)
            peak[head : head + 1, :] = new
            total[head : head + 1, :] = total[head : head + 1, :] * fade + jnp.sum(expo, axis=0, keepdims=True)
            acc[head] = acc[head] * fade + dot(values_t, expo.astype(BF))
        return 0

    lax.fori_loop(0, index + 1, step, 0)
    for head in range(GROUP):
        out = acc[head] / total[head : head + 1, :]
        out_ref[:, head * HEAD_DIM : (head + 1) * HEAD_DIM] = out.T.astype(BF)
    total_ref[0] = peak[...] + jnp.log(total[...])


def attend(me, q, k, v, query_row, key_col, rows):
    kv_local, length = k.shape[0], k.shape[1]
    count = length // rows
    width = GROUP * HEAD_DIM
    return pl.pallas_call(
        functools.partial(attend_kernel, rows),
        grid_spec=pltpu.PrefetchScalarGridSpec(
            num_scalar_prefetch=1,
            grid=(kv_local, count),
            in_specs=[
                pl.BlockSpec((rows, width), lambda g, i, me: (i ^ me[0], g)),
                pl.BlockSpec((1, length, HEAD_DIM), lambda g, i, me: (g, 0, 0)),
                pl.BlockSpec((1, length, HEAD_DIM), lambda g, i, me: (g, 0, 0)),
                pl.BlockSpec((1, rows), lambda g, i, me: (0, i ^ me[0])),
                pl.BlockSpec((length, 1), lambda g, i, me: (0, 0)),
            ],
            out_specs=[
                pl.BlockSpec((rows, width), lambda g, i, me: (i ^ me[0], g)),
                pl.BlockSpec((1, GROUP, rows), lambda g, i, me: (g, 0, i ^ me[0])),
            ],
            scratch_shapes=[
                pltpu.VMEM((HEAD_DIM, length), BF),
                pltpu.VMEM((GROUP, rows), F32),
                pltpu.VMEM((GROUP, rows), F32),
                pltpu.VMEM((GROUP, HEAD_DIM, rows), F32),
            ],
        ),
        out_shape=[
            jax.ShapeDtypeStruct((length, kv_local * width), BF),
            jax.ShapeDtypeStruct((kv_local, GROUP, length), F32),
        ],
        compiler_params=params(2),
        cost_estimate=pl.CostEstimate(
            flops=kv_local * GROUP * length * length * HEAD_DIM * 8, bytes_accessed=1 << 24, transcendentals=0
        ),
        name="attend",
    )(me, q, k, v, query_row, key_col)


def attend_back_kernel(
    rows, count, me_ref, q_ref, k_ref, v_ref, out_ref, grad_ref, total_ref, query_row_ref, key_col_ref,
    cos_ref, sin_ref, cos_t_ref, sin_t_ref, dq_ref, dk_ref, dv_ref, k_t, inner, dq_t, dk_acc, dv_acc,
):
    me = me_ref[0]
    half = HEAD_DIM // 2
    k_t[...] = k_ref[0].astype(F32).T.astype(BF)
    dq_t[...] = jnp.zeros(dq_t.shape, F32)

    def prepare(i, _):
        here = pl.ds(pl.multiple_of(i * rows, rows), rows)
        for head in range(GROUP):
            cols = slice(head * HEAD_DIM, (head + 1) * HEAD_DIM)
            both = out_ref[here, cols].astype(F32) * grad_ref[here, cols].astype(F32)
            inner[head : head + 1, here] = jnp.sum(both.T, axis=0, keepdims=True)
        return 0

    lax.fori_loop(0, count, prepare, 0)

    def key_step(j, _):
        key_at = pl.ds(pl.multiple_of((j ^ me) * rows, rows), rows)
        keys, values = k_ref[0, key_at, :], v_ref[0, key_at, :]
        keys_t = k_t[:, key_at]
        key_col = key_col_ref[key_at, :]
        dk_acc[...] = jnp.zeros(dk_acc.shape, F32)
        dv_acc[...] = jnp.zeros(dv_acc.shape, F32)

        def query_step(i, _):
            at = pl.ds(pl.multiple_of((i ^ me) * rows, rows), rows)
            bias = pair_bias(rows, i, j, query_row_ref[:, at], key_col)
            for head in range(GROUP):
                cols = slice(head * HEAD_DIM, (head + 1) * HEAD_DIM)
                query, grad = q_ref[at, cols], grad_ref[at, cols]
                probs = jnp.exp(dot(keys, query, NT) + bias - total_ref[0, head : head + 1, at])
                dv_acc[...] += dot(probs.astype(BF), grad)
                grad_probs = dot(values, grad, NT)
                grad_scores = (probs * (grad_probs - inner[head : head + 1, at])).astype(BF)
                dk_acc[...] += dot(grad_scores, query)
                dq_t[head, :, at] += dot(keys_t, grad_scores)
            return 0

        lax.fori_loop(j, count, query_step, 0)
        dk = dk_acc[...]
        low, high = dk[:, :half], dk[:, half:]
        cosine, sine = cos_ref[key_at, :half], sin_ref[key_at, half:HEAD_DIM]
        dk_ref[0, key_at, :] = jnp.concatenate(
            [low * cosine + high * sine, high * cosine - low * sine], axis=1
        ).astype(BF)
        dv_ref[0, key_at, :] = dv_acc[...].astype(BF)
        return 0

    lax.fori_loop(0, count, key_step, 0)

    def finish(i, _):
        here = pl.ds(pl.multiple_of(i * rows, rows), rows)
        cosine, sine = cos_t_ref[:, here], sin_t_ref[:, here]
        for head in range(GROUP):
            low, high = dq_t[head, :half, here], dq_t[head, half:, here]
            turned = jnp.concatenate([low * cosine + high * sine, high * cosine - low * sine], axis=0) * SCALE
            dq_ref[here, head * HEAD_DIM : (head + 1) * HEAD_DIM] = turned.T.astype(BF)
        return 0

    lax.fori_loop(0, count, finish, 0)


def attend_back(me, q, k, v, out, grad, totals, query_row, key_col, cosine, sine, cosine_t, sine_t, rows):
    kv_local, length = k.shape[0], k.shape[1]
    width = GROUP * HEAD_DIM
    by_group = pl.BlockSpec((length, width), lambda g, me: (0, g))
    by_head = pl.BlockSpec((1, length, HEAD_DIM), lambda g, me: (g, 0, 0))
    whole = lambda shape: pl.BlockSpec(shape, lambda g, me: (0, 0))
    return pl.pallas_call(
        functools.partial(attend_back_kernel, rows, length // rows),
        grid_spec=pltpu.PrefetchScalarGridSpec(
            num_scalar_prefetch=1,
            grid=(kv_local,),
            in_specs=[
                by_group,
                by_head,
                by_head,
                by_group,
                by_group,
                pl.BlockSpec((1, GROUP, length), lambda g, me: (g, 0, 0)),
                whole((1, length)),
                whole((length, 1)),
                whole((length, LANES)),
                whole((length, LANES)),
                whole((HEAD_DIM // 2, length)),
                whole((HEAD_DIM // 2, length)),
            ],
            out_specs=[by_group, by_head, by_head],
            scratch_shapes=[
                pltpu.VMEM((HEAD_DIM, length), BF),
                pltpu.VMEM((GROUP, length), F32),
                pltpu.VMEM((GROUP, HEAD_DIM, length), F32),
                pltpu.VMEM((rows, HEAD_DIM), F32),
                pltpu.VMEM((rows, HEAD_DIM), F32),
            ],
        ),
        out_shape=[
            jax.ShapeDtypeStruct((length, kv_local * width), BF),
            jax.ShapeDtypeStruct((kv_local, length, HEAD_DIM), BF),
            jax.ShapeDtypeStruct((kv_local, length, HEAD_DIM), BF),
        ],
        compiler_params=params(1),
        cost_estimate=pl.CostEstimate(
            flops=kv_local * GROUP * length * length * HEAD_DIM * 20, bytes_accessed=1 << 24, transcendentals=0
        ),
        name="attend_back",
    )(me, q, k, v, out, grad, totals, query_row, key_col, cosine, sine, cosine_t, sine_t)


def norm_scale(values):
    return lax.rsqrt(jnp.mean(values * values, axis=-1, keepdims=True) + EPSILON)


def norm_back(grad_normed, values, inv_rms, gain_row):
    unit_rows = values * inv_rms
    scaled = grad_normed * gain_row
    return inv_rms * (scaled - unit_rows * jnp.mean(scaled * unit_rows, axis=-1, keepdims=True))


def blocks_of(values, count):
    rows = values.shape[0] // count
    return [values[k * rows : (k + 1) * rows] for k in range(count)]


def whole_columns(blocks, me):
    stacked = jnp.stack(blocks)
    ordered = [
        lax.dynamic_index_in_dim(stacked, p ^ me, 0, keepdims=False) for p in range(len(blocks))
    ]
    return jnp.concatenate(ordered, axis=1).astype(F32)


def body(
    inputs, cotangent, segments, valid_mask, query_weight, key_weight, value_weight, out_weight,
    gate_weight, up_weight, down_weight, attn_gain, mlp_gain,
):
    count = lax.axis_size("seq")
    me = lax.axis_index("seq")
    me_row = me.reshape(1).astype(jnp.int32)
    rows = inputs.shape[1]
    length = rows * count
    kv_local = KV_HEADS // count
    q_width = kv_local * GROUP * HEAD_DIM
    kv_width = kv_local * HEAD_DIM
    ff_local = FF // count
    shard_rows = gate_weight.shape[0]

    def mine(weight, width, axis=1):
        return lax.dynamic_slice_in_dim(weight, me * width, width, axis)

    gains = jnp.pad(jnp.stack([attn_gain, mlp_gain], axis=1), ((0, 0), (0, LANES - 2)))
    qkv_shard = jnp.concatenate(
        [mine(query_weight, q_width), mine(key_weight, kv_width), mine(value_weight, kv_width), gains], axis=1
    )
    qkv_full = gather_fsdp(qkv_shard)
    out_slice = gather_fsdp(mine(out_weight, q_width, 0).T)
    down_t = gather_fsdp(mine(down_weight, ff_local, 0).T)
    gate_up = gather_fsdp(jnp.concatenate([mine(gate_weight, ff_local), mine(up_weight, ff_local)], axis=1))
    gain_one = qkv_full[:, q_width + 2 * kv_width].astype(F32).reshape(1, D)
    gain_two = qkv_full[:, q_width + 2 * kv_width + 1].astype(F32).reshape(1, D)
    qkv_weight = qkv_full[:, : q_width + 2 * kv_width]

    marks = jnp.stack([segments[0], valid_mask[0]])
    marks_all = jnp.stack(gather_stream(marks, bit_orders()[0]))
    segment_all = marks_all[:, 0].reshape(length)
    valid_all = marks_all[:, 1].reshape(length)
    x_all = jnp.concatenate(gather_seq(inputs[0]), axis=0)
    valid_col = valid_mask[0].astype(F32)[:, None]
    grad_final = cotangent[0].astype(F32) * valid_col
    grad_mlp = jnp.concatenate(gather_seq(grad_final.astype(BF)), axis=0)

    position = (
        (jnp.arange(count, dtype=jnp.int32) ^ me)[:, None] * rows + jnp.arange(rows, dtype=jnp.int32)[None, :]
    ).reshape(length)
    same = (segment_all[:, None] == segment_all[None, :]) & (position[None, :] < position[:, None])
    places = jnp.sum(same.astype(jnp.int32), axis=1).astype(F32)
    half = HEAD_DIM // 2
    frequency = ROPE_BASE ** (-2.0 * jnp.arange(half, dtype=F32) / HEAD_DIM)
    angles_t = frequency[:, None] * places[None, :]
    cosine_t, sine_t = jnp.cos(angles_t), jnp.sin(angles_t)
    cosine = jnp.tile(cosine_t.T, (1, LANES // half))
    sign = jnp.tile(jnp.repeat(jnp.array([-1.0, 1.0], F32), half), LANES // HEAD_DIM)
    sine = jnp.tile(sine_t.T, (1, LANES // half)) * sign[None, :]
    query_row = jnp.where(valid_all == 1, segment_all, -1).reshape(1, length)
    key_col = segment_all.reshape(length, 1)

    normed_one, q, k, v = project(x_all, gain_one, qkv_full, cosine, sine, kv_local)
    heads_own, totals = attend(me_row, q, k, v, query_row, key_col, rows)

    heads_blocks = gather_seq(heads_own)
    heads_all = jnp.concatenate(
        [
            jnp.concatenate([blocks_of(heads_blocks[k], count)[i ^ k] for i in range(count)], axis=0)
            for k in range(count)
        ],
        axis=1,
    )
    out_blocks = gather_seq(out_slice)
    out_t = jnp.concatenate(out_blocks, axis=1)
    attn_all = dot(heads_all, out_t, NT)
    middle_all = x_all.astype(F32) + attn_all
    normed_two = (middle_all * norm_scale(middle_all) * gain_two).astype(BF)
    tokens = inputs[0].astype(F32)
    attn_branch = attn_all[:rows]
    middle = tokens + attn_branch
    inv_two = norm_scale(middle)

    gate_full, up_full = gate_up[:, :ff_local], gate_up[:, ff_local:]
    gate_lin = dot(normed_two, gate_full)
    up_lin = dot(normed_two, up_full)
    sigmoid_gate = jax.nn.sigmoid(gate_lin)
    silu_gate = gate_lin * sigmoid_gate
    activated = (silu_gate * up_lin).astype(BF)
    grad_act = dot(grad_mlp, down_t)
    grad_gate = (grad_act * up_lin * sigmoid_gate * (1.0 + gate_lin * (1.0 - sigmoid_gate))).astype(BF)
    grad_up = (grad_act * silu_gate).astype(BF)
    mlp_part = dot(activated, down_t, NT).astype(BF)
    grad_both = jnp.concatenate([grad_gate, grad_up], axis=1)
    grad_two_part = dot(grad_both, gate_up, NT).astype(BF)
    grad_normed_two = reduce_seq(blocks_of(grad_two_part, count))
    mlp_branch = reduce_seq(blocks_of(mlp_part, count))
    final = middle + mlp_branch
    outputs = final.astype(BF)[None]

    gate_up_grad = scatter_fsdp(dot(normed_two, grad_both, TN).astype(BF))
    down_grad_t = scatter_fsdp(dot(grad_mlp, activated, TN).astype(BF))

    grad_middle = grad_final + norm_back(grad_normed_two, middle, inv_two, gain_two)
    grad_attn = grad_middle.astype(BF)
    grad_heads = jnp.concatenate(
        exchange_seq([dot(grad_attn, b).astype(BF) for b in out_blocks]), axis=0
    )
    grad_attn_all = jnp.concatenate(gather_seq(grad_attn), axis=0)
    out_grad_t = scatter_fsdp(dot(grad_attn_all, heads_own, TN).astype(BF))

    dq, dk, dv = attend_back(
        me_row, q, k, v, heads_own, grad_heads, totals, query_row, key_col, cosine, sine, cosine_t, sine_t, rows
    )
    dqkv = jnp.concatenate([dq] + [dk[g] for g in range(kv_local)] + [dv[g] for g in range(kv_local)], axis=1)
    qkv_grad = scatter_fsdp(dot(normed_one, dqkv, TN).astype(BF))
    weight_blocks = gather_seq(qkv_weight)
    parts = exchange_seq(blocks_of(dqkv, count))
    grad_normed_one = dot(jnp.concatenate(parts, axis=1), jnp.concatenate(weight_blocks, axis=1), NT)
    inv_one = norm_scale(tokens)
    input_grad = (grad_middle + norm_back(grad_normed_one, tokens, inv_one, gain_one)).astype(BF)[None]

    gate_up_blocks = gather_seq(gate_up_grad)
    gate_grad = whole_columns([b[:, :ff_local] for b in gate_up_blocks], me)
    up_grad = whole_columns([b[:, ff_local:] for b in gate_up_blocks], me)
    down_grad = whole_columns(gather_seq(down_grad_t), me).T
    out_grad = whole_columns(gather_seq(out_grad_t), me).T
    qkv_blocks = gather_seq(qkv_grad)
    query_grad = whole_columns([b[:, :q_width] for b in qkv_blocks], me)
    key_grad = whole_columns([b[:, q_width : q_width + kv_width] for b in qkv_blocks], me)
    value_grad = whole_columns([b[:, q_width + kv_width :] for b in qkv_blocks], me)

    def rows_dot(weight, grad):
        return jnp.sum(weight.astype(F32) * grad, axis=1)

    attn_gain_grad = (
        rows_dot(query_weight, query_grad) + rows_dot(key_weight, key_grad) + rows_dot(value_weight, value_grad)
    ) / attn_gain.astype(F32)
    mlp_gain_grad = (rows_dot(gate_weight, gate_grad) + rows_dot(up_weight, up_grad)) / mlp_gain.astype(F32)

    squares = [jnp.sum(valid_col * part * part) for part in (tokens, middle, final, attn_branch, mlp_branch)]
    stats = jnp.stack([jnp.sum(valid_col)] + squares)
    stats = jnp.broadcast_to(jnp.pad(stats, (0, LANES - 6))[None, :], (8, LANES))
    for bit in bit_orders()[0]:
        stats = stats + swap(stats, bit)
    rms_stats = jnp.sqrt(stats[:1, 1:6] / (stats[:1, :1] * D))
    return (
        outputs, input_grad, query_grad, key_grad, value_grad, out_grad, gate_grad, up_grad, down_grad,
        attn_gain_grad, mlp_gain_grad, rms_stats,
    )


def solution(mesh):
    rows_in = P("fsdp", None)
    columns_in = P(None, "fsdp")
    placed = (
        P("fsdp", "seq", None), P("fsdp", "seq", None), P("fsdp", "seq"), P("fsdp", "seq"),
        rows_in, rows_in, rows_in, columns_in, rows_in, rows_in, columns_in, P("fsdp"), P("fsdp"),
    )
    return jax.shard_map(
        body,
        mesh=mesh,
        in_specs=placed,
        out_specs=(
            P("fsdp", "seq", None), P("fsdp", "seq", None), rows_in, rows_in, rows_in, columns_in,
            rows_in, rows_in, columns_in, P("fsdp"), P("fsdp"), P("fsdp", None),
        ),
        check_vma=False,
    )
```

```python
import functools

import jax
import jax.numpy as jnp
from jax import lax
from jax.experimental import pallas as pl
from jax.experimental.pallas import tpu as pltpu
from jax.sharding import PartitionSpec as P

D = 2048
HEADS = 32
KV_HEADS = 8
HEAD_DIM = 64
GROUP = HEADS // KV_HEADS
FF = 8192
EPSILON = 1e-05
ROPE_BASE = 500000.0
NEGATIVE = -1e30
SCALE = HEAD_DIM**-0.5
BF = jnp.bfloat16
F32 = jnp.float32
LANES = 128
VMEM_LIMIT = 60 * 1024 * 1024
NT = (((1,), (1,)), ((), ()))
NN = (((1,), (0,)), ((), ()))
TN = (((0,), (0,)), ((), ()))


def dot(left, right, dims=NN):
    return lax.dot_general(left, right, dims, preferred_element_type=F32)


def params(grid_rank):
    return pltpu.CompilerParams(
        dimension_semantics=("arbitrary",) * grid_rank, vmem_limit_bytes=VMEM_LIMIT
    )


def swap(values, bit):
    count = lax.axis_size("seq")
    return lax.ppermute(values, "seq", [(i, i ^ bit) for i in range(count)])


def bit_orders():
    bits = [1 << b for b in range(lax.axis_size("seq").bit_length() - 1)]
    return bits, bits[::-1]


def gather_stream(block, order):
    held, owners = block[None], [0]
    for bit in order:
        held = jnp.concatenate([held, swap(held, bit)], axis=0)
        owners = owners + [k ^ bit for k in owners]
    return [held[owners.index(k)] for k in range(len(owners))]


def gather_seq(block):
    half = block.shape[-1] // 2
    low_order, high_order = bit_orders()
    low = gather_stream(block[..., :half], low_order)
    high = gather_stream(block[..., half:], high_order)
    return [jnp.concatenate(pair, axis=-1) for pair in zip(low, high)]


def reduce_stream(blocks, order):
    held = {k: b for k, b in enumerate(blocks)}
    for bit in order:
        away = sorted(k for k in held if k & bit)
        sent = swap(jnp.stack([held[k].astype(BF) for k in away]), bit)
        held = {
            k: held[k].astype(F32) + sent[away.index(k ^ bit)].astype(F32)
            for k in held
            if not k & bit
        }
    return held[0]


def reduce_seq(blocks):
    half = blocks[0].shape[-1] // 2
    low_order, high_order = bit_orders()
    low = reduce_stream([b[..., :half] for b in blocks], low_order)
    high = reduce_stream([b[..., half:] for b in blocks], high_order)
    return jnp.concatenate([low, high], axis=-1)


def exchange_seq(blocks):
    return [b if k == 0 else swap(b, k) for k, b in enumerate(blocks)]


def gather_fsdp(shard):
    return lax.all_gather(shard, "fsdp", axis=0, tiled=True)


def scatter_fsdp(values):
    return lax.psum_scatter(values, "fsdp", scatter_dimension=0, tiled=True)


def turn(values, cosine, sine):
    lane = lax.broadcasted_iota(jnp.int32, values.shape, 1)
    half = HEAD_DIM // 2
    ahead = pltpu.roll(values, LANES - half, 1)
    behind = pltpu.roll(values, half, 1)
    return values * cosine + jnp.where(lane % HEAD_DIM < half, ahead, behind) * sine


def project_kernel(kv_local, x_ref, gain_ref, w_ref, cos_ref, sin_ref, normed_ref, q_ref, k_ref, v_ref):
    x = x_ref[...].astype(F32)
    inv = lax.rsqrt(jnp.mean(x * x, axis=-1, keepdims=True) + EPSILON)
    normed = (x * inv * gain_ref[...]).astype(BF)
    normed_ref[...] = normed
    q_width = kv_local * GROUP * HEAD_DIM
    kv_width = kv_local * HEAD_DIM
    lin = dot(normed, w_ref[:, : q_width + 2 * kv_width])
    cosine, sine = cos_ref[...], sin_ref[...]
    for start in range(0, q_width, LANES):
        part = turn(lin[:, start : start + LANES], cosine, sine) * SCALE
        q_ref[:, start : start + LANES] = part.astype(BF)
    for start in range(0, kv_width, LANES):
        part = turn(lin[:, q_width + start : q_width + start + LANES], cosine, sine)
        for at in range(0, min(LANES, kv_width - start), HEAD_DIM):
            k_ref[(start + at) // HEAD_DIM] = part[:, at : at + HEAD_DIM].astype(BF)
    for head in range(kv_local):
        start = q_width + kv_width + head * HEAD_DIM
        v_ref[head] = lin[:, start : start + HEAD_DIM].astype(BF)


def project(x, gain_row, weight, cosine, sine, kv_local):
    rows = x.shape[0]
    block = 256
    q_width = kv_local * GROUP * HEAD_DIM
    by_row = lambda i: (i, 0)
    whole = lambda i: (0, 0)
    by_head = lambda i: (0, i, 0)
    return pl.pallas_call(
        functools.partial(project_kernel, kv_local),
        grid=(rows // block,),
        in_specs=[
            pl.BlockSpec((block, D), by_row),
            pl.BlockSpec((1, D), whole),
            pl.BlockSpec(weight.shape, whole),
            pl.BlockSpec((block, LANES), by_row),
            pl.BlockSpec((block, LANES), by_row),
        ],
        out_specs=[
            pl.BlockSpec((block, D), by_row),
            pl.BlockSpec((block, q_width), by_row),
            pl.BlockSpec((kv_local, block, HEAD_DIM), by_head),
            pl.BlockSpec((kv_local, block, HEAD_DIM), by_head),
        ],
        out_shape=[
            jax.ShapeDtypeStruct((rows, D), BF),
            jax.ShapeDtypeStruct((rows, q_width), BF),
            jax.ShapeDtypeStruct((kv_local, rows, HEAD_DIM), BF),
            jax.ShapeDtypeStruct((kv_local, rows, HEAD_DIM), BF),
        ],
        compiler_params=params(1),
        cost_estimate=pl.CostEstimate(
            flops=2 * rows * D * weight.shape[1], bytes_accessed=rows * D * 6, transcendentals=0
        ),
        name="project",
    )(x, gain_row, weight, cosine, sine)


def pair_bias(rows, query_index, key_index, query_row, key_col):
    key_pos = key_index * rows + lax.broadcasted_iota(jnp.int32, (rows, rows), 0)
    query_pos = query_index * rows + lax.broadcasted_iota(jnp.int32, (rows, rows), 1)
    allowed = ((key_col == query_row) & (key_pos <= query_pos)) | (key_pos == query_pos)
    return jnp.where(allowed, 0.0, NEGATIVE)


def attend_kernel(rows, me_ref, q_ref, k_ref, v_ref, query_row_ref, key_col_ref, out_ref, total_ref, v_t, peak, total, acc):
    index = pl.program_id(1)
    me = me_ref[0]

    @pl.when(index == 0)
    def _():
        v_t[...] = v_ref[0].astype(F32).T.astype(BF)

    peak[...] = jnp.full(peak.shape, NEGATIVE, F32)
    total[...] = jnp.zeros(total.shape, F32)
    acc[...] = jnp.zeros(acc.shape, F32)

    def step(j, _):
        at = pl.multiple_of((j ^ me) * rows, rows)
        keys = k_ref[0, pl.ds(at, rows), :]
        values_t = v_t[:, pl.ds(at, rows)]
        bias = pair_bias(rows, index, j, query_row_ref[...], key_col_ref[pl.ds(at, rows), :])
        for head in range(GROUP):
            query = q_ref[:, head * HEAD_DIM : (head + 1) * HEAD_DIM]
            scores = dot(keys, query, NT) + bias
            old = peak[head : head + 1, :]
            new = jnp.maximum(old, jnp.max(scores, axis=0, keepdims=True))
            expo = jnp.exp(scores - new)
            fade = jnp.exp(old - new)
            peak[head : head + 1, :] = new
            total[head : head + 1, :] = total[head : head + 1, :] * fade + jnp.sum(expo, axis=0, keepdims=True)
            acc[head] = acc[head] * fade + dot(values_t, expo.astype(BF))
        return 0

    lax.fori_loop(0, index + 1, step, 0)
    for head in range(GROUP):
        out = acc[head] / total[head : head + 1, :]
        out_ref[:, head * HEAD_DIM : (head + 1) * HEAD_DIM] = out.T.astype(BF)
    total_ref[0] = peak[...] + jnp.log(total[...])


def attend(me, q, k, v, query_row, key_col, rows):
    kv_local, length = k.shape[0], k.shape[1]
    count = length // rows
    width = GROUP * HEAD_DIM
    return pl.pallas_call(
        functools.partial(attend_kernel, rows),
        grid_spec=pltpu.PrefetchScalarGridSpec(
            num_scalar_prefetch=1,
            grid=(kv_local, count),
            in_specs=[
                pl.BlockSpec((rows, width), lambda g, i, me: (i ^ me[0], g)),
                pl.BlockSpec((1, length, HEAD_DIM), lambda g, i, me: (g, 0, 0)),
                pl.BlockSpec((1, length, HEAD_DIM), lambda g, i, me: (g, 0, 0)),
                pl.BlockSpec((1, rows), lambda g, i, me: (0, i ^ me[0])),
                pl.BlockSpec((length, 1), lambda g, i, me: (0, 0)),
            ],
            out_specs=[
                pl.BlockSpec((rows, width), lambda g, i, me: (i ^ me[0], g)),
                pl.BlockSpec((1, GROUP, rows), lambda g, i, me: (g, 0, i ^ me[0])),
            ],
            scratch_shapes=[
                pltpu.VMEM((HEAD_DIM, length), BF),
                pltpu.VMEM((GROUP, rows), F32),
                pltpu.VMEM((GROUP, rows), F32),
                pltpu.VMEM((GROUP, HEAD_DIM, rows), F32),
            ],
        ),
        out_shape=[
            jax.ShapeDtypeStruct((length, kv_local * width), BF),
            jax.ShapeDtypeStruct((kv_local, GROUP, length), F32),
        ],
        compiler_params=params(2),
        cost_estimate=pl.CostEstimate(
            flops=kv_local * GROUP * length * length * HEAD_DIM * 8, bytes_accessed=1 << 24, transcendentals=0
        ),
        name="attend",
    )(me, q, k, v, query_row, key_col)


def attend_back_kernel(
    rows, count, me_ref, q_ref, k_ref, v_ref, out_ref, grad_ref, total_ref, query_row_ref, key_col_ref,
    cos_ref, sin_ref, cos_t_ref, sin_t_ref, dq_ref, dk_ref, dv_ref, k_t, inner, dq_t, dk_acc, dv_acc,
):
    me = me_ref[0]
    half = HEAD_DIM // 2
    k_t[...] = k_ref[0].astype(F32).T.astype(BF)
    dq_t[...] = jnp.zeros(dq_t.shape, F32)

    def prepare(i, _):
        here = pl.ds(pl.multiple_of(i * rows, rows), rows)
        for head in range(GROUP):
            cols = slice(head * HEAD_DIM, (head + 1) * HEAD_DIM)
            both = out_ref[here, cols].astype(F32) * grad_ref[here, cols].astype(F32)
            inner[head : head + 1, here] = jnp.sum(both.T, axis=0, keepdims=True)
        return 0

    lax.fori_loop(0, count, prepare, 0)

    def key_step(j, _):
        key_at = pl.ds(pl.multiple_of((j ^ me) * rows, rows), rows)
        keys, values = k_ref[0, key_at, :], v_ref[0, key_at, :]
        keys_t = k_t[:, key_at]
        key_col = key_col_ref[key_at, :]
        dk_acc[...] = jnp.zeros(dk_acc.shape, F32)
        dv_acc[...] = jnp.zeros(dv_acc.shape, F32)

        def query_step(i, _):
            at = pl.ds(pl.multiple_of((i ^ me) * rows, rows), rows)
            bias = pair_bias(rows, i, j, query_row_ref[:, at], key_col)
            for head in range(GROUP):
                cols = slice(head * HEAD_DIM, (head + 1) * HEAD_DIM)
                query, grad = q_ref[at, cols], grad_ref[at, cols]
                probs = jnp.exp(dot(keys, query, NT) + bias - total_ref[0, head : head + 1, at])
                dv_acc[...] += dot(probs.astype(BF), grad)
                grad_probs = dot(values, grad, NT)
                grad_scores = (probs * (grad_probs - inner[head : head + 1, at])).astype(BF)
                dk_acc[...] += dot(grad_scores, query)
                dq_t[head, :, at] += dot(keys_t, grad_scores)
            return 0

        lax.fori_loop(j, count, query_step, 0)
        dk = dk_acc[...]
        low, high = dk[:, :half], dk[:, half:]
        cosine, sine = cos_ref[key_at, :half], sin_ref[key_at, half:HEAD_DIM]
        dk_ref[0, key_at, :] = jnp.concatenate(
            [low * cosine + high * sine, high * cosine - low * sine], axis=1
        ).astype(BF)
        dv_ref[0, key_at, :] = dv_acc[...].astype(BF)
        return 0

    lax.fori_loop(0, count, key_step, 0)

    def finish(i, _):
        here = pl.ds(pl.multiple_of(i * rows, rows), rows)
        cosine, sine = cos_t_ref[:, here], sin_t_ref[:, here]
        for head in range(GROUP):
            low, high = dq_t[head, :half, here], dq_t[head, half:, here]
            turned = jnp.concatenate([low * cosine + high * sine, high * cosine - low * sine], axis=0) * SCALE
            dq_ref[here, head * HEAD_DIM : (head + 1) * HEAD_DIM] = turned.T.astype(BF)
        return 0

    lax.fori_loop(0, count, finish, 0)


def attend_back(me, q, k, v, out, grad, totals, query_row, key_col, cosine, sine, cosine_t, sine_t, rows):
    kv_local, length = k.shape[0], k.shape[1]
    width = GROUP * HEAD_DIM
    by_group = pl.BlockSpec((length, width), lambda g, me: (0, g))
    by_head = pl.BlockSpec((1, length, HEAD_DIM), lambda g, me: (g, 0, 0))
    whole = lambda shape: pl.BlockSpec(shape, lambda g, me: (0, 0))
    return pl.pallas_call(
        functools.partial(attend_back_kernel, rows, length // rows),
        grid_spec=pltpu.PrefetchScalarGridSpec(
            num_scalar_prefetch=1,
            grid=(kv_local,),
            in_specs=[
                by_group,
                by_head,
                by_head,
                by_group,
                by_group,
                pl.BlockSpec((1, GROUP, length), lambda g, me: (g, 0, 0)),
                whole((1, length)),
                whole((length, 1)),
                whole((length, LANES)),
                whole((length, LANES)),
                whole((HEAD_DIM // 2, length)),
                whole((HEAD_DIM // 2, length)),
            ],
            out_specs=[by_group, by_head, by_head],
            scratch_shapes=[
                pltpu.VMEM((HEAD_DIM, length), BF),
                pltpu.VMEM((GROUP, length), F32),
                pltpu.VMEM((GROUP, HEAD_DIM, length), F32),
                pltpu.VMEM((rows, HEAD_DIM), F32),
                pltpu.VMEM((rows, HEAD_DIM), F32),
            ],
        ),
        out_shape=[
            jax.ShapeDtypeStruct((length, kv_local * width), BF),
            jax.ShapeDtypeStruct((kv_local, length, HEAD_DIM), BF),
            jax.ShapeDtypeStruct((kv_local, length, HEAD_DIM), BF),
        ],
        compiler_params=params(1),
        cost_estimate=pl.CostEstimate(
            flops=kv_local * GROUP * length * length * HEAD_DIM * 20, bytes_accessed=1 << 24, transcendentals=0
        ),
        name="attend_back",
    )(me, q, k, v, out, grad, totals, query_row, key_col, cosine, sine, cosine_t, sine_t)


def norm_scale(values):
    return lax.rsqrt(jnp.mean(values * values, axis=-1, keepdims=True) + EPSILON)


def norm_back(grad_normed, values, inv_rms, gain_row):
    unit_rows = values * inv_rms
    scaled = grad_normed * gain_row
    return inv_rms * (scaled - unit_rows * jnp.mean(scaled * unit_rows, axis=-1, keepdims=True))


def blocks_of(values, count):
    rows = values.shape[0] // count
    return [values[k * rows : (k + 1) * rows] for k in range(count)]


def whole_columns(blocks, me):
    stacked = jnp.stack(blocks)
    ordered = [
        lax.dynamic_index_in_dim(stacked, p ^ me, 0, keepdims=False) for p in range(len(blocks))
    ]
    return jnp.concatenate(ordered, axis=1).astype(F32)


def general_body(
    inputs, cotangent, segments, valid_mask, query_weight, key_weight, value_weight, out_weight,
    gate_weight, up_weight, down_weight, attn_gain, mlp_gain,
):
    count = lax.axis_size("seq")
    me = lax.axis_index("seq")
    me_row = me.reshape(1).astype(jnp.int32)
    rows = inputs.shape[1]
    length = rows * count
    kv_local = KV_HEADS // count
    q_width = kv_local * GROUP * HEAD_DIM
    kv_width = kv_local * HEAD_DIM
    ff_local = FF // count
    shard_rows = gate_weight.shape[0]

    def mine(weight, width, axis=1):
        return lax.dynamic_slice_in_dim(weight, me * width, width, axis)

    gains = jnp.pad(jnp.stack([attn_gain, mlp_gain], axis=1), ((0, 0), (0, LANES - 2)))
    qkv_shard = jnp.concatenate(
        [mine(query_weight, q_width), mine(key_weight, kv_width), mine(value_weight, kv_width), gains], axis=1
    )
    qkv_full = gather_fsdp(qkv_shard)
    out_slice = gather_fsdp(mine(out_weight, q_width, 0).T)
    down_t = gather_fsdp(mine(down_weight, ff_local, 0).T)
    gate_up = gather_fsdp(jnp.concatenate([mine(gate_weight, ff_local), mine(up_weight, ff_local)], axis=1))
    gain_one = qkv_full[:, q_width + 2 * kv_width].astype(F32).reshape(1, D)
    gain_two = qkv_full[:, q_width + 2 * kv_width + 1].astype(F32).reshape(1, D)
    qkv_weight = qkv_full[:, : q_width + 2 * kv_width]

    marks = jnp.stack([segments[0], valid_mask[0]])
    marks_all = jnp.stack(gather_stream(marks, bit_orders()[0]))
    segment_all = marks_all[:, 0].reshape(length)
    valid_all = marks_all[:, 1].reshape(length)
    x_all = jnp.concatenate(gather_seq(inputs[0]), axis=0)
    valid_col = valid_mask[0].astype(F32)[:, None]
    grad_final = cotangent[0].astype(F32) * valid_col
    grad_mlp = jnp.concatenate(gather_seq(grad_final.astype(BF)), axis=0)

    position = (
        (jnp.arange(count, dtype=jnp.int32) ^ me)[:, None] * rows + jnp.arange(rows, dtype=jnp.int32)[None, :]
    ).reshape(length)
    same = (segment_all[:, None] == segment_all[None, :]) & (position[None, :] < position[:, None])
    places = jnp.sum(same.astype(jnp.int32), axis=1).astype(F32)
    half = HEAD_DIM // 2
    frequency = ROPE_BASE ** (-2.0 * jnp.arange(half, dtype=F32) / HEAD_DIM)
    angles_t = frequency[:, None] * places[None, :]
    cosine_t, sine_t = jnp.cos(angles_t), jnp.sin(angles_t)
    cosine = jnp.tile(cosine_t.T, (1, LANES // half))
    sign = jnp.tile(jnp.repeat(jnp.array([-1.0, 1.0], F32), half), LANES // HEAD_DIM)
    sine = jnp.tile(sine_t.T, (1, LANES // half)) * sign[None, :]
    query_row = jnp.where(valid_all == 1, segment_all, -1).reshape(1, length)
    key_col = segment_all.reshape(length, 1)

    normed_one, q, k, v = project(x_all, gain_one, qkv_full, cosine, sine, kv_local)
    heads_own, totals = attend(me_row, q, k, v, query_row, key_col, rows)

    heads_blocks = gather_seq(heads_own)
    heads_all = jnp.concatenate(
        [
            jnp.concatenate([blocks_of(heads_blocks[k], count)[i ^ k] for i in range(count)], axis=0)
            for k in range(count)
        ],
        axis=1,
    )
    out_blocks = gather_seq(out_slice)
    out_t = jnp.concatenate(out_blocks, axis=1)
    attn_all = dot(heads_all, out_t, NT)
    middle_all = x_all.astype(F32) + attn_all
    normed_two = (middle_all * norm_scale(middle_all) * gain_two).astype(BF)
    tokens = inputs[0].astype(F32)
    attn_branch = attn_all[:rows]
    middle = tokens + attn_branch
    inv_two = norm_scale(middle)

    gate_full, up_full = gate_up[:, :ff_local], gate_up[:, ff_local:]
    gate_lin = dot(normed_two, gate_full)
    up_lin = dot(normed_two, up_full)
    sigmoid_gate = jax.nn.sigmoid(gate_lin)
    silu_gate = gate_lin * sigmoid_gate
    activated = (silu_gate * up_lin).astype(BF)
    grad_act = dot(grad_mlp, down_t)
    grad_gate = (grad_act * up_lin * sigmoid_gate * (1.0 + gate_lin * (1.0 - sigmoid_gate))).astype(BF)
    grad_up = (grad_act * silu_gate).astype(BF)
    mlp_part = dot(activated, down_t, NT).astype(BF)
    grad_both = jnp.concatenate([grad_gate, grad_up], axis=1)
    grad_two_part = dot(grad_both, gate_up, NT).astype(BF)
    grad_normed_two = reduce_seq(blocks_of(grad_two_part, count))
    mlp_branch = reduce_seq(blocks_of(mlp_part, count))
    final = middle + mlp_branch
    outputs = final.astype(BF)[None]

    gate_up_grad = scatter_fsdp(dot(normed_two, grad_both, TN).astype(BF))
    down_grad_t = scatter_fsdp(dot(grad_mlp, activated, TN).astype(BF))

    grad_middle = grad_final + norm_back(grad_normed_two, middle, inv_two, gain_two)
    grad_attn = grad_middle.astype(BF)
    grad_heads = jnp.concatenate(
        exchange_seq([dot(grad_attn, b).astype(BF) for b in out_blocks]), axis=0
    )
    grad_attn_all = jnp.concatenate(gather_seq(grad_attn), axis=0)
    out_grad_t = scatter_fsdp(dot(grad_attn_all, heads_own, TN).astype(BF))

    dq, dk, dv = attend_back(
        me_row, q, k, v, heads_own, grad_heads, totals, query_row, key_col, cosine, sine, cosine_t, sine_t, rows
    )
    dqkv = jnp.concatenate([dq] + [dk[g] for g in range(kv_local)] + [dv[g] for g in range(kv_local)], axis=1)
    qkv_grad = scatter_fsdp(dot(normed_one, dqkv, TN).astype(BF))
    weight_blocks = gather_seq(qkv_weight)
    parts = exchange_seq(blocks_of(dqkv, count))
    grad_normed_one = dot(jnp.concatenate(parts, axis=1), jnp.concatenate(weight_blocks, axis=1), NT)
    inv_one = norm_scale(tokens)
    input_grad = (grad_middle + norm_back(grad_normed_one, tokens, inv_one, gain_one)).astype(BF)[None]

    gate_up_blocks = gather_seq(gate_up_grad)
    gate_grad = whole_columns([b[:, :ff_local] for b in gate_up_blocks], me)
    up_grad = whole_columns([b[:, ff_local:] for b in gate_up_blocks], me)
    down_grad = whole_columns(gather_seq(down_grad_t), me).T
    out_grad = whole_columns(gather_seq(out_grad_t), me).T
    qkv_blocks = gather_seq(qkv_grad)
    query_grad = whole_columns([b[:, :q_width] for b in qkv_blocks], me)
    key_grad = whole_columns([b[:, q_width : q_width + kv_width] for b in qkv_blocks], me)
    value_grad = whole_columns([b[:, q_width + kv_width :] for b in qkv_blocks], me)

    def rows_dot(weight, grad):
        return jnp.sum(weight.astype(F32) * grad, axis=1)

    attn_gain_grad = (
        rows_dot(query_weight, query_grad) + rows_dot(key_weight, key_grad) + rows_dot(value_weight, value_grad)
    ) / attn_gain.astype(F32)
    mlp_gain_grad = (rows_dot(gate_weight, gate_grad) + rows_dot(up_weight, up_grad)) / mlp_gain.astype(F32)

    squares = [jnp.sum(valid_col * part * part) for part in (tokens, middle, final, attn_branch, mlp_branch)]
    stats = jnp.stack([jnp.sum(valid_col)] + squares)
    stats = jnp.broadcast_to(jnp.pad(stats, (0, LANES - 6))[None, :], (8, LANES))
    for bit in bit_orders()[0]:
        stats = stats + swap(stats, bit)
    rms_stats = jnp.sqrt(stats[:1, 1:6] / (stats[:1, :1] * D))
    return (
        outputs, input_grad, query_grad, key_grad, value_grad, out_grad, gate_grad, up_grad, down_grad,
        attn_gain_grad, mlp_gain_grad, rms_stats,
    )


TILE = 256


def after(value, *events):
    return lax.optimization_barrier((value,) + events)[0]


def to_both(block):
    return swap(block, 1), swap(block, 2)


def pass_on(by_x, by_y, *events):
    half = by_x.shape[0] // 2
    return swap(after(by_y[:half], *events), 1), swap(after(by_x[half:], *events), 2)


def add_low(a, b):
    return (a.astype(F32) + b.astype(F32)).astype(BF)


def send_far(block):
    half = block.shape[0] // 2
    return swap(block[:half], 1), swap(block[half:], 2)


def add_far(for_x, for_y, low, high):
    half = for_x.shape[0] // 2
    return (
        jnp.concatenate([for_x[:half], add_low(for_x[half:], high)], axis=0),
        jnp.concatenate([add_low(for_y[:half], low), for_y[half:]], axis=0),
    )


def call(kernel, grid, in_specs, out_specs, out_shape, args, name, flops=0, moved=0, scratch=(), prefetch=0, aliases=None):
    return pl.pallas_call(
        kernel,
        grid_spec=pltpu.PrefetchScalarGridSpec(
            num_scalar_prefetch=prefetch,
            grid=grid,
            in_specs=in_specs,
            out_specs=out_specs,
            scratch_shapes=list(scratch),
        ),
        out_shape=out_shape,
        input_output_aliases=aliases or {},
        compiler_params=params(len(grid)),
        cost_estimate=pl.CostEstimate(flops=int(flops), bytes_accessed=int(moved), transcendentals=0),
        name=name,
    )(*args)


def shape_of(shape, dtype=BF):
    return jax.ShapeDtypeStruct(shape, dtype)


def fixed(shape, buffers=None):
    mode = {} if buffers is None else {"pipeline_mode": pl.Buffered(buffers)}
    return pl.BlockSpec(shape, lambda *_: (0,) * len(shape), **mode)


def piece_specs(pieces, tile):
    specs, spans, start = [], [], 0
    for piece in pieces:
        tiles = piece.shape[0] // tile
        specs.append(
            pl.BlockSpec(
                (tile, piece.shape[1]),
                lambda i, *_, start=start, tiles=tiles: (jnp.clip(i - start, 0, tiles - 1), 0),
            )
        )
        spans.append((start, start + tiles))
        start += tiles
    return specs, spans


def copy_piece(refs, spans, index, target):
    for ref, (first, last) in zip(refs, spans):

        @pl.when((index >= first) & (index < last))
        def _(ref=ref):
            target[...] = ref[...]


def join_kernel(spans, *refs):
    copy_piece(refs[:-1], spans, pl.program_id(0), refs[-1])


def join(pieces):
    specs, spans = piece_specs(pieces, TILE)
    rows, width = spans[-1][1] * TILE, pieces[0].shape[1]
    return call(
        functools.partial(join_kernel, spans), (rows // TILE,), specs,
        pl.BlockSpec((TILE, width), lambda i: (i, 0)), shape_of((rows, width)), pieces, "join",
        moved=4 * rows * width,
    )


def act_back_kernel(spans, others, *refs):
    weight_ref = refs[len(spans)]
    whole_ref, out_ref = refs[len(spans) + 1 + others :]
    copy_piece(refs[: len(spans)], spans, pl.program_id(0), whole_ref)
    out_ref[...] = dot(whole_ref[...], weight_ref[...]).astype(BF)


def act_back(pieces, weight, first, rows, before=()):
    specs, spans = piece_specs(pieces, TILE)
    tiles, skip, width = spans[-1][1], first // TILE, weight.shape[1]
    by_row = lambda w: pl.BlockSpec((TILE, w), lambda i: (skip + i, 0))
    count = len(pieces) + 1
    return call(
        functools.partial(act_back_kernel, spans, len(before)), (tiles,),
        specs + [fixed(weight.shape)] + [pl.BlockSpec(memory_space=pl.ANY)] * len(before),
        [by_row(D), by_row(width)], [shape_of((rows, D)), shape_of((rows, width))],
        (*pieces, weight, *before), "act_back", flops=2 * tiles * TILE * D * width, moved=tiles * TILE * D * 6,
        aliases={count + k: k for k in range(len(before))},
    )


def pack_qkv_kernel(kv_local, me_ref, q_ref, k_ref, v_ref, gains_ref, out_ref):
    width = GROUP * HEAD_DIM
    parts = []
    for g in range(kv_local):
        head = slice(g * HEAD_DIM, (g + 1) * HEAD_DIM)
        parts += [q_ref[:, g * width : (g + 1) * width], jnp.concatenate([k_ref[:, head], v_ref[:, head]], axis=1)]
    out_ref[...] = jnp.concatenate(parts + [gains_ref[...]], axis=1)


def pack_qkv(me_row, query_weight, key_weight, value_weight, gains, kv_local):
    rows = query_weight.shape[0]
    q_width, kv_width = kv_local * GROUP * HEAD_DIM, kv_local * HEAD_DIM
    total = q_width + 2 * kv_width + LANES
    mine = lambda width: pl.BlockSpec((rows, width), lambda i, me: (0, me[0]))
    return call(
        functools.partial(pack_qkv_kernel, kv_local), (1,),
        [mine(q_width), mine(kv_width), mine(kv_width), fixed((rows, LANES))],
        fixed((rows, total)), shape_of((rows, total)),
        (me_row, query_weight, key_weight, value_weight, gains), "pack_qkv", moved=4 * rows * total, prefetch=1,
    )


def pack_rows_kernel(me_ref, in_ref, out_ref):
    out_ref[...] = in_ref[...].astype(F32).T.astype(BF)


def pack_rows(me_row, weight, rows):
    tile = 512
    tiles, columns = rows // tile, weight.shape[1]
    return call(
        pack_rows_kernel, (tiles,), [pl.BlockSpec((tile, columns), lambda i, me: (me[0] * tiles + i, 0))],
        pl.BlockSpec((columns, tile), lambda i, me: (0, i)), shape_of((columns, rows)), (me_row, weight),
        "pack_rows", moved=4 * rows * columns, prefetch=1,
    )


def pack_pair_kernel(me_ref, a_ref, b_ref, out_ref):
    width = a_ref.shape[1]
    out_ref[:, :width] = a_ref[...]
    out_ref[:, width:] = b_ref[...]


def pack_pair(me_row, a, b, chunks, chunk, width):
    rows = a.shape[0]
    spec = pl.BlockSpec((rows, width), lambda i, me: (0, me[0] * chunks + chunk))
    return call(
        pack_pair_kernel, (1,), [spec, spec], fixed((rows, 2 * width)), shape_of((rows, 2 * width)), (me_row, a, b),
        "pack_pair", moved=8 * rows * width, prefetch=1,
    )


def enter_kernel(kv_local, spans, others, *refs):
    pieces = refs[: len(spans)]
    gain_ref, w_ref, cos_ref, sin_ref = refs[len(spans) : len(spans) + 4]
    x_ref, normed_ref, q_ref, k_ref, v_ref = refs[len(spans) + 4 + others :]
    copy_piece(pieces, spans, pl.program_id(0), x_ref)
    x = x_ref[...].astype(F32)
    inv = lax.rsqrt(jnp.mean(x * x, axis=-1, keepdims=True) + EPSILON)
    normed = (x * inv * gain_ref[...]).astype(BF)
    normed_ref[...] = normed
    width = GROUP * HEAD_DIM
    step = width + 2 * HEAD_DIM
    lin = dot(normed, w_ref[:, : kv_local * step])
    cosine, sine = cos_ref[...], sin_ref[...]
    for g in range(kv_local):
        for start in range(0, width, LANES):
            part = turn(lin[:, g * step + start : g * step + start + LANES], cosine, sine) * SCALE
            q_ref[:, g * width + start : g * width + start + LANES] = part.astype(BF)
        pair = lin[:, g * step + width : (g + 1) * step]
        k_ref[g] = turn(pair, cosine, sine)[:, :HEAD_DIM].astype(BF)
        v_ref[g] = pair[:, HEAD_DIM:].astype(BF)


def enter(pieces, gain_row, weight, cosine, sine, kv_local, first, rows, before=()):
    specs, spans = piece_specs(pieces, TILE)
    tiles, skip = spans[-1][1], first // TILE
    q_width = kv_local * GROUP * HEAD_DIM
    by_row = lambda width: pl.BlockSpec((TILE, width), lambda i: (skip + i, 0))
    by_head = pl.BlockSpec((kv_local, TILE, HEAD_DIM), lambda i: (0, skip + i, 0))
    heads = shape_of((kv_local, rows, HEAD_DIM))
    count = len(pieces) + 4
    return call(
        functools.partial(enter_kernel, kv_local, spans, len(before)), (tiles,),
        specs
        + [fixed((1, D)), fixed(weight.shape), by_row(LANES), by_row(LANES)]
        + [pl.BlockSpec(memory_space=pl.ANY)] * len(before),
        [by_row(D), by_row(D), by_row(q_width), by_head, by_head],
        [shape_of((rows, D)), shape_of((rows, D)), shape_of((rows, q_width)), heads, heads],
        (*pieces, gain_row, weight, cosine, sine, *before), "enter",
        flops=2 * tiles * TILE * D * weight.shape[1], moved=tiles * TILE * D * 8,
        aliases={count + k: k for k in range(len(before))},
    )


def attend_one(me_row, q, k, v, query_row, key_col, rows, group):
    length = k.shape[1]
    width = GROUP * HEAD_DIM
    head = pl.BlockSpec((1, length, HEAD_DIM), lambda g, i, me: (group, 0, 0))
    return call(
        functools.partial(attend_kernel, rows), (1, length // rows),
        [
            pl.BlockSpec((rows, width), lambda g, i, me: (i ^ me[0], group)),
            head,
            head,
            pl.BlockSpec((1, rows), lambda g, i, me: (0, i ^ me[0])),
            fixed((length, 1)),
        ],
        [
            pl.BlockSpec((rows, width), lambda g, i, me: (i ^ me[0], 0)),
            pl.BlockSpec((1, GROUP, rows), lambda g, i, me: (0, 0, i ^ me[0])),
        ],
        [shape_of((length, width)), shape_of((1, GROUP, length), F32)],
        (me_row, q, k, v, query_row, key_col), "attend", flops=2.6e10, moved=1 << 22, prefetch=1,
        scratch=[
            pltpu.VMEM((HEAD_DIM, length), BF),
            pltpu.VMEM((GROUP, rows), F32),
            pltpu.VMEM((GROUP, rows), F32),
            pltpu.VMEM((GROUP, HEAD_DIM, rows), F32),
        ],
    )


def leave_kernel(groups, per, tiles, x_ref, gain_ref, *refs):
    heads, weights, (normed_ref, attn_ref) = refs[: 5 * groups], refs[5 * groups : 5 * groups + 5], refs[5 * groups + 5 :]
    index = pl.program_id(0)
    attn = jnp.zeros(x_ref.shape, F32)
    for k in range(3):
        attn = attn + dot(jnp.concatenate([heads[5 * g + k][...] for g in range(groups)], axis=1), weights[k][...], NT)
    stored = ((index // per) ^ 3) * per + index % per
    is_low = stored < tiles // 2
    far = jnp.concatenate(
        [jnp.where(is_low, heads[5 * g + 3][...], heads[5 * g + 4][...]) for g in range(groups)], axis=1
    )
    attn = attn + jnp.concatenate([dot(far, weights[3][...], NT), dot(far, weights[4][...], NT)], axis=1)
    middle = x_ref[...].astype(F32) + attn
    inv = lax.rsqrt(jnp.mean(middle * middle, axis=-1, keepdims=True) + EPSILON)
    normed_ref[...] = (middle * inv * gain_ref[...]).astype(BF)

    @pl.when(index < per)
    def _():
        attn_ref[...] = attn


def leave(x_all, gain_row, heads, weights, rows):
    length = x_all.shape[0]
    per, tiles = rows // TILE, length // TILE
    by_row = pl.BlockSpec((TILE, D), lambda i: (i, 0))

    def head_spec(k, low, high, width):
        return pl.BlockSpec(
            (TILE, width), lambda i: (jnp.clip(((i // per) ^ k) * per + i % per - low, 0, high - low - 1), 0)
        )

    specs = []
    for pieces in heads:
        width = pieces[0].shape[1]
        for k in range(3):
            specs.append(head_spec(k, 0, tiles, width))
        specs += [head_spec(3, 0, tiles // 2, width), head_spec(3, tiles // 2, tiles, width)]
    return call(
        functools.partial(leave_kernel, len(heads), per, tiles), (tiles,),
        [by_row, fixed((1, D))] + specs + [fixed(w.shape) for w in weights],
        [by_row, pl.BlockSpec((TILE, D), lambda i: (jnp.minimum(i, per - 1), 0))],
        [shape_of((length, D)), shape_of((rows, D), F32)],
        (x_all, gain_row, *[p for pieces in heads for p in pieces], *weights), "leave",
        flops=2 * length * D * D, moved=length * D * 8,
    )


def up_kernel(normed_ref, gate_ref, up_ref, grad_ref, act_ref, grad_gate_ref, grad_up_ref):
    normed = normed_ref[...]
    for start in range(0, act_ref.shape[1], 256):
        part = slice(start, start + 256)
        gate = dot(normed, gate_ref[:, part])
        up = dot(normed, up_ref[:, part])
        grad = grad_ref[:, part].astype(F32)
        sigmoid = jax.nn.sigmoid(gate)
        silu = gate * sigmoid
        act_ref[:, part] = (silu * up).astype(BF)
        grad_gate_ref[:, part] = (grad * up * (sigmoid + silu * (1.0 - sigmoid))).astype(BF)
        grad_up_ref[:, part] = (grad * silu).astype(BF)


def up_project(normed, gate_up, grad_act, chunk):
    length, width = normed.shape[0], gate_up.shape[1] // 2
    tall, wide = 1024, 512
    across = width // wide
    out = pl.BlockSpec((tall, wide), lambda i, j: (i, j))
    return call(
        up_kernel, (length // tall, across),
        [
            pl.BlockSpec((tall, D), lambda i, j: (i, 0)),
            pl.BlockSpec((D, wide), lambda i, j: (0, j)),
            pl.BlockSpec((D, wide), lambda i, j: (0, across + j)),
            pl.BlockSpec((tall, wide), lambda i, j: (i, chunk * across + j)),
        ],
        [out] * 3, [shape_of((length, width))] * 3, (normed, gate_up, gate_up, grad_act), "up_project",
        flops=4 * length * D * width, moved=length * (D + 4 * width) * 2 + 8 * D * width,
    )


def sum_kernel(*refs):
    total = None
    for i in range(0, len(refs) - 1, 2):
        part = dot(refs[i][...], refs[i + 1][...], NT)
        total = part if total is None else total + part
    refs[-1][...] = total.astype(BF)


def sum_of(terms, first, rows):
    tall, wide = 512, 512
    specs, args = [], []
    for left, right, column in terms:
        width = left.shape[1]
        specs.append(pl.BlockSpec((tall, width), lambda i, j: (first // tall + i, 0)))
        specs.append(pl.BlockSpec((wide, width), lambda i, j, column=column: (j, column)))
        args += [left, right]
    depth = sum(left.shape[1] for left, _, _ in terms)
    return call(
        sum_kernel, (rows // tall, D // wide), specs, pl.BlockSpec((tall, wide), lambda i, j: (i, j)),
        shape_of((rows, D)), args, "sum_of", flops=2 * rows * D * depth, moved=2 * depth * (rows + D) + 2 * rows * D,
    )


def outer_kernel(across, count, left_ref, *refs):
    for k in range(count):

        @pl.when(pl.program_id(1) // across == k)
        def _(k=k):
            refs[-1][...] = dot(left_ref[...], refs[k][...], TN).astype(BF)


def outer(left, rights, wide, total=None, first=0, before=()):
    length, tall, width = left.shape[0], 1024, rights[0].shape[1]
    across, count = width // wide, len(rights)
    right_spec = lambda k: pl.BlockSpec((length, wide), lambda i, j: (0, jnp.clip(j - k * across, 0, across - 1)))
    return call(
        functools.partial(outer_kernel, across, count), (left.shape[1] // tall, across * count),
        [pl.BlockSpec((length, tall), lambda i, j: (0, i))]
        + [right_spec(k) for k in range(count)]
        + [pl.BlockSpec(memory_space=pl.ANY)] * len(before),
        pl.BlockSpec((tall, wide), lambda i, j: (i, first // wide + j)),
        shape_of((left.shape[1], total or width * count)),
        (left, *rights, *before), "outer", flops=2 * length * left.shape[1] * width * count,
        moved=2 * (length + left.shape[1]) * (left.shape[1] + width * count),
        aliases={1 + count: 0} if before else None,
    )


def turn_back_kernel(own_ref, by_x_ref, by_y_ref, x_ref, attn_ref, cot_ref, valid_ref, gain_ref, *refs):
    weights, (middle_ref, low_ref, heads_ref) = refs[:5], refs[5:]
    grad = own_ref[...].astype(F32) + by_x_ref[...].astype(F32) + by_y_ref[...].astype(F32)
    middle = x_ref[...].astype(F32) + attn_ref[...]
    inv = lax.rsqrt(jnp.mean(middle * middle, axis=-1, keepdims=True) + EPSILON)
    grad_middle = cot_ref[...].astype(F32) * valid_ref[...] + norm_back(grad, middle, inv, gain_ref[...])
    middle_ref[...] = grad_middle
    low = grad_middle.astype(BF)
    low_ref[...] = low
    for k in range(3):
        heads_ref[k] = dot(low, weights[k][...]).astype(BF)
    heads_ref[3] = (dot(low[:, : D // 2], weights[3][...]) + dot(low[:, D // 2 :], weights[4][...])).astype(BF)


def turn_back(terms, x, attn, cot, valid_col, gain_row, weights):
    rows, width = x.shape[0], weights[0].shape[1]
    by_row = lambda w: pl.BlockSpec((TILE, w), lambda i: (i, 0))
    return call(
        turn_back_kernel, (rows // TILE,),
        [by_row(D)] * 6 + [by_row(1), fixed((1, D))] + [fixed(w.shape) for w in weights],
        [by_row(D), by_row(D), pl.BlockSpec((4, TILE, width), lambda i: (0, i, 0))],
        [shape_of((rows, D), F32), shape_of((rows, D)), shape_of((4, rows, width))],
        (*terms, x, attn, cot, valid_col, gain_row, *weights), "turn_back",
        flops=8 * rows * D * width, moved=rows * D * 20,
    )


def attend_back_one_kernel(rows, count, me_ref, *refs):
    q, k, v, out, own, by_x, by_y, by_xy, total, query_row, key_col, cos, sin, cos_t, sin_t = refs[:15]
    out_ref, grad, k_t, inner, dq_t, dk_acc, dv_acc = refs[15:]
    for block, ref in enumerate((own, by_x, by_y, by_xy)):
        grad[block * rows : (block + 1) * rows, :] = ref[...] if len(ref.shape) == 2 else ref[0]
    width = GROUP * HEAD_DIM
    attend_back_kernel(
        rows, count, me_ref, q, k, v, out, grad, total, query_row, key_col, cos, sin, cos_t, sin_t,
        out_ref.at[:, :width], LaneSlice(out_ref, width), LaneSlice(out_ref, width + HEAD_DIM),
        k_t, inner, dq_t, dk_acc, dv_acc,
    )


class LaneSlice:
    def __init__(self, ref, start):
        self.ref, self.start = ref, start

    def __setitem__(self, key, value):
        self.ref[key[1], self.start : self.start + HEAD_DIM] = value


def attend_back_one(me_row, q, k, v, out, grads, totals, query_row, key_col, tables, rows, group):
    length = k.shape[1]
    width = GROUP * HEAD_DIM
    whole = lambda shape: fixed(shape, 1)
    head = pl.BlockSpec((1, length, HEAD_DIM), lambda i, me: (group, 0, 0), pipeline_mode=pl.Buffered(1))
    part = pl.BlockSpec((rows, width), lambda i, me: (0, group))
    own = pl.BlockSpec((1, rows, width), lambda i, me: (0, 0, group))
    out_width = width + 2 * HEAD_DIM
    return call(
        functools.partial(attend_back_one_kernel, rows, length // rows), (1,),
        [
            pl.BlockSpec((length, width), lambda i, me: (0, group)), head, head, whole((length, width)),
            own, part, part, part, whole((1, GROUP, length)), whole((1, length)), whole((length, 1)),
            whole((length, LANES)), whole((length, LANES)),
            whole((HEAD_DIM // 2, length)), whole((HEAD_DIM // 2, length)),
        ],
        whole((length, out_width)), shape_of((length, out_width)),
        (me_row, q, k, v, out, *grads, totals, query_row, key_col, *tables), "attend_back",
        flops=3.4e10, moved=1 << 22, prefetch=1,
        scratch=[
            pltpu.VMEM((length, width), BF),
            pltpu.VMEM((HEAD_DIM, length), BF),
            pltpu.VMEM((GROUP, length), F32),
            pltpu.VMEM((GROUP, HEAD_DIM, length), F32),
            pltpu.VMEM((rows, HEAD_DIM), F32),
            pltpu.VMEM((rows, HEAD_DIM), F32),
        ],
    )


def finish_kernel(groups, step, x_ref, middle_ref, gain_ref, *refs):
    grads, weights, out_ref = refs[: 4 * groups], refs[4 * groups : 4 * groups + 5], refs[-1]
    columns = slice(0, groups * step)
    grad = jnp.zeros(x_ref.shape, F32)
    for k in range(3):
        low = jnp.concatenate([grads[4 * g + k][...] for g in range(groups)], axis=1)
        grad = grad + dot(low, weights[k][:, columns], NT)
    low = jnp.concatenate([grads[4 * g + 3][...] for g in range(groups)], axis=1)
    grad = grad + jnp.concatenate([dot(low, weights[3][:, columns], NT), dot(low, weights[4][:, columns], NT)], axis=1)
    x = x_ref[...].astype(F32)
    inv = lax.rsqrt(jnp.mean(x * x, axis=-1, keepdims=True) + EPSILON)
    out_ref[...] = (middle_ref[...] + norm_back(grad, x, inv, gain_ref[...])).astype(BF)


def finish(x, grad_middle, gain_row, grads, weights):
    rows, step = x.shape[0], grads[0][0].shape[1]
    by_row = lambda w: pl.BlockSpec((TILE, w), lambda i: (i, 0))
    return call(
        functools.partial(finish_kernel, len(grads), step), (rows // TILE,),
        [by_row(D), by_row(D), fixed((1, D))] + [by_row(step)] * (4 * len(grads)) + [fixed(w.shape) for w in weights],
        by_row(D), shape_of((rows, D)),
        (x, grad_middle, gain_row, *[p for parts in grads for p in parts], *weights), "finish",
        flops=8 * rows * D * step * len(grads), moved=rows * D * 8 + 4 * D * step * 4,
    )


def each_piece(refs, emit):
    block = pl.program_id(0)
    for k in range(3):

        @pl.when(block == k)
        def _(k=k):
            emit(refs[k][...])

    @pl.when(block == 3)
    def _():
        emit(jnp.concatenate([refs[3][...], refs[4][...]], axis=0))


def fold(values):
    return sum(values[:, at : at + LANES] for at in range(0, values.shape[1], LANES))


def place_pair_kernel(first, me_ref, *refs):
    pieces, weight_a, weight_b = refs[:5], refs[5], refs[6]
    out_a, out_b, dot_ref = refs[-3:]
    width = out_a.shape[1]

    @pl.when(pl.program_id(0) == 0)
    def _():
        dot_ref[...] = jnp.zeros(dot_ref.shape, F32) if first else refs[9][...]

    def emit(values):
        a, b = values[:, :width].astype(F32), values[:, width:].astype(F32)
        out_a[...], out_b[...] = a, b
        dot_ref[...] += fold(a * weight_a[...].astype(F32)) + fold(b * weight_b[...].astype(F32))

    each_piece(pieces, emit)


def place_pair(me_row, pieces, weight_a, weight_b, chunks, chunk, before):
    rows, total = weight_a.shape
    width = pieces[0].shape[1] // 2
    column = pl.BlockSpec((rows, width), lambda i, me: (0, (i ^ me[0]) * chunks + chunk))
    any_spec = pl.BlockSpec(memory_space=pl.ANY)
    specs = [fixed(p.shape) for p in pieces] + [column, column]
    args = [me_row, *pieces, weight_a, weight_b]
    aliases = {}
    if before is not None:
        specs += [any_spec, any_spec, fixed((rows, LANES))]
        args += before
        aliases = {8: 0, 9: 1}
    return call(
        functools.partial(place_pair_kernel, before is None), (4,), specs, [column, column, fixed((rows, LANES))],
        [shape_of((rows, total), F32)] * 2 + [shape_of((rows, LANES), F32)], args, "place_pair",
        moved=rows * width * 64, prefetch=1, aliases=aliases,
    )


def place_rows_kernel(me_ref, *refs):
    def emit(values):
        refs[5][...] = values.astype(F32).T

    each_piece(refs[:5], emit)


def place_rows(me_row, pieces, tall):
    columns, rows = pieces[0].shape[0], pieces[0].shape[1]
    across = rows // tall

    def spec(k, piece):
        return pl.BlockSpec((piece.shape[0], tall), lambda i, j, me: (0, jnp.where(i == k, j, 0)))

    return call(
        place_rows_kernel, (4, across), [spec(min(k, 3), p) for k, p in enumerate(pieces)],
        pl.BlockSpec((tall, columns), lambda i, j, me: ((i ^ me[0]) * across + j, 0)),
        shape_of((4 * rows, columns), F32), (me_row, *pieces), "place_rows", moved=rows * columns * 24, prefetch=1,
    )


def place_attn_kernel(kv_local, me_ref, *refs):
    pieces, weights, outs, out_ref, dot_ref = refs[:5], refs[5:8], refs[8:11], refs[11], refs[12]
    width = GROUP * HEAD_DIM
    step = width + 2 * HEAD_DIM

    @pl.when(pl.program_id(0) == 0)
    def _():
        dot_ref[...] = jnp.zeros(dot_ref.shape, F32)

    def emit(values):
        values = values.astype(F32)
        take = lambda start, size: jnp.concatenate(
            [values[:, g * step + start : g * step + start + size] for g in range(kv_local)], axis=1
        )
        parts = (take(0, width), take(width, HEAD_DIM), take(width + HEAD_DIM, HEAD_DIM))
        for part, weight, out in zip(parts, weights, outs):
            out[...] = part
            dot_ref[...] += fold(part * weight[...].astype(F32))
        out_ref[...] = values[:, kv_local * step :].T

    each_piece(pieces, emit)


def place_attn(me_row, pieces, query_weight, key_weight, value_weight, kv_local):
    rows = query_weight.shape[0]
    q_width = kv_local * GROUP * HEAD_DIM
    column = lambda width: pl.BlockSpec((rows, width), lambda i, me: (0, i ^ me[0]))
    columns = [column(q_width), column(kv_local * HEAD_DIM), column(kv_local * HEAD_DIM)]
    weights = (query_weight, key_weight, value_weight)
    return call(
        functools.partial(place_attn_kernel, kv_local), (4,), [fixed(p.shape) for p in pieces] + columns,
        columns + [pl.BlockSpec((q_width, rows), lambda i, me: (i ^ me[0], 0)), fixed((rows, LANES))],
        [shape_of(w.shape, F32) for w in weights] + [shape_of((4 * q_width, rows), F32), shape_of((rows, LANES), F32)],
        (me_row, *pieces, *weights), "place_attn", moved=rows * 5120 * 8, prefetch=1,
    )


CHUNKS = 2


def square_body(
    inputs, cotangent, segments, valid_mask, query_weight, key_weight, value_weight, out_weight,
    gate_weight, up_weight, down_weight, attn_gain, mlp_gain,
):
    count = 4
    me = lax.axis_index("seq")
    me_row = me.reshape(1).astype(jnp.int32)
    rows = inputs.shape[1]
    length = rows * count
    kv_local = KV_HEADS // count
    q_width = kv_local * GROUP * HEAD_DIM
    ff_local = FF // count
    ff_chunk = ff_local // CHUNKS
    step = (GROUP + 2) * HEAD_DIM

    tokens_low, cot_low = inputs[0], cotangent[0]
    marks = jnp.stack([segments[0], valid_mask[0]])
    marks_all = jnp.stack([marks] + [swap(marks, k) for k in range(1, count)])
    x_x, x_y = to_both(after(tokens_low, marks_all))

    segment_all = marks_all[:, 0].reshape(length)
    valid_all = marks_all[:, 1].reshape(length)
    valid_col = valid_mask[0].astype(F32)[:, None]

    position = (
        (jnp.arange(count, dtype=jnp.int32) ^ me)[:, None] * rows + jnp.arange(rows, dtype=jnp.int32)[None, :]
    ).reshape(length)
    same = (segment_all[:, None] == segment_all[None, :]) & (position[None, :] < position[:, None])
    places = jnp.sum(same.astype(jnp.int32), axis=1).astype(F32)
    half = HEAD_DIM // 2
    frequency = ROPE_BASE ** (-2.0 * jnp.arange(half, dtype=F32) / HEAD_DIM)
    angles_t = frequency[:, None] * places[None, :]
    cosine_t, sine_t = jnp.cos(angles_t), jnp.sin(angles_t)
    cosine = jnp.tile(cosine_t.T, (1, LANES // half))
    sign = jnp.tile(jnp.repeat(jnp.array([-1.0, 1.0], F32), half), LANES // HEAD_DIM)
    sine = jnp.tile(sine_t.T, (1, LANES // half)) * sign[None, :]
    query_row = jnp.where(valid_all == 1, segment_all, -1).reshape(1, length)
    key_col = segment_all.reshape(length, 1)
    tables = (cosine, sine, cosine_t, sine_t)

    gains = jnp.pad(jnp.stack([attn_gain, mlp_gain], axis=1), ((0, 0), (0, LANES - 2)))
    qkv_full = gather_fsdp(pack_qkv(me_row, query_weight, key_weight, value_weight, gains, kv_local))
    out_slice = gather_fsdp(pack_rows(me_row, out_weight, q_width))
    down_t = gather_fsdp(pack_rows(me_row, after(down_weight, x_x, x_y, cosine, sine), ff_local))
    later_gate = after(gate_weight, x_x, x_y, cosine, sine)
    gate_up = [
        gather_fsdp(pack_pair(me_row, later_gate, up_weight, CHUNKS, c, ff_chunk)) for c in range(CHUNKS)
    ]
    gain_one = qkv_full[:, kv_local * step].astype(F32).reshape(1, D)
    gain_two = qkv_full[:, kv_local * step + 1].astype(F32).reshape(1, D)

    x_far = pass_on(x_x, x_y, cosine, sine)
    entered = enter([tokens_low, x_x, x_y], gain_one, qkv_full, cosine, sine, kv_local, 0, length)

    done = (*x_far, entered[0])
    o_own = after(out_slice, *done)
    o_x, o_y = to_both(o_own)
    x_all, normed_one, q, k, v = enter(
        list(x_far), gain_one, qkv_full, cosine, sine, kv_local, 3 * rows, length, tuple(entered)
    )
    out_0, total_0 = attend_one(me_row, q, k, v, query_row, key_col, rows, 0)

    done = (o_x, o_y, out_0)
    o_far = pass_on(o_x, o_y, *done)
    out_pieces = [out_slice, o_x, o_y, *o_far]
    h_x, h_y = to_both(after(out_0, *done))
    out_1, total_1 = attend_one(me_row, after(q, *done), k, v, query_row, key_col, rows, 1)
    heads, totals = [out_0, out_1], [total_0, total_1]

    done = (*o_far, h_x, h_y, out_1)
    h_far = pass_on(h_x, h_y, *done)
    heads_0 = [out_0, h_x, h_y, *h_far]
    h_x, h_y = to_both(after(out_1, *done))
    grad_low = (after(cot_low, *done).astype(F32) * valid_col).astype(BF)

    done = (*h_far, h_x, h_y, grad_low)
    h_far = pass_on(h_x, h_y, *done)
    heads_1 = [out_1, h_x, h_y, *h_far]

    c_own = after(grad_low, *h_far)
    c_x, c_y = to_both(c_own)
    normed_two, attn_branch = leave(after(x_all, *h_far), gain_two, [heads_0, heads_1], out_pieces, rows)

    done = (c_x, c_y, normed_two, down_t)
    c_far = pass_on(c_x, c_y, *done)
    acted = act_back([after(c_own, *done), c_x, c_y], down_t, 0, length)

    done = (*c_far, acted[0])
    w_own = after(qkv_full, *done)[:, : kv_local * step]
    w_x, w_y = to_both(w_own)
    grad_mlp, grad_act = act_back(list(c_far), down_t, 3 * rows, length, tuple(acted))
    act_0, gate_0, up_0 = up_project(normed_two, gate_up[0], grad_act, 0)
    grad_0 = outer(normed_two, [gate_0, up_0], 1024)

    done = (w_x, w_y, grad_0)
    gate_up_0 = scatter_fsdp(after(grad_0, *done))
    w_far = pass_on(w_x, w_y, *done)
    weight_pieces = [w_own, w_x, w_y, *w_far]
    act_1, gate_1, up_1 = up_project(after(normed_two, *done), gate_up[1], grad_act, 1)
    terms = [(gate_0, gate_up[0], 0), (up_0, gate_up[0], 1), (gate_1, gate_up[1], 0), (up_1, gate_up[1], 1)]
    far = sum_of(terms, 3 * rows, rows)

    done = (far, *w_far)
    g_far = send_far(after(far, *done))
    near = sum_of([(after(gate_0, *done), *terms[0][1:])] + terms[1:], rows, 2 * rows)

    for_x, for_y = add_far(near[:rows], near[rows:], *g_far)
    g_x, g_y = swap(for_x, 1), swap(for_y, 2)
    own = sum_of([(after(gate_0, for_x, for_y), *terms[0][1:])] + terms[1:], 0, rows)
    grad_1 = outer(after(normed_two, own), [gate_1, up_1], 1024)

    grad_middle, grad_attn, grad_heads = turn_back(
        [after(own, grad_1), g_x, g_y], tokens_low, attn_branch, cot_low, valid_col, gain_two, out_pieces
    )

    head_grads = [grad_heads] + [swap(grad_heads[k], k) for k in range(1, count)]
    grad_down = outer(after(grad_mlp, grad_attn), [act_0, act_1], 1024)

    gate_up_1 = scatter_fsdp(after(grad_1, grad_attn))
    down_sum = scatter_fsdp(after(grad_down, *head_grads[1:]))

    def attention_back(queries, group):
        return attend_back_one(
            me_row, queries, k, v, heads[group], head_grads, totals[group], query_row, key_col, tables, rows, group
        )

    done = (*head_grads[1:], grad_down)
    a_own = after(grad_attn, *done)
    a_x, a_y = to_both(a_own)
    dqkv_0 = attention_back(after(q, *done), 0)

    done = (a_x, a_y, dqkv_0)
    a_far = pass_on(a_x, a_y, *done)
    parts_0 = exchange_seq(blocks_of(after(dqkv_0, *done), count))
    dqkv_1 = attention_back(after(q, *done), 1)

    done = (*a_far, *parts_0[1:], dqkv_1)
    parts_1 = exchange_seq(blocks_of(after(dqkv_1, *done), count))
    p_own = after(gate_up_0, *done)
    p_x, p_y = to_both(p_own)
    total = kv_local * step + q_width
    grad_attn_all = join([after(a_own, *done), a_x, a_y, *a_far])
    grad_weights = outer(after(normed_one, *done), [dqkv_0, dqkv_1], step, total)
    grad_weights = outer(
        grad_attn_all, heads, GROUP * HEAD_DIM, total, kv_local * step, (grad_weights,)
    )

    done = (*parts_1[1:], p_x, p_y, grad_weights)
    attn_sum = scatter_fsdp(after(grad_weights, *done))
    p_far = pass_on(p_x, p_y, *done)
    p_pieces = [p_own, p_x, p_y, *p_far]
    p_own = after(gate_up_1, *done)
    p_x, p_y = to_both(p_own)
    mlp_part = sum_of([(after(act_0, *done), down_t, 0), (act_1, down_t, 1)], 0, length)

    done = (*p_far, p_x, p_y, mlp_part)
    mlp_blocks = blocks_of(after(mlp_part, *done), count)
    m_far = send_far(mlp_blocks[3])
    p_far = pass_on(p_x, p_y, *done)
    input_grad = finish(after(tokens_low, *done), grad_middle, gain_one, [parts_0, parts_1], weight_pieces)
    placed = place_pair(
        me_row, [after(p_pieces[0], input_grad)] + p_pieces[1:], gate_weight, up_weight, CHUNKS, 0, None
    )
    input_grad = input_grad[None]

    done = (*m_far, *p_far, placed[2])
    m_x, m_y = add_far(mlp_blocks[1], mlp_blocks[2], *m_far)
    m_x, m_y = swap(after(m_x, *done), 1), swap(m_y, 2)
    gate_grad, up_grad, gate_up_dot = place_pair(
        me_row, [after(p_own, *done), p_x, p_y, *p_far], gate_weight, up_weight, CHUNKS, 1, placed
    )

    done = (m_x, m_y, gate_up_dot)
    d_x, d_y = to_both(after(down_sum, *done))
    mlp_branch = mlp_blocks[0].astype(F32) + m_x.astype(F32) + m_y.astype(F32)
    tokens = after(tokens_low, *done).astype(F32)
    middle = tokens + attn_branch
    final = middle + mlp_branch
    outputs = final.astype(BF)[None]

    done = (d_x, d_y, outputs)
    d_far = pass_on(d_x, d_y, *done)
    t_x, t_y = to_both(after(attn_sum, *d_far))
    down_grad = place_rows(me_row, [down_sum, d_x, d_y, *d_far], 512)
    query_grad, key_grad, value_grad, out_grad, qkv_dot = place_attn(
        me_row, [attn_sum, t_x, t_y, *pass_on(t_x, t_y, down_grad)], query_weight, key_weight, value_weight, kv_local
    )
    attn_gain_grad = jnp.sum(qkv_dot, axis=1) / attn_gain.astype(F32)
    mlp_gain_grad = jnp.sum(gate_up_dot, axis=1) / mlp_gain.astype(F32)

    squares = [jnp.sum(valid_col * part * part) for part in (tokens, middle, final, attn_branch, mlp_branch)]
    stats = jnp.stack([jnp.sum(valid_col)] + squares)
    stats = jnp.broadcast_to(jnp.pad(stats, (0, LANES - 6))[None, :], (8, LANES))
    for bit in bit_orders()[0]:
        stats = stats + swap(stats, bit)
    rms_stats = jnp.sqrt(stats[:1, 1:6] / (stats[:1, :1] * D))
    return (
        outputs, input_grad, query_grad, key_grad, value_grad, out_grad, gate_grad, up_grad, down_grad,
        attn_gain_grad, mlp_gain_grad, rms_stats,
    )


def solution(mesh):
    rows_in = P("fsdp", None)
    columns_in = P(None, "fsdp")
    placed = (
        P("fsdp", "seq", None), P("fsdp", "seq", None), P("fsdp", "seq"), P("fsdp", "seq"),
        rows_in, rows_in, rows_in, columns_in, rows_in, rows_in, columns_in, P("fsdp"), P("fsdp"),
    )
    return jax.shard_map(
        square_body if mesh.shape["seq"] == 4 else general_body,
        mesh=mesh,
        in_specs=placed,
        out_specs=(
            P("fsdp", "seq", None), P("fsdp", "seq", None), rows_in, rows_in, rows_in, columns_in,
            rows_in, rows_in, columns_in, P("fsdp"), P("fsdp"), P("fsdp", None),
        ),
        check_vma=False,
    )
```

```python
import functools

import jax
import jax.numpy as jnp
from jax import lax
from jax.experimental import pallas as pl
from jax.experimental.pallas import tpu as pltpu
from jax.sharding import PartitionSpec as P

D = 2048
HEADS = 32
KV_HEADS = 8
HEAD_DIM = 64
GROUP = HEADS // KV_HEADS
FF = 8192
EPSILON = 1e-05
ROPE_BASE = 500000.0
NEGATIVE = -1e30
SCALE = HEAD_DIM**-0.5
BF = jnp.bfloat16
F32 = jnp.float32
LANES = 128
VMEM_LIMIT = 60 * 1024 * 1024
NT = (((1,), (1,)), ((), ()))
NN = (((1,), (0,)), ((), ()))
TN = (((0,), (0,)), ((), ()))


def dot(left, right, dims=NN):
    return lax.dot_general(left, right, dims, preferred_element_type=F32)


def params(grid_rank):
    return pltpu.CompilerParams(
        dimension_semantics=("arbitrary",) * grid_rank, vmem_limit_bytes=VMEM_LIMIT
    )


def swap(values, bit):
    count = lax.axis_size("seq")
    return lax.ppermute(values, "seq", [(i, i ^ bit) for i in range(count)])


def bit_orders():
    bits = [1 << b for b in range(lax.axis_size("seq").bit_length() - 1)]
    return bits, bits[::-1]


def gather_stream(block, order):
    held, owners = block[None], [0]
    for bit in order:
        held = jnp.concatenate([held, swap(held, bit)], axis=0)
        owners = owners + [k ^ bit for k in owners]
    return [held[owners.index(k)] for k in range(len(owners))]


def gather_seq(block):
    half = block.shape[-1] // 2
    low_order, high_order = bit_orders()
    low = gather_stream(block[..., :half], low_order)
    high = gather_stream(block[..., half:], high_order)
    return [jnp.concatenate(pair, axis=-1) for pair in zip(low, high)]


def reduce_stream(blocks, order):
    held = {k: b for k, b in enumerate(blocks)}
    for bit in order:
        away = sorted(k for k in held if k & bit)
        sent = swap(jnp.stack([held[k].astype(BF) for k in away]), bit)
        held = {
            k: held[k].astype(F32) + sent[away.index(k ^ bit)].astype(F32)
            for k in held
            if not k & bit
        }
    return held[0]


def reduce_seq(blocks):
    half = blocks[0].shape[-1] // 2
    low_order, high_order = bit_orders()
    low = reduce_stream([b[..., :half] for b in blocks], low_order)
    high = reduce_stream([b[..., half:] for b in blocks], high_order)
    return jnp.concatenate([low, high], axis=-1)


def exchange_seq(blocks):
    return [b if k == 0 else swap(b, k) for k, b in enumerate(blocks)]


def gather_fsdp(shard):
    return lax.all_gather(shard, "fsdp", axis=0, tiled=True)


def scatter_fsdp(values):
    return lax.psum_scatter(values, "fsdp", scatter_dimension=0, tiled=True)


def turn(values, cosine, sine):
    lane = lax.broadcasted_iota(jnp.int32, values.shape, 1)
    half = HEAD_DIM // 2
    ahead = pltpu.roll(values, LANES - half, 1)
    behind = pltpu.roll(values, half, 1)
    return values * cosine + jnp.where(lane % HEAD_DIM < half, ahead, behind) * sine


def project_kernel(kv_local, x_ref, gain_ref, w_ref, cos_ref, sin_ref, normed_ref, q_ref, k_ref, v_ref):
    x = x_ref[...].astype(F32)
    inv = lax.rsqrt(jnp.mean(x * x, axis=-1, keepdims=True) + EPSILON)
    normed = (x * inv * gain_ref[...]).astype(BF)
    normed_ref[...] = normed
    q_width = kv_local * GROUP * HEAD_DIM
    kv_width = kv_local * HEAD_DIM
    lin = dot(normed, w_ref[:, : q_width + 2 * kv_width])
    cosine, sine = cos_ref[...], sin_ref[...]
    for start in range(0, q_width, LANES):
        part = turn(lin[:, start : start + LANES], cosine, sine) * SCALE
        q_ref[:, start : start + LANES] = part.astype(BF)
    for start in range(0, kv_width, LANES):
        part = turn(lin[:, q_width + start : q_width + start + LANES], cosine, sine)
        for at in range(0, min(LANES, kv_width - start), HEAD_DIM):
            k_ref[(start + at) // HEAD_DIM] = part[:, at : at + HEAD_DIM].astype(BF)
    for head in range(kv_local):
        start = q_width + kv_width + head * HEAD_DIM
        v_ref[head] = lin[:, start : start + HEAD_DIM].astype(BF)


def project(x, gain_row, weight, cosine, sine, kv_local):
    rows = x.shape[0]
    block = 256
    q_width = kv_local * GROUP * HEAD_DIM
    by_row = lambda i: (i, 0)
    whole = lambda i: (0, 0)
    by_head = lambda i: (0, i, 0)
    return pl.pallas_call(
        functools.partial(project_kernel, kv_local),
        grid=(rows // block,),
        in_specs=[
            pl.BlockSpec((block, D), by_row),
            pl.BlockSpec((1, D), whole),
            pl.BlockSpec(weight.shape, whole),
            pl.BlockSpec((block, LANES), by_row),
            pl.BlockSpec((block, LANES), by_row),
        ],
        out_specs=[
            pl.BlockSpec((block, D), by_row),
            pl.BlockSpec((block, q_width), by_row),
            pl.BlockSpec((kv_local, block, HEAD_DIM), by_head),
            pl.BlockSpec((kv_local, block, HEAD_DIM), by_head),
        ],
        out_shape=[
            jax.ShapeDtypeStruct((rows, D), BF),
            jax.ShapeDtypeStruct((rows, q_width), BF),
            jax.ShapeDtypeStruct((kv_local, rows, HEAD_DIM), BF),
            jax.ShapeDtypeStruct((kv_local, rows, HEAD_DIM), BF),
        ],
        compiler_params=params(1),
        cost_estimate=pl.CostEstimate(
            flops=2 * rows * D * weight.shape[1], bytes_accessed=rows * D * 6, transcendentals=0
        ),
        name="project",
    )(x, gain_row, weight, cosine, sine)


def pair_bias(rows, query_index, key_index, query_row, key_col):
    key_pos = key_index * rows + lax.broadcasted_iota(jnp.int32, (rows, rows), 0)
    query_pos = query_index * rows + lax.broadcasted_iota(jnp.int32, (rows, rows), 1)
    allowed = ((key_col == query_row) & (key_pos <= query_pos)) | (key_pos == query_pos)
    return jnp.where(allowed, 0.0, NEGATIVE)


def attend_kernel(rows, me_ref, q_ref, k_ref, v_ref, query_row_ref, key_col_ref, out_ref, total_ref, v_t, peak, total, acc):
    index = pl.program_id(1)
    me = me_ref[0]

    @pl.when(index == 0)
    def _():
        v_t[...] = v_ref[0].astype(F32).T.astype(BF)

    peak[...] = jnp.full(peak.shape, NEGATIVE, F32)
    total[...] = jnp.zeros(total.shape, F32)
    acc[...] = jnp.zeros(acc.shape, F32)

    def step(j, _):
        at = pl.multiple_of((j ^ me) * rows, rows)
        keys = k_ref[0, pl.ds(at, rows), :]
        values_t = v_t[:, pl.ds(at, rows)]
        bias = pair_bias(rows, index, j, query_row_ref[...], key_col_ref[pl.ds(at, rows), :])
        for head in range(GROUP):
            query = q_ref[:, head * HEAD_DIM : (head + 1) * HEAD_DIM]
            scores = dot(keys, query, NT) + bias
            old = peak[head : head + 1, :]
            new = jnp.maximum(old, jnp.max(scores, axis=0, keepdims=True))
            expo = jnp.exp(scores - new)
            fade = jnp.exp(old - new)
            peak[head : head + 1, :] = new
            total[head : head + 1, :] = total[head : head + 1, :] * fade + jnp.sum(expo, axis=0, keepdims=True)
            acc[head] = acc[head] * fade + dot(values_t, expo.astype(BF))
        return 0

    lax.fori_loop(0, index + 1, step, 0)
    for head in range(GROUP):
        out = acc[head] / total[head : head + 1, :]
        out_ref[:, head * HEAD_DIM : (head + 1) * HEAD_DIM] = out.T.astype(BF)
    total_ref[0] = peak[...] + jnp.log(total[...])


def attend(me, q, k, v, query_row, key_col, rows):
    kv_local, length = k.shape[0], k.shape[1]
    count = length // rows
    width = GROUP * HEAD_DIM
    return pl.pallas_call(
        functools.partial(attend_kernel, rows),
        grid_spec=pltpu.PrefetchScalarGridSpec(
            num_scalar_prefetch=1,
            grid=(kv_local, count),
            in_specs=[
                pl.BlockSpec((rows, width), lambda g, i, me: (i ^ me[0], g)),
                pl.BlockSpec((1, length, HEAD_DIM), lambda g, i, me: (g, 0, 0)),
                pl.BlockSpec((1, length, HEAD_DIM), lambda g, i, me: (g, 0, 0)),
                pl.BlockSpec((1, rows), lambda g, i, me: (0, i ^ me[0])),
                pl.BlockSpec((length, 1), lambda g, i, me: (0, 0)),
            ],
            out_specs=[
                pl.BlockSpec((rows, width), lambda g, i, me: (i ^ me[0], g)),
                pl.BlockSpec((1, GROUP, rows), lambda g, i, me: (g, 0, i ^ me[0])),
            ],
            scratch_shapes=[
                pltpu.VMEM((HEAD_DIM, length), BF),
                pltpu.VMEM((GROUP, rows), F32),
                pltpu.VMEM((GROUP, rows), F32),
                pltpu.VMEM((GROUP, HEAD_DIM, rows), F32),
            ],
        ),
        out_shape=[
            jax.ShapeDtypeStruct((length, kv_local * width), BF),
            jax.ShapeDtypeStruct((kv_local, GROUP, length), F32),
        ],
        compiler_params=params(2),
        cost_estimate=pl.CostEstimate(
            flops=kv_local * GROUP * length * length * HEAD_DIM * 8, bytes_accessed=1 << 24, transcendentals=0
        ),
        name="attend",
    )(me, q, k, v, query_row, key_col)


def attend_back_kernel(
    rows, count, me_ref, q_ref, k_ref, v_ref, out_ref, grad_ref, total_ref, query_row_ref, key_col_ref,
    cos_ref, sin_ref, cos_t_ref, sin_t_ref, dq_ref, dk_ref, dv_ref, k_t, inner, dq_t, dk_acc, dv_acc,
):
    me = me_ref[0]
    half = HEAD_DIM // 2
    k_t[...] = k_ref[0].astype(F32).T.astype(BF)
    dq_t[...] = jnp.zeros(dq_t.shape, F32)

    def prepare(i, _):
        here = pl.ds(pl.multiple_of(i * rows, rows), rows)
        for head in range(GROUP):
            cols = slice(head * HEAD_DIM, (head + 1) * HEAD_DIM)
            both = out_ref[here, cols].astype(F32) * grad_ref[here, cols].astype(F32)
            inner[head : head + 1, here] = jnp.sum(both.T, axis=0, keepdims=True)
        return 0

    lax.fori_loop(0, count, prepare, 0)

    def key_step(j, _):
        key_at = pl.ds(pl.multiple_of((j ^ me) * rows, rows), rows)
        keys, values = k_ref[0, key_at, :], v_ref[0, key_at, :]
        keys_t = k_t[:, key_at]
        key_col = key_col_ref[key_at, :]
        dk_acc[...] = jnp.zeros(dk_acc.shape, F32)
        dv_acc[...] = jnp.zeros(dv_acc.shape, F32)

        def query_step(i, _):
            at = pl.ds(pl.multiple_of((i ^ me) * rows, rows), rows)
            bias = pair_bias(rows, i, j, query_row_ref[:, at], key_col)
            for head in range(GROUP):
                cols = slice(head * HEAD_DIM, (head + 1) * HEAD_DIM)
                query, grad = q_ref[at, cols], grad_ref[at, cols]
                probs = jnp.exp(dot(keys, query, NT) + bias - total_ref[0, head : head + 1, at])
                dv_acc[...] += dot(probs.astype(BF), grad)
                grad_probs = dot(values, grad, NT)
                grad_scores = (probs * (grad_probs - inner[head : head + 1, at])).astype(BF)
                dk_acc[...] += dot(grad_scores, query)
                dq_t[head, :, at] += dot(keys_t, grad_scores)
            return 0

        lax.fori_loop(j, count, query_step, 0)
        dk = dk_acc[...]
        low, high = dk[:, :half], dk[:, half:]
        cosine, sine = cos_ref[key_at, :half], sin_ref[key_at, half:HEAD_DIM]
        dk_ref[0, key_at, :] = jnp.concatenate(
            [low * cosine + high * sine, high * cosine - low * sine], axis=1
        ).astype(BF)
        dv_ref[0, key_at, :] = dv_acc[...].astype(BF)
        return 0

    lax.fori_loop(0, count, key_step, 0)

    def finish(i, _):
        here = pl.ds(pl.multiple_of(i * rows, rows), rows)
        cosine, sine = cos_t_ref[:, here], sin_t_ref[:, here]
        for head in range(GROUP):
            low, high = dq_t[head, :half, here], dq_t[head, half:, here]
            turned = jnp.concatenate([low * cosine + high * sine, high * cosine - low * sine], axis=0) * SCALE
            dq_ref[here, head * HEAD_DIM : (head + 1) * HEAD_DIM] = turned.T.astype(BF)
        return 0

    lax.fori_loop(0, count, finish, 0)


def attend_back(me, q, k, v, out, grad, totals, query_row, key_col, cosine, sine, cosine_t, sine_t, rows):
    kv_local, length = k.shape[0], k.shape[1]
    width = GROUP * HEAD_DIM
    by_group = pl.BlockSpec((length, width), lambda g, me: (0, g))
    by_head = pl.BlockSpec((1, length, HEAD_DIM), lambda g, me: (g, 0, 0))
    whole = lambda shape: pl.BlockSpec(shape, lambda g, me: (0, 0))
    return pl.pallas_call(
        functools.partial(attend_back_kernel, rows, length // rows),
        grid_spec=pltpu.PrefetchScalarGridSpec(
            num_scalar_prefetch=1,
            grid=(kv_local,),
            in_specs=[
                by_group,
                by_head,
                by_head,
                by_group,
                by_group,
                pl.BlockSpec((1, GROUP, length), lambda g, me: (g, 0, 0)),
                whole((1, length)),
                whole((length, 1)),
                whole((length, LANES)),
                whole((length, LANES)),
                whole((HEAD_DIM // 2, length)),
                whole((HEAD_DIM // 2, length)),
            ],
            out_specs=[by_group, by_head, by_head],
            scratch_shapes=[
                pltpu.VMEM((HEAD_DIM, length), BF),
                pltpu.VMEM((GROUP, length), F32),
                pltpu.VMEM((GROUP, HEAD_DIM, length), F32),
                pltpu.VMEM((rows, HEAD_DIM), F32),
                pltpu.VMEM((rows, HEAD_DIM), F32),
            ],
        ),
        out_shape=[
            jax.ShapeDtypeStruct((length, kv_local * width), BF),
            jax.ShapeDtypeStruct((kv_local, length, HEAD_DIM), BF),
            jax.ShapeDtypeStruct((kv_local, length, HEAD_DIM), BF),
        ],
        compiler_params=params(1),
        cost_estimate=pl.CostEstimate(
            flops=kv_local * GROUP * length * length * HEAD_DIM * 20, bytes_accessed=1 << 24, transcendentals=0
        ),
        name="attend_back",
    )(me, q, k, v, out, grad, totals, query_row, key_col, cosine, sine, cosine_t, sine_t)


def norm_scale(values):
    return lax.rsqrt(jnp.mean(values * values, axis=-1, keepdims=True) + EPSILON)


def norm_back(grad_normed, values, inv_rms, gain_row):
    unit_rows = values * inv_rms
    scaled = grad_normed * gain_row
    return inv_rms * (scaled - unit_rows * jnp.mean(scaled * unit_rows, axis=-1, keepdims=True))


def blocks_of(values, count):
    rows = values.shape[0] // count
    return [values[k * rows : (k + 1) * rows] for k in range(count)]


def whole_columns(blocks, me):
    stacked = jnp.stack(blocks)
    ordered = [
        lax.dynamic_index_in_dim(stacked, p ^ me, 0, keepdims=False) for p in range(len(blocks))
    ]
    return jnp.concatenate(ordered, axis=1).astype(F32)


def general_body(
    inputs, cotangent, segments, valid_mask, query_weight, key_weight, value_weight, out_weight,
    gate_weight, up_weight, down_weight, attn_gain, mlp_gain,
):
    count = lax.axis_size("seq")
    me = lax.axis_index("seq")
    me_row = me.reshape(1).astype(jnp.int32)
    rows = inputs.shape[1]
    length = rows * count
    kv_local = KV_HEADS // count
    q_width = kv_local * GROUP * HEAD_DIM
    kv_width = kv_local * HEAD_DIM
    ff_local = FF // count
    shard_rows = gate_weight.shape[0]

    def mine(weight, width, axis=1):
        return lax.dynamic_slice_in_dim(weight, me * width, width, axis)

    gains = jnp.pad(jnp.stack([attn_gain, mlp_gain], axis=1), ((0, 0), (0, LANES - 2)))
    qkv_shard = jnp.concatenate(
        [mine(query_weight, q_width), mine(key_weight, kv_width), mine(value_weight, kv_width), gains], axis=1
    )
    qkv_full = gather_fsdp(qkv_shard)
    out_slice = gather_fsdp(mine(out_weight, q_width, 0).T)
    down_t = gather_fsdp(mine(down_weight, ff_local, 0).T)
    gate_up = gather_fsdp(jnp.concatenate([mine(gate_weight, ff_local), mine(up_weight, ff_local)], axis=1))
    gain_one = qkv_full[:, q_width + 2 * kv_width].astype(F32).reshape(1, D)
    gain_two = qkv_full[:, q_width + 2 * kv_width + 1].astype(F32).reshape(1, D)
    qkv_weight = qkv_full[:, : q_width + 2 * kv_width]

    marks = jnp.stack([segments[0], valid_mask[0]])
    marks_all = jnp.stack(gather_stream(marks, bit_orders()[0]))
    segment_all = marks_all[:, 0].reshape(length)
    valid_all = marks_all[:, 1].reshape(length)
    x_all = jnp.concatenate(gather_seq(inputs[0]), axis=0)
    valid_col = valid_mask[0].astype(F32)[:, None]
    grad_final = cotangent[0].astype(F32) * valid_col
    grad_mlp = jnp.concatenate(gather_seq(grad_final.astype(BF)), axis=0)

    position = (
        (jnp.arange(count, dtype=jnp.int32) ^ me)[:, None] * rows + jnp.arange(rows, dtype=jnp.int32)[None, :]
    ).reshape(length)
    same = (segment_all[:, None] == segment_all[None, :]) & (position[None, :] < position[:, None])
    places = jnp.sum(same.astype(jnp.int32), axis=1).astype(F32)
    half = HEAD_DIM // 2
    frequency = ROPE_BASE ** (-2.0 * jnp.arange(half, dtype=F32) / HEAD_DIM)
    angles_t = frequency[:, None] * places[None, :]
    cosine_t, sine_t = jnp.cos(angles_t), jnp.sin(angles_t)
    cosine = jnp.tile(cosine_t.T, (1, LANES // half))
    sign = jnp.tile(jnp.repeat(jnp.array([-1.0, 1.0], F32), half), LANES // HEAD_DIM)
    sine = jnp.tile(sine_t.T, (1, LANES // half)) * sign[None, :]
    query_row = jnp.where(valid_all == 1, segment_all, -1).reshape(1, length)
    key_col = segment_all.reshape(length, 1)

    normed_one, q, k, v = project(x_all, gain_one, qkv_full, cosine, sine, kv_local)
    heads_own, totals = attend(me_row, q, k, v, query_row, key_col, rows)

    heads_blocks = gather_seq(heads_own)
    heads_all = jnp.concatenate(
        [
            jnp.concatenate([blocks_of(heads_blocks[k], count)[i ^ k] for i in range(count)], axis=0)
            for k in range(count)
        ],
        axis=1,
    )
    out_blocks = gather_seq(out_slice)
    out_t = jnp.concatenate(out_blocks, axis=1)
    attn_all = dot(heads_all, out_t, NT)
    middle_all = x_all.astype(F32) + attn_all
    normed_two = (middle_all * norm_scale(middle_all) * gain_two).astype(BF)
    tokens = inputs[0].astype(F32)
    attn_branch = attn_all[:rows]
    middle = tokens + attn_branch
    inv_two = norm_scale(middle)

    gate_full, up_full = gate_up[:, :ff_local], gate_up[:, ff_local:]
    gate_lin = dot(normed_two, gate_full)
    up_lin = dot(normed_two, up_full)
    sigmoid_gate = jax.nn.sigmoid(gate_lin)
    silu_gate = gate_lin * sigmoid_gate
    activated = (silu_gate * up_lin).astype(BF)
    grad_act = dot(grad_mlp, down_t)
    grad_gate = (grad_act * up_lin * sigmoid_gate * (1.0 + gate_lin * (1.0 - sigmoid_gate))).astype(BF)
    grad_up = (grad_act * silu_gate).astype(BF)
    mlp_part = dot(activated, down_t, NT).astype(BF)
    grad_both = jnp.concatenate([grad_gate, grad_up], axis=1)
    grad_two_part = dot(grad_both, gate_up, NT).astype(BF)
    grad_normed_two = reduce_seq(blocks_of(grad_two_part, count))
    mlp_branch = reduce_seq(blocks_of(mlp_part, count))
    final = middle + mlp_branch
    outputs = final.astype(BF)[None]

    gate_up_grad = scatter_fsdp(dot(normed_two, grad_both, TN).astype(BF))
    down_grad_t = scatter_fsdp(dot(grad_mlp, activated, TN).astype(BF))

    grad_middle = grad_final + norm_back(grad_normed_two, middle, inv_two, gain_two)
    grad_attn = grad_middle.astype(BF)
    grad_heads = jnp.concatenate(
        exchange_seq([dot(grad_attn, b).astype(BF) for b in out_blocks]), axis=0
    )
    grad_attn_all = jnp.concatenate(gather_seq(grad_attn), axis=0)
    out_grad_t = scatter_fsdp(dot(grad_attn_all, heads_own, TN).astype(BF))

    dq, dk, dv = attend_back(
        me_row, q, k, v, heads_own, grad_heads, totals, query_row, key_col, cosine, sine, cosine_t, sine_t, rows
    )
    dqkv = jnp.concatenate([dq] + [dk[g] for g in range(kv_local)] + [dv[g] for g in range(kv_local)], axis=1)
    qkv_grad = scatter_fsdp(dot(normed_one, dqkv, TN).astype(BF))
    weight_blocks = gather_seq(qkv_weight)
    parts = exchange_seq(blocks_of(dqkv, count))
    grad_normed_one = dot(jnp.concatenate(parts, axis=1), jnp.concatenate(weight_blocks, axis=1), NT)
    inv_one = norm_scale(tokens)
    input_grad = (grad_middle + norm_back(grad_normed_one, tokens, inv_one, gain_one)).astype(BF)[None]

    gate_up_blocks = gather_seq(gate_up_grad)
    gate_grad = whole_columns([b[:, :ff_local] for b in gate_up_blocks], me)
    up_grad = whole_columns([b[:, ff_local:] for b in gate_up_blocks], me)
    down_grad = whole_columns(gather_seq(down_grad_t), me).T
    out_grad = whole_columns(gather_seq(out_grad_t), me).T
    qkv_blocks = gather_seq(qkv_grad)
    query_grad = whole_columns([b[:, :q_width] for b in qkv_blocks], me)
    key_grad = whole_columns([b[:, q_width : q_width + kv_width] for b in qkv_blocks], me)
    value_grad = whole_columns([b[:, q_width + kv_width :] for b in qkv_blocks], me)

    def rows_dot(weight, grad):
        return jnp.sum(weight.astype(F32) * grad, axis=1)

    attn_gain_grad = (
        rows_dot(query_weight, query_grad) + rows_dot(key_weight, key_grad) + rows_dot(value_weight, value_grad)
    ) / attn_gain.astype(F32)
    mlp_gain_grad = (rows_dot(gate_weight, gate_grad) + rows_dot(up_weight, up_grad)) / mlp_gain.astype(F32)

    squares = [jnp.sum(valid_col * part * part) for part in (tokens, middle, final, attn_branch, mlp_branch)]
    stats = jnp.stack([jnp.sum(valid_col)] + squares)
    stats = jnp.broadcast_to(jnp.pad(stats, (0, LANES - 6))[None, :], (8, LANES))
    for bit in bit_orders()[0]:
        stats = stats + swap(stats, bit)
    rms_stats = jnp.sqrt(stats[:1, 1:6] / (stats[:1, :1] * D))
    return (
        outputs, input_grad, query_grad, key_grad, value_grad, out_grad, gate_grad, up_grad, down_grad,
        attn_gain_grad, mlp_gain_grad, rms_stats,
    )


TILE = 256

def after(value, *events):
    return lax.optimization_barrier((value,) + events)[0]


def to_both(block):
    return swap(block, 1), swap(block, 2)


def pass_on(by_x, by_y, *events):
    half = by_x.shape[0] // 2
    return swap(after(by_y[:half], *events), 1), swap(after(by_x[half:], *events), 2)


def swap_core(values):
    count = lax.axis_size("fsdp")
    return lax.ppermute(values, "fsdp", [(i, i ^ 1) for i in range(count)])


def core_half(weight, core):
    half = weight.shape[0] // 2
    return lax.dynamic_slice_in_dim(weight, core * half, half, 0)


def in_order(core, mine, other):
    return jnp.where(core == 0, jnp.concatenate([mine, other], axis=1), jnp.concatenate([other, mine], axis=1))


def add_low(a, b):
    return (a.astype(F32) + b.astype(F32)).astype(BF)


def send_far(low, high):
    return swap(low, 1), swap(high, 2)


def add_far(near, low, high):
    x_low, x_high, y_low, y_high = near
    return [x_low, add_low(x_high, high), add_low(y_low, low), y_high]


def send_near(near):
    return [swap(part, bit) for part, bit in zip(near, (1, 1, 2, 2))]


def call(kernel, grid, in_specs, out_specs, out_shape, args, name, flops=0, moved=0, scratch=(), prefetch=0, aliases=None):
    return pl.pallas_call(
        kernel,
        grid_spec=pltpu.PrefetchScalarGridSpec(
            num_scalar_prefetch=prefetch,
            grid=grid,
            in_specs=in_specs,
            out_specs=out_specs,
            scratch_shapes=list(scratch),
        ),
        out_shape=out_shape,
        input_output_aliases=aliases or {},
        compiler_params=pltpu.CompilerParams(
            dimension_semantics=("arbitrary",) * len(grid), vmem_limit_bytes=VMEM_LIMIT
        ),
        cost_estimate=pl.CostEstimate(flops=int(flops), bytes_accessed=int(moved), transcendentals=0),
        name=name,
    )(*args)


def shape_of(shape, dtype=BF):
    return jax.ShapeDtypeStruct(shape, dtype)


def fixed(shape, buffers=None):
    mode = {} if buffers is None else {"pipeline_mode": pl.Buffered(buffers)}
    return pl.BlockSpec(shape, lambda *_: (0,) * len(shape), **mode)


def piece_specs(pieces, tile):
    specs, spans, start = [], [], 0
    for piece in pieces:
        tiles = piece.shape[0] // tile
        specs.append(
            pl.BlockSpec(
                (tile, piece.shape[1]),
                lambda i, *_, start=start, tiles=tiles: (jnp.clip(i - start, 0, tiles - 1), 0),
            )
        )
        spans.append((start, start + tiles))
        start += tiles
    return specs, spans


def copy_piece(refs, spans, index, target):
    for ref, (first, last) in zip(refs, spans):

        @pl.when((index >= first) & (index < last))
        def _(ref=ref):
            target[...] = ref[...]


def act_back_kernel(spans, others, *refs):
    weight_ref = refs[len(spans)]
    whole_ref, out_ref = refs[len(spans) + 1 + others :]
    copy_piece(refs[: len(spans)], spans, pl.program_id(0), whole_ref)
    out_ref[...] = dot(whole_ref[...], weight_ref[...]).astype(BF)


def act_back(pieces, weight, first, rows, before=()):
    specs, spans = piece_specs(pieces, TILE)
    tiles, skip, width = spans[-1][1], first // TILE, weight.shape[1]
    by_row = lambda w: pl.BlockSpec((TILE, w), lambda i: (skip + i, 0))
    count = len(pieces) + 1
    return call(
        functools.partial(act_back_kernel, spans, len(before)), (tiles,),
        specs + [fixed(weight.shape)] + [pl.BlockSpec(memory_space=pl.ANY)] * len(before),
        [by_row(D), by_row(width)], [shape_of((rows, D)), shape_of((rows, width))],
        (*pieces, weight, *before), "act_back", flops=2 * tiles * TILE * D * width, moved=tiles * TILE * D * 6,
        aliases={count + k: k for k in range(len(before))},
    )


def pack_qkv_kernel(kv_local, me_ref, q_ref, k_ref, v_ref, gains_ref, out_ref):
    width = GROUP * HEAD_DIM
    parts = []
    for g in range(kv_local):
        head = slice(g * HEAD_DIM, (g + 1) * HEAD_DIM)
        parts += [q_ref[:, g * width : (g + 1) * width], jnp.concatenate([k_ref[:, head], v_ref[:, head]], axis=1)]
    out_ref[...] = jnp.concatenate(parts + [gains_ref[...]], axis=1)


def pack_qkv(me_row, query_weight, key_weight, value_weight, gains, kv_local):
    rows = query_weight.shape[0]
    q_width, kv_width = kv_local * GROUP * HEAD_DIM, kv_local * HEAD_DIM
    total = q_width + 2 * kv_width + LANES
    mine = lambda width: pl.BlockSpec((rows, width), lambda i, me: (0, me[0]))
    return call(
        functools.partial(pack_qkv_kernel, kv_local), (1,),
        [mine(q_width), mine(kv_width), mine(kv_width), fixed((rows, LANES))],
        fixed((rows, total)), shape_of((rows, total)),
        (me_row, query_weight, key_weight, value_weight, gains), "pack_qkv", moved=4 * rows * total, prefetch=1,
    )


def pack_rows_kernel(me_ref, in_ref, out_ref):
    out_ref[...] = in_ref[...].astype(F32).T.astype(BF)


def pack_rows(me_row, weight, rows, owners=(0,)):
    tile = 512
    tiles, columns = rows // tile, weight.shape[1]

    def index(i, me):
        owner = sum(jnp.where(i // tiles == k, owner, 0) for k, owner in enumerate(owners))
        return ((me[0] ^ owner) * tiles + i % tiles, 0)

    return call(
        pack_rows_kernel, (tiles * len(owners),), [pl.BlockSpec((tile, columns), index)],
        pl.BlockSpec((columns, tile), lambda i, me: (0, i)), shape_of((columns, rows * len(owners))), (me_row, weight),
        "pack_rows", moved=4 * rows * columns, prefetch=1,
    )


def pack_pair_kernel(me_ref, a_ref, b_ref, out_ref):
    width = a_ref.shape[1]
    out_ref[:, :width] = a_ref[...]
    out_ref[:, width:] = b_ref[...]


def pack_pair(me_row, a, b, chunks, chunk, width):
    rows = a.shape[0]
    spec = pl.BlockSpec((rows, width), lambda i, me: (0, me[0] * chunks + chunk))
    return call(
        pack_pair_kernel, (1,), [spec, spec], fixed((rows, 2 * width)), shape_of((rows, 2 * width)), (me_row, a, b),
        "pack_pair", moved=8 * rows * width, prefetch=1,
    )


def enter_kernel(kv_local, spans, others, *refs):
    pieces = refs[: len(spans)]
    gain_ref, w_ref, cos_ref, sin_ref = refs[len(spans) : len(spans) + 4]
    x_ref, normed_ref, q_ref, k_ref, v_ref = refs[len(spans) + 4 + others :]
    copy_piece(pieces, spans, pl.program_id(0), x_ref)
    x = x_ref[...].astype(F32)
    inv = lax.rsqrt(jnp.mean(x * x, axis=-1, keepdims=True) + EPSILON)
    normed = (x * inv * gain_ref[...]).astype(BF)
    normed_ref[...] = normed
    width = GROUP * HEAD_DIM
    step = width + 2 * HEAD_DIM
    lin = dot(normed, w_ref[:, : kv_local * step])
    cosine, sine = cos_ref[...], sin_ref[...]
    for g in range(kv_local):
        for start in range(0, width, LANES):
            part = turn(lin[:, g * step + start : g * step + start + LANES], cosine, sine) * SCALE
            q_ref[:, g * width + start : g * width + start + LANES] = part.astype(BF)
        pair = lin[:, g * step + width : (g + 1) * step]
        k_ref[g] = turn(pair, cosine, sine)[:, :HEAD_DIM].astype(BF)
        v_ref[g] = pair[:, HEAD_DIM:].astype(BF)


def enter(pieces, gain_row, weight, cosine, sine, kv_local, first, rows, before=()):
    specs, spans = piece_specs(pieces, TILE)
    tiles, skip = spans[-1][1], first // TILE
    q_width = kv_local * GROUP * HEAD_DIM
    by_row = lambda width: pl.BlockSpec((TILE, width), lambda i: (skip + i, 0))
    by_head = pl.BlockSpec((kv_local, TILE, HEAD_DIM), lambda i: (0, skip + i, 0))
    heads = shape_of((kv_local, rows, HEAD_DIM))
    count = len(pieces) + 4
    return call(
        functools.partial(enter_kernel, kv_local, spans, len(before)), (tiles,),
        specs
        + [fixed((1, D)), fixed(weight.shape), by_row(LANES), by_row(LANES)]
        + [pl.BlockSpec(memory_space=pl.ANY)] * len(before),
        [by_row(D), by_row(D), by_row(q_width), by_head, by_head],
        [shape_of((rows, D)), shape_of((rows, D)), shape_of((rows, q_width)), heads, heads],
        (*pieces, gain_row, weight, cosine, sine, *before), "enter",
        flops=2 * tiles * TILE * D * weight.shape[1], moved=tiles * TILE * D * 8,
        aliases={count + k: k for k in range(len(before))},
    )


def allowed_bias(rows, size, first, query_row, key_col, diagonal):
    allowed = key_col == query_row
    if diagonal:
        key_pos = lax.broadcasted_iota(jnp.int32, (size, rows - first), 0)
        query_pos = lax.broadcasted_iota(jnp.int32, (size, rows - first), 1)
        allowed = (allowed & (key_pos <= query_pos)) | (key_pos == query_pos)
    return jnp.where(allowed, 0.0, NEGATIVE)


def attend_one_kernel(rows, me_ref, q_ref, k_ref, v_ref, query_row_ref, key_col_ref, out_ref, total_ref, v_t, peak, total, acc):
    index = pl.program_id(1)
    me = me_ref[0]
    half = rows // 2

    @pl.when(index == 0)
    def _():
        v_t[...] = v_ref[0].astype(F32).T.astype(BF)

    peak[...] = jnp.full(peak.shape, NEGATIVE, F32)
    total[...] = jnp.zeros(total.shape, F32)
    acc[...] = jnp.zeros(acc.shape, F32)

    def visit(at, size, first, diagonal):
        keys = k_ref[0, pl.ds(at, size), :]
        values_t = v_t[:, pl.ds(at, size)]
        bias = allowed_bias(rows, size, first, query_row_ref[:, first:], key_col_ref[pl.ds(at, size), :], diagonal)
        for head in range(GROUP):
            query = q_ref[first:, head * HEAD_DIM : (head + 1) * HEAD_DIM]
            scores = dot(keys, query, NT) + bias
            old = peak[head : head + 1, first:]
            new = jnp.maximum(old, jnp.max(scores, axis=0, keepdims=True))
            expo = jnp.exp(scores - new)
            fade = jnp.exp(old - new)
            peak[head : head + 1, first:] = new
            total[head : head + 1, first:] = total[head : head + 1, first:] * fade + jnp.sum(expo, axis=0, keepdims=True)
            acc[head, :, first:] = acc[head, :, first:] * fade + dot(values_t, expo.astype(BF))

    here = pl.multiple_of((index ^ me) * rows, rows)
    visit(here, half, 0, True)
    visit(pl.multiple_of(here + half, half), half, half, True)

    def step(j, _):
        visit(pl.multiple_of((j ^ me) * rows, rows), rows, 0, False)
        return 0

    lax.fori_loop(0, index, step, 0)
    for head in range(GROUP):
        out = acc[head] / total[head : head + 1, :]
        out_ref[:, head * HEAD_DIM : (head + 1) * HEAD_DIM] = out.T.astype(BF)
    total_ref[0] = peak[...] + jnp.log(total[...])


def attend_one(me_row, q, k, v, query_row, key_col, rows, group):
    length = k.shape[1]
    width = GROUP * HEAD_DIM
    head = pl.BlockSpec((1, length, HEAD_DIM), lambda g, i, me: (group, 0, 0))
    return call(
        functools.partial(attend_one_kernel, rows), (1, length // rows),
        [
            pl.BlockSpec((rows, width), lambda g, i, me: (i ^ me[0], group)),
            head,
            head,
            pl.BlockSpec((1, rows), lambda g, i, me: (0, i ^ me[0])),
            fixed((length, 1)),
        ],
        [
            pl.BlockSpec((rows, width), lambda g, i, me: (i ^ me[0], 0)),
            pl.BlockSpec((1, GROUP, rows), lambda g, i, me: (0, 0, i ^ me[0])),
        ],
        [shape_of((length, width)), shape_of((1, GROUP, length), F32)],
        (me_row, q, k, v, query_row, key_col), "attend", flops=2.6e10, moved=1 << 22, prefetch=1,
        scratch=[
            pltpu.VMEM((HEAD_DIM, length), BF),
            pltpu.VMEM((GROUP, rows), F32),
            pltpu.VMEM((GROUP, rows), F32),
            pltpu.VMEM((GROUP, HEAD_DIM, rows), F32),
        ],
    )


def leave_kernel(groups, per, tiles, core_ref, x_ref, gain_ref, *refs):
    heads, weights, (normed_ref, attn_ref) = refs[: 5 * groups], refs[5 * groups : 5 * groups + 7], refs[5 * groups + 7 :]
    index = pl.program_id(0)
    stored = ((index // per) ^ 3) * per + index % per
    is_low = stored < tiles // 2
    attn, mine, other = None, 0.0, 0.0
    for k in range(4):
        parts = [
            heads[5 * g + k][...] if k < 3 else jnp.where(is_low, heads[5 * g + 3][...], heads[5 * g + 4][...])
            for g in range(groups)
        ]
        part = jnp.concatenate(parts, axis=1)
        if k == 0:
            attn = dot(part, weights[0][...], NT)
        else:
            mine = mine + dot(part, weights[k][...], NT)
            other = other + dot(part, weights[3 + k][...], NT)
    attn = attn + in_order(core_ref[0], mine, other)
    middle = x_ref[...].astype(F32) + attn
    inv = lax.rsqrt(jnp.mean(middle * middle, axis=-1, keepdims=True) + EPSILON)
    normed_ref[...] = (middle * inv * gain_ref[...]).astype(BF)

    @pl.when(index < per)
    def _():
        attn_ref[...] = attn


def weight_specs(weights):
    plain = [fixed(w.shape, 1) for w in weights if len(w.shape) == 2]
    stacked = [w.shape[1:] for w in weights if len(w.shape) == 3]
    return plain + [
        pl.BlockSpec((None,) + shape, lambda *_, k=k: (k, 0, 0), pipeline_mode=pl.Buffered(1))
        for shape in stacked
        for k in range(3)
    ]


def weight_args(weights):
    return [w for w in weights for _ in range(3 if len(w.shape) == 3 else 1)]


def leave(core_row, x_all, gain_row, heads, weights, rows):
    length = x_all.shape[0]
    per, tiles = rows // TILE, length // TILE
    by_row = pl.BlockSpec((TILE, D), lambda i, core: (i, 0))

    def head_spec(k, low, high, width):
        return pl.BlockSpec(
            (TILE, width), lambda i, core: (jnp.clip(((i // per) ^ k) * per + i % per - low, 0, high - low - 1), 0)
        )

    specs = []
    for pieces in heads:
        width = pieces[0].shape[1]
        for k in range(3):
            specs.append(head_spec(k, 0, tiles, width))
        specs += [head_spec(3, 0, tiles // 2, width), head_spec(3, tiles // 2, tiles, width)]
    return call(
        functools.partial(leave_kernel, len(heads), per, tiles), (tiles,),
        [by_row, fixed((1, D))] + specs + weight_specs(weights),
        [by_row, pl.BlockSpec((TILE, D), lambda i, core: (jnp.minimum(i, per - 1), 0))],
        [shape_of((length, D)), shape_of((rows, D), F32)],
        (core_row, x_all, gain_row, *[p for pieces in heads for p in pieces], *weight_args(weights)), "leave",
        flops=2 * length * D * D, moved=length * D * 8, prefetch=1,
    )


def up_kernel(normed_ref, gate_ref, up_ref, grad_ref, act_ref, grad_gate_ref, grad_up_ref):
    normed = normed_ref[...]
    for start in range(0, act_ref.shape[1], 256):
        part = slice(start, start + 256)
        gate = dot(normed, gate_ref[:, part])
        up = dot(normed, up_ref[:, part])
        grad = grad_ref[:, part].astype(F32)
        sigmoid = jax.nn.sigmoid(gate)
        silu = gate * sigmoid
        act_ref[:, part] = (silu * up).astype(BF)
        grad_gate_ref[:, part] = (grad * up * (sigmoid + silu * (1.0 - sigmoid))).astype(BF)
        grad_up_ref[:, part] = (grad * silu).astype(BF)


def up_project(normed, gate_up, grad_act, chunk):
    length, width = normed.shape[0], gate_up.shape[1] // 2
    tall, wide = 1024, 512
    across = width // wide
    out = pl.BlockSpec((tall, wide), lambda i, j: (i, j))
    return call(
        up_kernel, (length // tall, across),
        [
            pl.BlockSpec((tall, D), lambda i, j: (i, 0)),
            pl.BlockSpec((D, wide), lambda i, j: (0, j)),
            pl.BlockSpec((D, wide), lambda i, j: (0, across + j)),
            pl.BlockSpec((tall, wide), lambda i, j: (i, chunk * across + j)),
        ],
        [out] * 3, [shape_of((length, width))] * 3, (normed, gate_up, gate_up, grad_act), "up_project",
        flops=4 * length * D * width, moved=length * (D + 4 * width) * 2 + 8 * D * width,
    )


def sum_kernel(places, count, *refs):
    total = None
    for i in range(0, 2 * count, 2):
        part = dot(refs[i][...], refs[i + 1][...], NT)
        total = part if total is None else total + part
    total = total.astype(BF)
    for (tile, start, size), ref in zip(places, refs[2 * count :]):

        @pl.when(pl.program_id(0) == tile)
        def _(start=start, size=size, ref=ref):
            ref[...] = total[start : start + size]


def sum_of(terms, first, rows, halves):
    tall, wide = 512, 512
    specs, args = [], []
    for left, right, column in terms:
        width = left.shape[1]
        specs.append(pl.BlockSpec((tall, width), lambda i, j: (first // tall + i, 0)))
        specs.append(pl.BlockSpec((wide, width), lambda i, j, column=column: (j, column)))
        args += [left, right]
    size = tall // 2 if halves else tall
    places = [(i, start, size) for i in range(rows // tall) for start in range(0, tall, size)]
    last = D // wide - 1
    depth = sum(left.shape[1] for left, _, _ in terms)

    def out_spec(tile):
        return pl.BlockSpec((size, wide), lambda i, j: (0, jnp.where(i == tile, j, jnp.where(i < tile, 0, last))))

    return call(
        functools.partial(sum_kernel, places, len(terms)), (rows // tall, D // wide), specs,
        [out_spec(tile) for tile, _, _ in places], [shape_of((size, D))] * len(places), args, "sum_of",
        flops=2 * rows * D * depth, moved=2 * depth * (rows + D) + 2 * rows * D,
    )


def outer_kernel(across, count, left_ref, *refs):
    for k in range(count):

        @pl.when(pl.program_id(1) // across == k)
        def _(k=k):
            refs[-1][...] = dot(left_ref[...], refs[k][...], TN).astype(BF)


def outer(left, rights, wide, total=None):
    length, tall, width = left.shape[0], 1024, rights[0].shape[1]
    across, count = width // wide, len(rights)
    right_spec = lambda k: pl.BlockSpec((length, wide), lambda i, j: (0, jnp.clip(j - k * across, 0, across - 1)))
    return call(
        functools.partial(outer_kernel, across, count), (left.shape[1] // tall, across * count),
        [pl.BlockSpec((length, tall), lambda i, j: (0, i))] + [right_spec(k) for k in range(count)],
        pl.BlockSpec((tall, wide), lambda i, j: (i, j)), shape_of((left.shape[1], total or width * count)),
        (left, *rights), "outer", flops=2 * length * left.shape[1] * width * count,
        moved=2 * (length + left.shape[1]) * (left.shape[1] + width * count),
    )


def outer_local_kernel(groups, left_ref, *refs):
    for k in range(4):

        @pl.when(pl.program_id(1) == k)
        def _(k=k):
            right = jnp.concatenate([refs[4 * g + k][...] for g in range(groups)], axis=1)
            refs[-1][...] = dot(left_ref[...], right, TN).astype(BF)


def outer_local(left, heads):
    rows, width, tall = left.shape[0], heads[0][0].shape[1], 1024
    specs, args = [], []
    for pieces in heads:
        for k, piece, block in ((0, pieces[0], 0), (1, pieces[1], 1), (2, pieces[2], 2), (3, pieces[4], 1)):
            specs.append(pl.BlockSpec((rows, width), lambda i, k, block=block: (block, 0)))
            args.append(piece)
    across = width * len(heads)
    return call(
        functools.partial(outer_local_kernel, len(heads)), (D // tall, 4),
        [pl.BlockSpec((rows, tall), lambda i, k: (0, i))] + specs, pl.BlockSpec((tall, across), lambda i, k: (i, k)),
        shape_of((D, 4 * across)), (left, *args), "outer_local", flops=8 * rows * D * across,
        moved=2 * D * (rows + 4 * across),
    )


def outer_rows_kernel(count, *refs):
    for k in range(count):

        @pl.when(pl.program_id(0) == k)
        def _(k=k):
            refs[-1][...] = dot(refs[k][...], refs[count][...], TN).astype(BF)


def outer_rows(lefts, right, shard):
    length, width = lefts[0].shape
    count, shards = len(lefts), right.shape[1] // shard
    return call(
        functools.partial(outer_rows_kernel, count), (count, shards),
        [pl.BlockSpec((length, width), lambda f, s: (0, 0))] * count + [pl.BlockSpec((length, shard), lambda f, s: (0, s))],
        pl.BlockSpec((width, shard), lambda f, s: (s * count + f, 0)), shape_of((shards * count * width, shard)),
        (*lefts, right), "outer_rows", flops=2 * length * right.shape[1] * width * count,
        moved=2 * (length + right.shape[1]) * width * count,
    )


def two_halves(refs):
    return jnp.where(pl.program_id(0) == 0, refs[0][...], refs[1][...]).astype(F32)


def turn_back_kernel(core_ref, own_ref, x_low, x_high, y_low, y_high, x_ref, attn_ref, cot_ref, valid_ref, gain_ref, *refs):
    weights, (middle_ref, low_ref, heads_ref) = refs[:7], refs[7:]
    grad = own_ref[...].astype(F32) + two_halves((x_low, x_high)) + two_halves((y_low, y_high))
    middle = x_ref[...].astype(F32) + attn_ref[...]
    inv = lax.rsqrt(jnp.mean(middle * middle, axis=-1, keepdims=True) + EPSILON)
    grad_middle = cot_ref[...].astype(F32) * valid_ref[...] + norm_back(grad, middle, inv, gain_ref[...])
    middle_ref[...] = grad_middle
    low = grad_middle.astype(BF)
    low_ref[...] = low
    first, second = low[:, : D // 2], low[:, D // 2 :]
    mine = jnp.where(core_ref[0] == 0, first, second)
    other = jnp.where(core_ref[0] == 0, second, first)
    heads_ref[0] = dot(low, weights[0][...]).astype(BF)
    for k in range(1, 4):
        heads_ref[k] = (dot(mine, weights[k][...]) + dot(other, weights[3 + k][...])).astype(BF)


def turn_back(core_row, own, terms, x, attn, cot, valid_col, gain_row, weights):
    rows, width = x.shape[0], weights[0].shape[1]
    by_row = lambda w: pl.BlockSpec((TILE, w), lambda i, core: (i, 0))
    return call(
        turn_back_kernel, (rows // TILE,),
        [by_row(D)] + [fixed((TILE, D))] * 4 + [by_row(D)] * 3 + [by_row(1), fixed((1, D))] + weight_specs(weights),
        [by_row(D), by_row(D), pl.BlockSpec((4, TILE, width), lambda i, core: (0, i, 0))],
        [shape_of((rows, D), F32), shape_of((rows, D)), shape_of((4, rows, width))],
        (core_row, own, *terms, x, attn, cot, valid_col, gain_row, *weight_args(weights)), "turn_back",
        flops=8 * rows * D * width, moved=rows * D * 20, prefetch=1,
    )


def last_kernel(own_ref, by_x_ref, by_y_ref, x_ref, attn_ref, valid_ref, out_ref, stats_ref):
    mlp = own_ref[...].astype(F32) + by_x_ref[...].astype(F32) + by_y_ref[...].astype(F32)
    x, attn, valid = x_ref[...].astype(F32), attn_ref[...], valid_ref[...]
    middle = x + attn
    final = middle + mlp
    out_ref[...] = final.astype(BF)

    @pl.when(pl.program_id(0) == 0)
    def _():
        stats_ref[...] = jnp.zeros(stats_ref.shape, F32)

    for row, part in enumerate((x, middle, final, attn, mlp)):
        stats_ref[row : row + 1, :] += fold(jnp.sum(valid * part * part, axis=0, keepdims=True))


def last(own, by_x, by_y, x, attn, valid_col):
    rows = x.shape[0]
    by_row = lambda w: pl.BlockSpec((TILE, w), lambda i: (i, 0))
    return call(
        last_kernel, (rows // TILE,), [by_row(D)] * 5 + [by_row(1)], [by_row(D), fixed((8, LANES))],
        [shape_of((rows, D)), shape_of((8, LANES), F32)], (own, by_x, by_y, x, attn, valid_col), "last",
        moved=rows * D * 20,
    )


def attend_back_one_kernel(rows, count, me_ref, *refs):
    q_ref, k_ref, v_ref, out_ref, own, by_x, by_y, by_xy, total_ref, query_row_ref, key_col_ref = refs[:11]
    cos_ref, sin_ref, cos_t_ref, sin_t_ref, dqkv_ref, grad_ref, k_t, inner, dq_t, dk_acc, dv_acc = refs[11:]
    me = me_ref[0]
    half, width = HEAD_DIM // 2, GROUP * HEAD_DIM
    for block, ref in enumerate((own, by_x, by_y, by_xy)):
        grad_ref[block * rows : (block + 1) * rows, :] = ref[...] if len(ref.shape) == 2 else ref[0]
    k_t[...] = k_ref[0].astype(F32).T.astype(BF)
    dq_t[...] = jnp.zeros(dq_t.shape, F32)

    def prepare(i, _):
        here = pl.ds(pl.multiple_of(i * rows, rows), rows)
        for head in range(GROUP):
            cols = slice(head * HEAD_DIM, (head + 1) * HEAD_DIM)
            both = out_ref[here, cols].astype(F32) * grad_ref[here, cols].astype(F32)
            inner[head : head + 1, here] = jnp.sum(both.T, axis=0, keepdims=True)
        return 0

    lax.fori_loop(0, count, prepare, 0)

    def visit(key_at, size, local, query_at, first, diagonal):
        keys_here = pl.ds(key_at, size)
        here = pl.ds(pl.multiple_of(query_at + first, rows // 2), rows - first)
        keys, values, keys_t = k_ref[0, keys_here, :], v_ref[0, keys_here, :], k_t[:, keys_here]
        bias = allowed_bias(rows, size, first, query_row_ref[:, here], key_col_ref[keys_here, :], diagonal)
        for head in range(GROUP):
            cols = slice(head * HEAD_DIM, (head + 1) * HEAD_DIM)
            query, grad = q_ref[here, cols], grad_ref[here, cols]
            probs = jnp.exp(dot(keys, query, NT) + bias - total_ref[0, head : head + 1, here])
            dv_acc[local : local + size, :] += dot(probs.astype(BF), grad)
            grad_probs = dot(values, grad, NT)
            grad_scores = (probs * (grad_probs - inner[head : head + 1, here])).astype(BF)
            dk_acc[local : local + size, :] += dot(grad_scores, query)
            dq_t[head, :, here] += dot(keys_t, grad_scores)

    def key_step(j, _):
        key_start = pl.multiple_of((j ^ me) * rows, rows)
        key_at = pl.ds(key_start, rows)
        dk_acc[...] = jnp.zeros(dk_acc.shape, F32)
        dv_acc[...] = jnp.zeros(dv_acc.shape, F32)
        visit(key_start, rows // 2, 0, key_start, 0, True)
        visit(pl.multiple_of(key_start + rows // 2, rows // 2), rows // 2, rows // 2, key_start, rows // 2, True)

        def query_step(i, _):
            visit(key_start, rows, 0, pl.multiple_of((i ^ me) * rows, rows), 0, False)
            return 0

        lax.fori_loop(j + 1, count, query_step, 0)
        dk = dk_acc[...]
        low, high = dk[:, :half], dk[:, half:]
        cosine, sine = cos_ref[key_at, :half], sin_ref[key_at, half:HEAD_DIM]
        turned = jnp.concatenate([low * cosine + high * sine, high * cosine - low * sine], axis=1)
        dqkv_ref[key_at, width : width + HEAD_DIM] = turned.astype(BF)
        dqkv_ref[key_at, width + HEAD_DIM :] = dv_acc[...].astype(BF)
        return 0

    lax.fori_loop(0, count, key_step, 0)

    def finish_queries(i, _):
        here = pl.ds(pl.multiple_of(i * rows, rows), rows)
        cosine, sine = cos_t_ref[:, here], sin_t_ref[:, here]
        for head in range(GROUP):
            low, high = dq_t[head, :half, here], dq_t[head, half:, here]
            turned = jnp.concatenate([low * cosine + high * sine, high * cosine - low * sine], axis=0) * SCALE
            dqkv_ref[here, head * HEAD_DIM : (head + 1) * HEAD_DIM] = turned.T.astype(BF)
        return 0

    lax.fori_loop(0, count, finish_queries, 0)


def attend_back_one(me_row, q, k, v, out, grads, totals, query_row, key_col, tables, rows, group):
    length = k.shape[1]
    width = GROUP * HEAD_DIM
    whole = lambda shape: fixed(shape, 1)
    head = pl.BlockSpec((1, length, HEAD_DIM), lambda i, me: (group, 0, 0), pipeline_mode=pl.Buffered(1))
    part = pl.BlockSpec((rows, width), lambda i, me: (0, group))
    own = pl.BlockSpec((1, rows, width), lambda i, me: (0, 0, group))
    out_width = width + 2 * HEAD_DIM
    return call(
        functools.partial(attend_back_one_kernel, rows, length // rows), (1,),
        [
            pl.BlockSpec((length, width), lambda i, me: (0, group)), head, head, whole((length, width)),
            own, part, part, part, whole((1, GROUP, length)), whole((1, length)), whole((length, 1)),
            whole((length, LANES)), whole((length, LANES)),
            whole((HEAD_DIM // 2, length)), whole((HEAD_DIM // 2, length)),
        ],
        whole((length, out_width)), shape_of((length, out_width)),
        (me_row, q, k, v, out, *grads, totals, query_row, key_col, *tables), "attend_back",
        flops=3.4e10, moved=1 << 22, prefetch=1,
        scratch=[
            pltpu.VMEM((length, width), BF),
            pltpu.VMEM((HEAD_DIM, length), BF),
            pltpu.VMEM((GROUP, length), F32),
            pltpu.VMEM((GROUP, HEAD_DIM, length), F32),
            pltpu.VMEM((rows, HEAD_DIM), F32),
            pltpu.VMEM((rows, HEAD_DIM), F32),
        ],
    )


def finish_kernel(groups, step, core_ref, x_ref, middle_ref, gain_ref, *refs):
    grads, weights, out_ref = refs[: 4 * groups], refs[4 * groups : 4 * groups + 7], refs[-1]
    grad, mine, other = None, 0.0, 0.0
    for k in range(4):
        low = jnp.concatenate([grads[4 * g + k][...] for g in range(groups)], axis=1)
        if k == 0:
            grad = dot(low, weights[0][:, : groups * step], NT)
        else:
            mine = mine + dot(low, weights[k][...], NT)
            other = other + dot(low, weights[3 + k][...], NT)
    grad = grad + in_order(core_ref[0], mine, other)
    x = x_ref[...].astype(F32)
    inv = lax.rsqrt(jnp.mean(x * x, axis=-1, keepdims=True) + EPSILON)
    out_ref[...] = (middle_ref[...] + norm_back(grad, x, inv, gain_ref[...])).astype(BF)


def finish(core_row, x, grad_middle, gain_row, grads, weights):
    rows, step = x.shape[0], grads[0][0].shape[1]
    by_row = lambda w: pl.BlockSpec((TILE, w), lambda i, core: (i, 0))
    return call(
        functools.partial(finish_kernel, len(grads), step), (rows // TILE,),
        [by_row(D), by_row(D), fixed((1, D))] + [by_row(step)] * (4 * len(grads)) + weight_specs(weights),
        by_row(D), shape_of((rows, D)),
        (core_row, x, grad_middle, gain_row, *[p for parts in grads for p in parts], *weight_args(weights)), "finish",
        flops=8 * rows * D * step * len(grads), moved=rows * D * 8 + 4 * D * step * 4, prefetch=1,
    )


def each_piece(refs, emit):
    block = pl.program_id(0)
    for k in range(3):

        @pl.when(block == k)
        def _(k=k):
            emit(refs[k][...])

    @pl.when(block == 3)
    def _():
        emit(jnp.concatenate([refs[3][...], refs[4][...]], axis=0))


def fold(values):
    return sum(values[:, at : at + LANES] for at in range(0, values.shape[1], LANES))


def place_pair_kernel(first, me_ref, *refs):
    pieces, weight_a, weight_b = refs[:5], refs[5], refs[6]
    out_a, out_b, dot_ref = refs[-3:]
    width = out_a.shape[1]

    @pl.when(pl.program_id(0) == 0)
    def _():
        dot_ref[...] = jnp.zeros(dot_ref.shape, F32) if first else refs[9][...]

    def emit(values):
        a, b = values[:, :width].astype(F32), values[:, width:].astype(F32)
        out_a[...], out_b[...] = a, b
        dot_ref[...] += fold(a * weight_a[...].astype(F32)) + fold(b * weight_b[...].astype(F32))

    each_piece(pieces, emit)


def place_pair(me_row, pieces, weight_a, weight_b, chunks, chunk, before):
    rows, total = weight_a.shape
    width = pieces[0].shape[1] // 2
    column = pl.BlockSpec((rows, width), lambda i, me: (0, (i ^ me[0]) * chunks + chunk))
    any_spec = pl.BlockSpec(memory_space=pl.ANY)
    specs = [fixed(p.shape) for p in pieces] + [column, column]
    args = [me_row, *pieces, weight_a, weight_b]
    aliases = {}
    if before is not None:
        specs += [any_spec, any_spec, fixed((rows, LANES))]
        args += before
        aliases = {8: 0, 9: 1}
    return call(
        functools.partial(place_pair_kernel, before is None), (4,), specs, [column, column, fixed((rows, LANES))],
        [shape_of((rows, total), F32)] * 2 + [shape_of((rows, LANES), F32)], args, "place_pair",
        moved=rows * width * 64, prefetch=1, aliases=aliases,
    )


def place_rows_kernel(half, me_ref, *refs):
    block, tile = pl.program_id(0), pl.program_id(1)
    for k in range(5):
        first = jnp.minimum(block, 3) == min(k, 3)

        @pl.when(first if k < 3 else first & ((tile < half) == (k == 3)))
        def _(k=k):
            refs[5][...] = refs[k][...].astype(F32)


def place_rows(me_row, pieces, tall):
    rows, columns = pieces[0].shape
    across = rows // tall
    half = across // 2

    def spec(k):
        if k < 3:
            return pl.BlockSpec((tall, columns), lambda i, j, me: (jnp.where(i == k, j, 0), 0))
        low = (k - 3) * half
        return pl.BlockSpec((tall, columns), lambda i, j, me: (jnp.where(i == 3, jnp.clip(j - low, 0, half - 1), 0), 0))

    return call(
        functools.partial(place_rows_kernel, half), (4, across), [spec(k) for k in range(5)],
        pl.BlockSpec((tall, columns), lambda i, j, me: ((i ^ me[0]) * across + j, 0)),
        shape_of((4 * rows, columns), F32), (me_row, *pieces), "place_rows", moved=rows * columns * 24, prefetch=1,
    )


def place_attn_kernel(kv_local, me_ref, *refs):
    pieces, weights, outs, out_ref, dot_ref = refs[:5], refs[5:8], refs[8:11], refs[11], refs[12]
    width = GROUP * HEAD_DIM
    step = width + 2 * HEAD_DIM

    @pl.when(pl.program_id(0) == 0)
    def _():
        dot_ref[...] = jnp.zeros(dot_ref.shape, F32)

    def emit(values):
        values = values.astype(F32)
        take = lambda start, size: jnp.concatenate(
            [values[:, g * step + start : g * step + start + size] for g in range(kv_local)], axis=1
        )
        parts = (take(0, width), take(width, HEAD_DIM), take(width + HEAD_DIM, HEAD_DIM))
        for part, weight, out in zip(parts, weights, outs):
            out[...] = part
            dot_ref[...] += fold(part * weight[...].astype(F32))
        out_ref[...] = values[:, kv_local * step :].T

    each_piece(pieces, emit)


def place_attn(me_row, pieces, query_weight, key_weight, value_weight, kv_local):
    rows = query_weight.shape[0]
    q_width = kv_local * GROUP * HEAD_DIM
    column = lambda width: pl.BlockSpec((rows, width), lambda i, me: (0, i ^ me[0]))
    columns = [column(q_width), column(kv_local * HEAD_DIM), column(kv_local * HEAD_DIM)]
    weights = (query_weight, key_weight, value_weight)
    return call(
        functools.partial(place_attn_kernel, kv_local), (4,), [fixed(p.shape) for p in pieces] + columns,
        columns + [pl.BlockSpec((q_width, rows), lambda i, me: (i ^ me[0], 0)), fixed((rows, LANES))],
        [shape_of(w.shape, F32) for w in weights] + [shape_of((4 * q_width, rows), F32), shape_of((rows, LANES), F32)],
        (me_row, *pieces, *weights), "place_attn", moved=rows * 5120 * 8, prefetch=1,
    )


CHUNKS = 2


def square_body(
    inputs, cotangent, segments, valid_mask, query_weight, key_weight, value_weight, out_weight,
    gate_weight, up_weight, down_weight, attn_gain, mlp_gain,
):
    count = 4
    me = lax.axis_index("seq")
    me_row = me.reshape(1).astype(jnp.int32)
    core = lax.axis_index("fsdp") % 2
    core_row = core.reshape(1).astype(jnp.int32)
    rows = inputs.shape[1]
    length = rows * count
    kv_local = KV_HEADS // count
    q_width = kv_local * GROUP * HEAD_DIM
    ff_local = FF // count
    ff_chunk = ff_local // CHUNKS
    shard_rows = gate_weight.shape[0]
    step = (GROUP + 2) * HEAD_DIM

    tokens_low, cot_low = inputs[0], cotangent[0]
    marks = jnp.stack([segments[0], valid_mask[0]])
    marks_all = jnp.stack([marks] + [swap(marks, k) for k in range(1, count)])
    x_own = after(tokens_low, marks_all)
    x_x, x_y = to_both(x_own)

    segment_all = marks_all[:, 0].reshape(length)
    valid_all = marks_all[:, 1].reshape(length)
    valid_col = valid_mask[0].astype(F32)[:, None]

    position = (
        (jnp.arange(count, dtype=jnp.int32) ^ me)[:, None] * rows + jnp.arange(rows, dtype=jnp.int32)[None, :]
    ).reshape(length)
    same = (segment_all[:, None] == segment_all[None, :]) & (position[None, :] < position[:, None])
    places = jnp.sum(same.astype(jnp.int32), axis=1).astype(F32)
    half = HEAD_DIM // 2
    frequency = ROPE_BASE ** (-2.0 * jnp.arange(half, dtype=F32) / HEAD_DIM)
    angles_t = frequency[:, None] * places[None, :]
    cosine_t, sine_t = jnp.cos(angles_t), jnp.sin(angles_t)
    cosine = jnp.tile(cosine_t.T, (1, LANES // half))
    sign = jnp.tile(jnp.repeat(jnp.array([-1.0, 1.0], F32), half), LANES // HEAD_DIM)
    sine = jnp.tile(sine_t.T, (1, LANES // half)) * sign[None, :]
    query_row = jnp.where(valid_all == 1, segment_all, -1).reshape(1, length)
    key_col = segment_all.reshape(length, 1)
    tables = (cosine, sine, cosine_t, sine_t)

    gains = jnp.pad(jnp.stack([attn_gain, mlp_gain], axis=1), ((0, 0), (0, LANES - 2)))
    qkv_full = gather_fsdp(pack_qkv(me_row, query_weight, key_weight, value_weight, gains, kv_local))
    out_slice = gather_fsdp(pack_rows(me_row, out_weight, q_width))
    gain_one = qkv_full[:, kv_local * step].astype(F32).reshape(1, D)
    gain_two = qkv_full[:, kv_local * step + 1].astype(F32).reshape(1, D)

    x_far = pass_on(x_x, x_y, cosine, sine)
    entered = enter([x_own, x_x, x_y], gain_one, qkv_full, cosine, sine, kv_local, 0, length)

    down_t = gather_fsdp(pack_rows(me_row, after(down_weight, x_x, x_y, cosine, sine), ff_local))
    later_gate = after(gate_weight, x_x, x_y, cosine, sine)
    gate_up = [
        gather_fsdp(pack_pair(me_row, later_gate, up_weight, CHUNKS, c, ff_chunk)) for c in range(CHUNKS)
    ]

    done = (*x_far, entered[0])
    o_mine = [swap(core_half(after(out_slice, *done), core), k) for k in range(1, count)]
    grad_low = (cot_low.astype(F32) * valid_col).astype(BF)
    x_all, normed_one, q, k, v = enter(
        list(x_far), gain_one, qkv_full, cosine, sine, kv_local, 3 * rows, length, tuple(entered)
    )
    out_0, total_0 = attend_one(me_row, q, k, v, query_row, key_col, rows, 0)

    done = (*o_mine, out_0)
    h_x, h_y = to_both(after(out_0, *done))
    o_other = swap_core(jnp.stack([after(w, *done) for w in o_mine]))
    out_pieces = [out_slice, *o_mine, o_other]
    out_1, total_1 = attend_one(me_row, after(q, *done), k, v, query_row, key_col, rows, 1)
    heads, totals = [out_0, out_1], [total_0, total_1]

    done = (h_x, h_y, out_1, o_other)
    h_far = pass_on(h_x, h_y, *done)
    heads_0 = [out_0, h_x, h_y, *h_far]
    h_x, h_y = to_both(after(out_1, *done))

    done = (*h_far, h_x, h_y)
    h_far = pass_on(h_x, h_y, *done)
    heads_1 = [out_1, h_x, h_y, *h_far]
    c_own = after(grad_low, *done)
    c_x, c_y = to_both(c_own)
    normed_two, attn_branch = leave(core_row, after(x_all, *h_far), gain_two, [heads_0, heads_1], out_pieces, rows)

    done = (c_x, c_y, normed_two, down_t)
    c_far = pass_on(c_x, c_y, *done)
    acted = act_back([after(c_own, *done), c_x, c_y], down_t, 0, length)

    done = (*c_far, acted[0])
    w_mine = [swap(core_half(after(qkv_full, *done)[:, : kv_local * step], core), k) for k in range(1, count)]
    grad_mlp, grad_act = act_back(list(c_far), down_t, 3 * rows, length, tuple(acted))
    act_0, gate_0, up_0 = up_project(normed_two, gate_up[0], grad_act, 0)
    grad_0 = outer(normed_two, [gate_0, up_0], 1024)

    done = (*w_mine, grad_0)
    gate_up_0 = scatter_fsdp(after(grad_0, *done))
    w_other = [swap_core(after(w, *done)) for w in w_mine]
    weight_pieces = [qkv_full, *w_mine, *w_other]
    act_1, gate_1, up_1 = up_project(after(normed_two, *done), gate_up[1], grad_act, 1)
    terms = [(gate_0, gate_up[0], 0), (up_0, gate_up[0], 1), (gate_1, gate_up[1], 0), (up_1, gate_up[1], 1)]

    def terms_after(*events):
        return [(after(terms[0][0], *events), *terms[0][1:])] + terms[1:]

    far = sum_of(terms, 3 * rows, rows, True)

    done = (*far, *w_other)
    g_far = send_far(*far)
    near = sum_of(terms_after(*done), rows, 2 * rows, True)
    near = add_far(near, *g_far)
    g_near = send_near(near)
    [own] = sum_of(terms_after(*near), 0, rows, False)
    grad_1 = outer(after(normed_two, own), [gate_1, up_1], 1024)
    gate_up_1 = scatter_fsdp(after(grad_1, *g_near))
    grad_middle, grad_attn, grad_heads = turn_back(
        core_row, after(own, grad_1), g_near, tokens_low, attn_branch, cot_low, valid_col, gain_two, out_pieces
    )

    head_grads = [grad_heads] + [swap(grad_heads[k], k) for k in range(1, count)]
    p_own = after(gate_up_0, grad_attn)
    p_x, p_y = to_both(p_own)
    grad_down = outer_rows([act_0, act_1], after(grad_mlp, grad_attn), shard_rows)
    grad_out = outer_local(after(grad_attn, grad_down), [heads_0, heads_1])

    def attention_back(queries, group):
        return attend_back_one(
            me_row, queries, k, v, heads[group], head_grads, totals[group], query_row, key_col, tables, rows, group
        )

    done = (*head_grads[1:], p_x, p_y, grad_out)
    out_sum = scatter_fsdp(after(grad_out, *done))
    p_far = pass_on(p_x, p_y, *done)
    p_pieces = [p_own, p_x, p_y, *p_far]
    dqkv_0 = attention_back(after(q, *done), 0)

    done = (*p_far, dqkv_0)
    down_sum = scatter_fsdp(after(grad_down, *done))
    p_own = after(gate_up_1, *done)
    p_x, p_y = to_both(p_own)
    parts_0 = exchange_seq(blocks_of(after(dqkv_0, *done), count))
    dqkv_1 = attention_back(after(q, *done), 1)

    done = (p_x, p_y, *parts_0[1:], dqkv_1)
    parts_1 = exchange_seq(blocks_of(after(dqkv_1, *done), count))
    terms = [(act_0, down_t, 0), (act_1, down_t, 1)]
    far = sum_of(terms_after(*done), 3 * rows, rows, True)
    m_far = send_far(*far)
    near = sum_of(terms_after(*far, *parts_1[1:]), rows, 2 * rows, True)

    near = add_far(near, *m_far)
    near = [jnp.concatenate(near[:2]), jnp.concatenate(near[2:])]
    done = (*near, *parts_1[1:])
    m_x, m_y = swap(near[0], 1), swap(near[1], 2)
    p_far = pass_on(p_x, p_y, *done)
    grad_qkv = outer(after(normed_one, *done), [dqkv_0, dqkv_1], step)
    [own] = sum_of(terms_after(grad_qkv), 0, rows, False)
    input_grad = finish(core_row, after(tokens_low, own), grad_middle, gain_one, [parts_0, parts_1], weight_pieces)

    done = (m_x, m_y, *p_far, input_grad)
    qkv_sum = scatter_fsdp(after(grad_qkv, *done))
    input_grad = input_grad[None]
    out_ready = after(out_sum, *done)
    out_terms = exchange_seq([out_ready[:, k * q_width : (k + 1) * q_width] for k in range(count)])
    outputs, stats = last(after(own, *done), m_x, m_y, tokens_low, attn_branch, valid_col)
    outputs = outputs[None]
    placed = place_pair(me_row, [after(p_pieces[0], stats)] + p_pieces[1:], gate_weight, up_weight, CHUNKS, 0, None)

    done = (*out_terms[1:], placed[2])
    out_sum = sum(term.astype(F32) for term in out_terms).astype(BF)
    d_own = after(down_sum, *done)
    d_x, d_y = to_both(d_own)
    gate_grad, up_grad, gate_up_dot = place_pair(
        me_row, [after(p_own, *done), p_x, p_y, *p_far], gate_weight, up_weight, CHUNKS, 1, placed
    )

    done = (d_x, d_y, gate_up_dot)
    d_far = pass_on(d_x, d_y, *done)

    t_own = jnp.concatenate([after(qkv_sum, *d_far), out_sum], axis=1)
    t_x, t_y = to_both(t_own)
    stats = after(stats, *d_far)
    down_grad = place_rows(me_row, [after(down_sum, *d_far), d_x, d_y, *d_far], 1024)
    t_far = pass_on(t_x, t_y, t_x, t_y)
    query_grad, key_grad, value_grad, out_grad, qkv_dot = place_attn(
        me_row, [after(t_own, down_grad), t_x, t_y, *t_far], query_weight, key_weight, value_weight, kv_local
    )
    attn_gain_grad = jnp.sum(qkv_dot, axis=1) / attn_gain.astype(F32)
    mlp_gain_grad = jnp.sum(gate_up_dot, axis=1) / mlp_gain.astype(F32)

    for bit in bit_orders()[0]:
        stats = stats + swap(stats, bit)
    rms_stats = jnp.sqrt(jnp.sum(stats[:5], axis=1)[None, :] / (jnp.sum(valid_all).astype(F32) * D))
    return (
        outputs, input_grad, query_grad, key_grad, value_grad, out_grad, gate_grad, up_grad, down_grad,
        attn_gain_grad, mlp_gain_grad, rms_stats,
    )


def solution(mesh):
    rows_in = P("fsdp", None)
    columns_in = P(None, "fsdp")
    placed = (
        P("fsdp", "seq", None), P("fsdp", "seq", None), P("fsdp", "seq"), P("fsdp", "seq"),
        rows_in, rows_in, rows_in, columns_in, rows_in, rows_in, columns_in, P("fsdp"), P("fsdp"),
    )
    return jax.shard_map(
        square_body if mesh.shape["seq"] == 4 else general_body,
        mesh=mesh,
        in_specs=placed,
        out_specs=(
            P("fsdp", "seq", None), P("fsdp", "seq", None), rows_in, rows_in, rows_in, columns_in,
            rows_in, rows_in, columns_in, P("fsdp"), P("fsdp"), P("fsdp", None),
        ),
        check_vma=False,
    )
```

```python
import functools

import jax
import jax.numpy as jnp
from jax import lax
from jax.experimental import pallas as pl
from jax.experimental.pallas import tpu as pltpu
from jax.sharding import PartitionSpec as P

D = 2048
HEADS = 32
KV_HEADS = 8
HEAD_DIM = 64
GROUP = HEADS // KV_HEADS
FF = 8192
EPSILON = 1e-05
ROPE_BASE = 500000.0
NEGATIVE = -1e30
SCALE = HEAD_DIM**-0.5
BF = jnp.bfloat16
F32 = jnp.float32
LANES = 128
VMEM_LIMIT = 60 * 1024 * 1024
NT = (((1,), (1,)), ((), ()))
NN = (((1,), (0,)), ((), ()))
TN = (((0,), (0,)), ((), ()))


def dot(left, right, dims=NN):
    return lax.dot_general(left, right, dims, preferred_element_type=F32)


def params(grid_rank):
    return pltpu.CompilerParams(
        dimension_semantics=("arbitrary",) * grid_rank, vmem_limit_bytes=VMEM_LIMIT
    )


def swap(values, bit):
    count = lax.axis_size("seq")
    return lax.ppermute(values, "seq", [(i, i ^ bit) for i in range(count)])


def bit_orders():
    bits = [1 << b for b in range(lax.axis_size("seq").bit_length() - 1)]
    return bits, bits[::-1]


def gather_stream(block, order):
    held, owners = block[None], [0]
    for bit in order:
        held = jnp.concatenate([held, swap(held, bit)], axis=0)
        owners = owners + [k ^ bit for k in owners]
    return [held[owners.index(k)] for k in range(len(owners))]


def gather_seq(block):
    half = block.shape[-1] // 2
    low_order, high_order = bit_orders()
    low = gather_stream(block[..., :half], low_order)
    high = gather_stream(block[..., half:], high_order)
    return [jnp.concatenate(pair, axis=-1) for pair in zip(low, high)]


def reduce_stream(blocks, order):
    held = {k: b for k, b in enumerate(blocks)}
    for bit in order:
        away = sorted(k for k in held if k & bit)
        sent = swap(jnp.stack([held[k].astype(BF) for k in away]), bit)
        held = {
            k: held[k].astype(F32) + sent[away.index(k ^ bit)].astype(F32)
            for k in held
            if not k & bit
        }
    return held[0]


def reduce_seq(blocks):
    half = blocks[0].shape[-1] // 2
    low_order, high_order = bit_orders()
    low = reduce_stream([b[..., :half] for b in blocks], low_order)
    high = reduce_stream([b[..., half:] for b in blocks], high_order)
    return jnp.concatenate([low, high], axis=-1)


def exchange_seq(blocks):
    return [b if k == 0 else swap(b, k) for k, b in enumerate(blocks)]


def gather_fsdp(shard):
    return lax.all_gather(shard, "fsdp", axis=0, tiled=True)


def scatter_fsdp(values):
    return lax.psum_scatter(values, "fsdp", scatter_dimension=0, tiled=True)


def turn(values, cosine, sine):
    lane = lax.broadcasted_iota(jnp.int32, values.shape, 1)
    half = HEAD_DIM // 2
    ahead = pltpu.roll(values, LANES - half, 1)
    behind = pltpu.roll(values, half, 1)
    return values * cosine + jnp.where(lane % HEAD_DIM < half, ahead, behind) * sine


def project_kernel(kv_local, x_ref, gain_ref, w_ref, cos_ref, sin_ref, normed_ref, q_ref, k_ref, v_ref):
    x = x_ref[...].astype(F32)
    inv = lax.rsqrt(jnp.mean(x * x, axis=-1, keepdims=True) + EPSILON)
    normed = (x * inv * gain_ref[...]).astype(BF)
    normed_ref[...] = normed
    q_width = kv_local * GROUP * HEAD_DIM
    kv_width = kv_local * HEAD_DIM
    lin = dot(normed, w_ref[:, : q_width + 2 * kv_width])
    cosine, sine = cos_ref[...], sin_ref[...]
    for start in range(0, q_width, LANES):
        part = turn(lin[:, start : start + LANES], cosine, sine) * SCALE
        q_ref[:, start : start + LANES] = part.astype(BF)
    for start in range(0, kv_width, LANES):
        part = turn(lin[:, q_width + start : q_width + start + LANES], cosine, sine)
        for at in range(0, min(LANES, kv_width - start), HEAD_DIM):
            k_ref[(start + at) // HEAD_DIM] = part[:, at : at + HEAD_DIM].astype(BF)
    for head in range(kv_local):
        start = q_width + kv_width + head * HEAD_DIM
        v_ref[head] = lin[:, start : start + HEAD_DIM].astype(BF)


def project(x, gain_row, weight, cosine, sine, kv_local):
    rows = x.shape[0]
    block = 256
    q_width = kv_local * GROUP * HEAD_DIM
    by_row = lambda i: (i, 0)
    whole = lambda i: (0, 0)
    by_head = lambda i: (0, i, 0)
    return pl.pallas_call(
        functools.partial(project_kernel, kv_local),
        grid=(rows // block,),
        in_specs=[
            pl.BlockSpec((block, D), by_row),
            pl.BlockSpec((1, D), whole),
            pl.BlockSpec(weight.shape, whole),
            pl.BlockSpec((block, LANES), by_row),
            pl.BlockSpec((block, LANES), by_row),
        ],
        out_specs=[
            pl.BlockSpec((block, D), by_row),
            pl.BlockSpec((block, q_width), by_row),
            pl.BlockSpec((kv_local, block, HEAD_DIM), by_head),
            pl.BlockSpec((kv_local, block, HEAD_DIM), by_head),
        ],
        out_shape=[
            jax.ShapeDtypeStruct((rows, D), BF),
            jax.ShapeDtypeStruct((rows, q_width), BF),
            jax.ShapeDtypeStruct((kv_local, rows, HEAD_DIM), BF),
            jax.ShapeDtypeStruct((kv_local, rows, HEAD_DIM), BF),
        ],
        compiler_params=params(1),
        cost_estimate=pl.CostEstimate(
            flops=2 * rows * D * weight.shape[1], bytes_accessed=rows * D * 6, transcendentals=0
        ),
        name="project",
    )(x, gain_row, weight, cosine, sine)


def pair_bias(rows, query_index, key_index, query_row, key_col):
    key_pos = key_index * rows + lax.broadcasted_iota(jnp.int32, (rows, rows), 0)
    query_pos = query_index * rows + lax.broadcasted_iota(jnp.int32, (rows, rows), 1)
    allowed = ((key_col == query_row) & (key_pos <= query_pos)) | (key_pos == query_pos)
    return jnp.where(allowed, 0.0, NEGATIVE)


def attend_kernel(rows, me_ref, q_ref, k_ref, v_ref, query_row_ref, key_col_ref, out_ref, total_ref, v_t, peak, total, acc):
    index = pl.program_id(1)
    me = me_ref[0]

    @pl.when(index == 0)
    def _():
        v_t[...] = v_ref[0].astype(F32).T.astype(BF)

    peak[...] = jnp.full(peak.shape, NEGATIVE, F32)
    total[...] = jnp.zeros(total.shape, F32)
    acc[...] = jnp.zeros(acc.shape, F32)

    def step(j, _):
        at = pl.multiple_of((j ^ me) * rows, rows)
        keys = k_ref[0, pl.ds(at, rows), :]
        values_t = v_t[:, pl.ds(at, rows)]
        bias = pair_bias(rows, index, j, query_row_ref[...], key_col_ref[pl.ds(at, rows), :])
        for head in range(GROUP):
            query = q_ref[:, head * HEAD_DIM : (head + 1) * HEAD_DIM]
            scores = dot(keys, query, NT) + bias
            old = peak[head : head + 1, :]
            new = jnp.maximum(old, jnp.max(scores, axis=0, keepdims=True))
            expo = jnp.exp(scores - new)
            fade = jnp.exp(old - new)
            peak[head : head + 1, :] = new
            total[head : head + 1, :] = total[head : head + 1, :] * fade + jnp.sum(expo, axis=0, keepdims=True)
            acc[head] = acc[head] * fade + dot(values_t, expo.astype(BF))
        return 0

    lax.fori_loop(0, index + 1, step, 0)
    for head in range(GROUP):
        out = acc[head] / total[head : head + 1, :]
        out_ref[:, head * HEAD_DIM : (head + 1) * HEAD_DIM] = out.T.astype(BF)
    total_ref[0] = peak[...] + jnp.log(total[...])


def attend(me, q, k, v, query_row, key_col, rows):
    kv_local, length = k.shape[0], k.shape[1]
    count = length // rows
    width = GROUP * HEAD_DIM
    return pl.pallas_call(
        functools.partial(attend_kernel, rows),
        grid_spec=pltpu.PrefetchScalarGridSpec(
            num_scalar_prefetch=1,
            grid=(kv_local, count),
            in_specs=[
                pl.BlockSpec((rows, width), lambda g, i, me: (i ^ me[0], g)),
                pl.BlockSpec((1, length, HEAD_DIM), lambda g, i, me: (g, 0, 0)),
                pl.BlockSpec((1, length, HEAD_DIM), lambda g, i, me: (g, 0, 0)),
                pl.BlockSpec((1, rows), lambda g, i, me: (0, i ^ me[0])),
                pl.BlockSpec((length, 1), lambda g, i, me: (0, 0)),
            ],
            out_specs=[
                pl.BlockSpec((rows, width), lambda g, i, me: (i ^ me[0], g)),
                pl.BlockSpec((1, GROUP, rows), lambda g, i, me: (g, 0, i ^ me[0])),
            ],
            scratch_shapes=[
                pltpu.VMEM((HEAD_DIM, length), BF),
                pltpu.VMEM((GROUP, rows), F32),
                pltpu.VMEM((GROUP, rows), F32),
                pltpu.VMEM((GROUP, HEAD_DIM, rows), F32),
            ],
        ),
        out_shape=[
            jax.ShapeDtypeStruct((length, kv_local * width), BF),
            jax.ShapeDtypeStruct((kv_local, GROUP, length), F32),
        ],
        compiler_params=params(2),
        cost_estimate=pl.CostEstimate(
            flops=kv_local * GROUP * length * length * HEAD_DIM * 8, bytes_accessed=1 << 24, transcendentals=0
        ),
        name="attend",
    )(me, q, k, v, query_row, key_col)


def attend_back_kernel(
    rows, count, me_ref, q_ref, k_ref, v_ref, out_ref, grad_ref, total_ref, query_row_ref, key_col_ref,
    cos_ref, sin_ref, cos_t_ref, sin_t_ref, dq_ref, dk_ref, dv_ref, k_t, inner, dq_t, dk_acc, dv_acc,
):
    me = me_ref[0]
    half = HEAD_DIM // 2
    k_t[...] = k_ref[0].astype(F32).T.astype(BF)
    dq_t[...] = jnp.zeros(dq_t.shape, F32)

    def prepare(i, _):
        here = pl.ds(pl.multiple_of(i * rows, rows), rows)
        for head in range(GROUP):
            cols = slice(head * HEAD_DIM, (head + 1) * HEAD_DIM)
            both = out_ref[here, cols].astype(F32) * grad_ref[here, cols].astype(F32)
            inner[head : head + 1, here] = jnp.sum(both.T, axis=0, keepdims=True)
        return 0

    lax.fori_loop(0, count, prepare, 0)

    def key_step(j, _):
        key_at = pl.ds(pl.multiple_of((j ^ me) * rows, rows), rows)
        keys, values = k_ref[0, key_at, :], v_ref[0, key_at, :]
        keys_t = k_t[:, key_at]
        key_col = key_col_ref[key_at, :]
        dk_acc[...] = jnp.zeros(dk_acc.shape, F32)
        dv_acc[...] = jnp.zeros(dv_acc.shape, F32)

        def query_step(i, _):
            at = pl.ds(pl.multiple_of((i ^ me) * rows, rows), rows)
            bias = pair_bias(rows, i, j, query_row_ref[:, at], key_col)
            for head in range(GROUP):
                cols = slice(head * HEAD_DIM, (head + 1) * HEAD_DIM)
                query, grad = q_ref[at, cols], grad_ref[at, cols]
                probs = jnp.exp(dot(keys, query, NT) + bias - total_ref[0, head : head + 1, at])
                dv_acc[...] += dot(probs.astype(BF), grad)
                grad_probs = dot(values, grad, NT)
                grad_scores = (probs * (grad_probs - inner[head : head + 1, at])).astype(BF)
                dk_acc[...] += dot(grad_scores, query)
                dq_t[head, :, at] += dot(keys_t, grad_scores)
            return 0

        lax.fori_loop(j, count, query_step, 0)
        dk = dk_acc[...]
        low, high = dk[:, :half], dk[:, half:]
        cosine, sine = cos_ref[key_at, :half], sin_ref[key_at, half:HEAD_DIM]
        dk_ref[0, key_at, :] = jnp.concatenate(
            [low * cosine + high * sine, high * cosine - low * sine], axis=1
        ).astype(BF)
        dv_ref[0, key_at, :] = dv_acc[...].astype(BF)
        return 0

    lax.fori_loop(0, count, key_step, 0)

    def finish(i, _):
        here = pl.ds(pl.multiple_of(i * rows, rows), rows)
        cosine, sine = cos_t_ref[:, here], sin_t_ref[:, here]
        for head in range(GROUP):
            low, high = dq_t[head, :half, here], dq_t[head, half:, here]
            turned = jnp.concatenate([low * cosine + high * sine, high * cosine - low * sine], axis=0) * SCALE
            dq_ref[here, head * HEAD_DIM : (head + 1) * HEAD_DIM] = turned.T.astype(BF)
        return 0

    lax.fori_loop(0, count, finish, 0)


def attend_back(me, q, k, v, out, grad, totals, query_row, key_col, cosine, sine, cosine_t, sine_t, rows):
    kv_local, length = k.shape[0], k.shape[1]
    width = GROUP * HEAD_DIM
    by_group = pl.BlockSpec((length, width), lambda g, me: (0, g))
    by_head = pl.BlockSpec((1, length, HEAD_DIM), lambda g, me: (g, 0, 0))
    whole = lambda shape: pl.BlockSpec(shape, lambda g, me: (0, 0))
    return pl.pallas_call(
        functools.partial(attend_back_kernel, rows, length // rows),
        grid_spec=pltpu.PrefetchScalarGridSpec(
            num_scalar_prefetch=1,
            grid=(kv_local,),
            in_specs=[
                by_group,
                by_head,
                by_head,
                by_group,
                by_group,
                pl.BlockSpec((1, GROUP, length), lambda g, me: (g, 0, 0)),
                whole((1, length)),
                whole((length, 1)),
                whole((length, LANES)),
                whole((length, LANES)),
                whole((HEAD_DIM // 2, length)),
                whole((HEAD_DIM // 2, length)),
            ],
            out_specs=[by_group, by_head, by_head],
            scratch_shapes=[
                pltpu.VMEM((HEAD_DIM, length), BF),
                pltpu.VMEM((GROUP, length), F32),
                pltpu.VMEM((GROUP, HEAD_DIM, length), F32),
                pltpu.VMEM((rows, HEAD_DIM), F32),
                pltpu.VMEM((rows, HEAD_DIM), F32),
            ],
        ),
        out_shape=[
            jax.ShapeDtypeStruct((length, kv_local * width), BF),
            jax.ShapeDtypeStruct((kv_local, length, HEAD_DIM), BF),
            jax.ShapeDtypeStruct((kv_local, length, HEAD_DIM), BF),
        ],
        compiler_params=params(1),
        cost_estimate=pl.CostEstimate(
            flops=kv_local * GROUP * length * length * HEAD_DIM * 20, bytes_accessed=1 << 24, transcendentals=0
        ),
        name="attend_back",
    )(me, q, k, v, out, grad, totals, query_row, key_col, cosine, sine, cosine_t, sine_t)


def norm_scale(values):
    return lax.rsqrt(jnp.mean(values * values, axis=-1, keepdims=True) + EPSILON)


def norm_back(grad_normed, values, inv_rms, gain_row):
    unit_rows = values * inv_rms
    scaled = grad_normed * gain_row
    return inv_rms * (scaled - unit_rows * jnp.mean(scaled * unit_rows, axis=-1, keepdims=True))


def blocks_of(values, count):
    rows = values.shape[0] // count
    return [values[k * rows : (k + 1) * rows] for k in range(count)]


def whole_columns(blocks, me):
    stacked = jnp.stack(blocks)
    ordered = [
        lax.dynamic_index_in_dim(stacked, p ^ me, 0, keepdims=False) for p in range(len(blocks))
    ]
    return jnp.concatenate(ordered, axis=1).astype(F32)


def general_body(
    inputs, cotangent, segments, valid_mask, query_weight, key_weight, value_weight, out_weight,
    gate_weight, up_weight, down_weight, attn_gain, mlp_gain,
):
    count = lax.axis_size("seq")
    me = lax.axis_index("seq")
    me_row = me.reshape(1).astype(jnp.int32)
    rows = inputs.shape[1]
    length = rows * count
    kv_local = KV_HEADS // count
    q_width = kv_local * GROUP * HEAD_DIM
    kv_width = kv_local * HEAD_DIM
    ff_local = FF // count
    shard_rows = gate_weight.shape[0]

    def mine(weight, width, axis=1):
        return lax.dynamic_slice_in_dim(weight, me * width, width, axis)

    gains = jnp.pad(jnp.stack([attn_gain, mlp_gain], axis=1), ((0, 0), (0, LANES - 2)))
    qkv_shard = jnp.concatenate(
        [mine(query_weight, q_width), mine(key_weight, kv_width), mine(value_weight, kv_width), gains], axis=1
    )
    qkv_full = gather_fsdp(qkv_shard)
    out_slice = gather_fsdp(mine(out_weight, q_width, 0).T)
    down_t = gather_fsdp(mine(down_weight, ff_local, 0).T)
    gate_up = gather_fsdp(jnp.concatenate([mine(gate_weight, ff_local), mine(up_weight, ff_local)], axis=1))
    gain_one = qkv_full[:, q_width + 2 * kv_width].astype(F32).reshape(1, D)
    gain_two = qkv_full[:, q_width + 2 * kv_width + 1].astype(F32).reshape(1, D)
    qkv_weight = qkv_full[:, : q_width + 2 * kv_width]

    marks = jnp.stack([segments[0], valid_mask[0]])
    marks_all = jnp.stack(gather_stream(marks, bit_orders()[0]))
    segment_all = marks_all[:, 0].reshape(length)
    valid_all = marks_all[:, 1].reshape(length)
    x_all = jnp.concatenate(gather_seq(inputs[0]), axis=0)
    valid_col = valid_mask[0].astype(F32)[:, None]
    grad_final = cotangent[0].astype(F32) * valid_col
    grad_mlp = jnp.concatenate(gather_seq(grad_final.astype(BF)), axis=0)

    position = (
        (jnp.arange(count, dtype=jnp.int32) ^ me)[:, None] * rows + jnp.arange(rows, dtype=jnp.int32)[None, :]
    ).reshape(length)
    same = (segment_all[:, None] == segment_all[None, :]) & (position[None, :] < position[:, None])
    places = jnp.sum(same.astype(jnp.int32), axis=1).astype(F32)
    half = HEAD_DIM // 2
    frequency = ROPE_BASE ** (-2.0 * jnp.arange(half, dtype=F32) / HEAD_DIM)
    angles_t = frequency[:, None] * places[None, :]
    cosine_t, sine_t = jnp.cos(angles_t), jnp.sin(angles_t)
    cosine = jnp.tile(cosine_t.T, (1, LANES // half))
    sign = jnp.tile(jnp.repeat(jnp.array([-1.0, 1.0], F32), half), LANES // HEAD_DIM)
    sine = jnp.tile(sine_t.T, (1, LANES // half)) * sign[None, :]
    query_row = jnp.where(valid_all == 1, segment_all, -1).reshape(1, length)
    key_col = segment_all.reshape(length, 1)

    normed_one, q, k, v = project(x_all, gain_one, qkv_full, cosine, sine, kv_local)
    heads_own, totals = attend(me_row, q, k, v, query_row, key_col, rows)

    heads_blocks = gather_seq(heads_own)
    heads_all = jnp.concatenate(
        [
            jnp.concatenate([blocks_of(heads_blocks[k], count)[i ^ k] for i in range(count)], axis=0)
            for k in range(count)
        ],
        axis=1,
    )
    out_blocks = gather_seq(out_slice)
    out_t = jnp.concatenate(out_blocks, axis=1)
    attn_all = dot(heads_all, out_t, NT)
    middle_all = x_all.astype(F32) + attn_all
    normed_two = (middle_all * norm_scale(middle_all) * gain_two).astype(BF)
    tokens = inputs[0].astype(F32)
    attn_branch = attn_all[:rows]
    middle = tokens + attn_branch
    inv_two = norm_scale(middle)

    gate_full, up_full = gate_up[:, :ff_local], gate_up[:, ff_local:]
    gate_lin = dot(normed_two, gate_full)
    up_lin = dot(normed_two, up_full)
    sigmoid_gate = jax.nn.sigmoid(gate_lin)
    silu_gate = gate_lin * sigmoid_gate
    activated = (silu_gate * up_lin).astype(BF)
    grad_act = dot(grad_mlp, down_t)
    grad_gate = (grad_act * up_lin * sigmoid_gate * (1.0 + gate_lin * (1.0 - sigmoid_gate))).astype(BF)
    grad_up = (grad_act * silu_gate).astype(BF)
    mlp_part = dot(activated, down_t, NT).astype(BF)
    grad_both = jnp.concatenate([grad_gate, grad_up], axis=1)
    grad_two_part = dot(grad_both, gate_up, NT).astype(BF)
    grad_normed_two = reduce_seq(blocks_of(grad_two_part, count))
    mlp_branch = reduce_seq(blocks_of(mlp_part, count))
    final = middle + mlp_branch
    outputs = final.astype(BF)[None]

    gate_up_grad = scatter_fsdp(dot(normed_two, grad_both, TN).astype(BF))
    down_grad_t = scatter_fsdp(dot(grad_mlp, activated, TN).astype(BF))

    grad_middle = grad_final + norm_back(grad_normed_two, middle, inv_two, gain_two)
    grad_attn = grad_middle.astype(BF)
    grad_heads = jnp.concatenate(
        exchange_seq([dot(grad_attn, b).astype(BF) for b in out_blocks]), axis=0
    )
    grad_attn_all = jnp.concatenate(gather_seq(grad_attn), axis=0)
    out_grad_t = scatter_fsdp(dot(grad_attn_all, heads_own, TN).astype(BF))

    dq, dk, dv = attend_back(
        me_row, q, k, v, heads_own, grad_heads, totals, query_row, key_col, cosine, sine, cosine_t, sine_t, rows
    )
    dqkv = jnp.concatenate([dq] + [dk[g] for g in range(kv_local)] + [dv[g] for g in range(kv_local)], axis=1)
    qkv_grad = scatter_fsdp(dot(normed_one, dqkv, TN).astype(BF))
    weight_blocks = gather_seq(qkv_weight)
    parts = exchange_seq(blocks_of(dqkv, count))
    grad_normed_one = dot(jnp.concatenate(parts, axis=1), jnp.concatenate(weight_blocks, axis=1), NT)
    inv_one = norm_scale(tokens)
    input_grad = (grad_middle + norm_back(grad_normed_one, tokens, inv_one, gain_one)).astype(BF)[None]

    gate_up_blocks = gather_seq(gate_up_grad)
    gate_grad = whole_columns([b[:, :ff_local] for b in gate_up_blocks], me)
    up_grad = whole_columns([b[:, ff_local:] for b in gate_up_blocks], me)
    down_grad = whole_columns(gather_seq(down_grad_t), me).T
    out_grad = whole_columns(gather_seq(out_grad_t), me).T
    qkv_blocks = gather_seq(qkv_grad)
    query_grad = whole_columns([b[:, :q_width] for b in qkv_blocks], me)
    key_grad = whole_columns([b[:, q_width : q_width + kv_width] for b in qkv_blocks], me)
    value_grad = whole_columns([b[:, q_width + kv_width :] for b in qkv_blocks], me)

    def rows_dot(weight, grad):
        return jnp.sum(weight.astype(F32) * grad, axis=1)

    attn_gain_grad = (
        rows_dot(query_weight, query_grad) + rows_dot(key_weight, key_grad) + rows_dot(value_weight, value_grad)
    ) / attn_gain.astype(F32)
    mlp_gain_grad = (rows_dot(gate_weight, gate_grad) + rows_dot(up_weight, up_grad)) / mlp_gain.astype(F32)

    squares = [jnp.sum(valid_col * part * part) for part in (tokens, middle, final, attn_branch, mlp_branch)]
    stats = jnp.stack([jnp.sum(valid_col)] + squares)
    stats = jnp.broadcast_to(jnp.pad(stats, (0, LANES - 6))[None, :], (8, LANES))
    for bit in bit_orders()[0]:
        stats = stats + swap(stats, bit)
    rms_stats = jnp.sqrt(stats[:1, 1:6] / (stats[:1, :1] * D))
    return (
        outputs, input_grad, query_grad, key_grad, value_grad, out_grad, gate_grad, up_grad, down_grad,
        attn_gain_grad, mlp_gain_grad, rms_stats,
    )


TILE = 256

def after(value, *events):
    return lax.optimization_barrier((value,) + events)[0]


def to_both(block):
    return swap(block, 1), swap(block, 2)


def pass_on(by_x, by_y, *events):
    half = by_x.shape[0] // 2
    return swap(after(by_y[:half], *events), 1), swap(after(by_x[half:], *events), 2)


def swap_core(values):
    count = lax.axis_size("fsdp")
    return lax.ppermute(values, "fsdp", [(i, i ^ 1) for i in range(count)])


def core_half(weight, core):
    half = weight.shape[0] // 2
    return lax.dynamic_slice_in_dim(weight, core * half, half, 0)


def in_order(core, mine, other):
    return jnp.where(core == 0, jnp.concatenate([mine, other], axis=1), jnp.concatenate([other, mine], axis=1))


def add_low(a, b):
    return (a.astype(F32) + b.astype(F32)).astype(BF)


def send_far(low, high):
    return swap(low, 1), swap(high, 2)


def add_far(near, low, high):
    x_low, x_high, y_low, y_high = near
    return [x_low, add_low(x_high, high), add_low(y_low, low), y_high]


def send_near(near):
    return [swap(part, bit) for part, bit in zip(near, (1, 1, 2, 2))]


def call(kernel, grid, in_specs, out_specs, out_shape, args, name, flops=0, moved=0, scratch=(), prefetch=0, aliases=None):
    return pl.pallas_call(
        kernel,
        grid_spec=pltpu.PrefetchScalarGridSpec(
            num_scalar_prefetch=prefetch,
            grid=grid,
            in_specs=in_specs,
            out_specs=out_specs,
            scratch_shapes=list(scratch),
        ),
        out_shape=out_shape,
        input_output_aliases=aliases or {},
        compiler_params=pltpu.CompilerParams(
            dimension_semantics=("arbitrary",) * len(grid), vmem_limit_bytes=VMEM_LIMIT
        ),
        cost_estimate=pl.CostEstimate(flops=int(flops), bytes_accessed=int(moved), transcendentals=0),
        name=name,
    )(*args)


def shape_of(shape, dtype=BF):
    return jax.ShapeDtypeStruct(shape, dtype)


def fixed(shape, buffers=None):
    mode = {} if buffers is None else {"pipeline_mode": pl.Buffered(buffers)}
    return pl.BlockSpec(shape, lambda *_: (0,) * len(shape), **mode)


def piece_specs(pieces, tile):
    specs, spans, start = [], [], 0
    for piece in pieces:
        tiles = piece.shape[0] // tile
        specs.append(
            pl.BlockSpec(
                (tile, piece.shape[1]),
                lambda i, *_, start=start, tiles=tiles: (jnp.clip(i - start, 0, tiles - 1), 0),
            )
        )
        spans.append((start, start + tiles))
        start += tiles
    return specs, spans


def copy_piece(refs, spans, index, target):
    for ref, (first, last) in zip(refs, spans):

        @pl.when((index >= first) & (index < last))
        def _(ref=ref):
            target[...] = ref[...]


def act_back_kernel(spans, others, *refs):
    weight_ref = refs[len(spans)]
    whole_ref, out_ref = refs[len(spans) + 1 + others :]
    copy_piece(refs[: len(spans)], spans, pl.program_id(0), whole_ref)
    out_ref[...] = dot(whole_ref[...], weight_ref[...]).astype(BF)


def act_back(pieces, weight, first, rows, before=()):
    specs, spans = piece_specs(pieces, TILE)
    tiles, skip, width = spans[-1][1], first // TILE, weight.shape[1]
    by_row = lambda w: pl.BlockSpec((TILE, w), lambda i: (skip + i, 0))
    count = len(pieces) + 1
    return call(
        functools.partial(act_back_kernel, spans, len(before)), (tiles,),
        specs + [fixed(weight.shape)] + [pl.BlockSpec(memory_space=pl.ANY)] * len(before),
        [by_row(D), by_row(width)], [shape_of((rows, D)), shape_of((rows, width))],
        (*pieces, weight, *before), "act_back", flops=2 * tiles * TILE * D * width, moved=tiles * TILE * D * 6,
        aliases={count + k: k for k in range(len(before))},
    )


def pack_qkv_kernel(kv_local, me_ref, q_ref, k_ref, v_ref, gains_ref, out_ref):
    width = GROUP * HEAD_DIM
    parts = []
    for g in range(kv_local):
        head = slice(g * HEAD_DIM, (g + 1) * HEAD_DIM)
        parts += [q_ref[:, g * width : (g + 1) * width], jnp.concatenate([k_ref[:, head], v_ref[:, head]], axis=1)]
    out_ref[...] = jnp.concatenate(parts + [gains_ref[...]], axis=1)


def pack_qkv(me_row, query_weight, key_weight, value_weight, gains, kv_local):
    rows = query_weight.shape[0]
    q_width, kv_width = kv_local * GROUP * HEAD_DIM, kv_local * HEAD_DIM
    total = q_width + 2 * kv_width + LANES
    mine = lambda width: pl.BlockSpec((rows, width), lambda i, me: (0, me[0]))
    return call(
        functools.partial(pack_qkv_kernel, kv_local), (1,),
        [mine(q_width), mine(kv_width), mine(kv_width), fixed((rows, LANES))],
        fixed((rows, total)), shape_of((rows, total)),
        (me_row, query_weight, key_weight, value_weight, gains), "pack_qkv", moved=4 * rows * total, prefetch=1,
    )


def pack_rows_kernel(me_ref, in_ref, out_ref):
    out_ref[...] = in_ref[...].astype(F32).T.astype(BF)


def pack_rows(me_row, weight, rows, owners=(0,)):
    tile = 512
    tiles, columns = rows // tile, weight.shape[1]

    def index(i, me):
        owner = sum(jnp.where(i // tiles == k, owner, 0) for k, owner in enumerate(owners))
        return ((me[0] ^ owner) * tiles + i % tiles, 0)

    return call(
        pack_rows_kernel, (tiles * len(owners),), [pl.BlockSpec((tile, columns), index)],
        pl.BlockSpec((columns, tile), lambda i, me: (0, i)), shape_of((columns, rows * len(owners))), (me_row, weight),
        "pack_rows", moved=4 * rows * columns, prefetch=1,
    )


def pack_pair_kernel(me_ref, a_ref, b_ref, out_ref):
    width = a_ref.shape[1]
    out_ref[:, :width] = a_ref[...]
    out_ref[:, width:] = b_ref[...]


def pack_pair(me_row, a, b, chunks, chunk, width):
    rows = a.shape[0]
    spec = pl.BlockSpec((rows, width), lambda i, me: (0, me[0] * chunks + chunk))
    return call(
        pack_pair_kernel, (1,), [spec, spec], fixed((rows, 2 * width)), shape_of((rows, 2 * width)), (me_row, a, b),
        "pack_pair", moved=8 * rows * width, prefetch=1,
    )


def enter_kernel(kv_local, spans, others, *refs):
    pieces = refs[: len(spans)]
    gain_ref, w_ref, cos_ref, sin_ref = refs[len(spans) : len(spans) + 4]
    x_ref, normed_ref, q_ref, k_ref, v_ref = refs[len(spans) + 4 + others :]
    copy_piece(pieces, spans, pl.program_id(0), x_ref)
    x = x_ref[...].astype(F32)
    inv = lax.rsqrt(jnp.mean(x * x, axis=-1, keepdims=True) + EPSILON)
    normed = (x * inv * gain_ref[...]).astype(BF)
    normed_ref[...] = normed
    width = GROUP * HEAD_DIM
    step = width + 2 * HEAD_DIM
    lin = dot(normed, w_ref[:, : kv_local * step])
    cosine, sine = cos_ref[...], sin_ref[...]
    for g in range(kv_local):
        for start in range(0, width, LANES):
            part = turn(lin[:, g * step + start : g * step + start + LANES], cosine, sine) * SCALE
            q_ref[:, g * width + start : g * width + start + LANES] = part.astype(BF)
        pair = lin[:, g * step + width : (g + 1) * step]
        k_ref[g] = turn(pair, cosine, sine)[:, :HEAD_DIM].astype(BF)
        v_ref[g] = pair[:, HEAD_DIM:].astype(BF)


def enter(pieces, gain_row, weight, cosine, sine, kv_local, first, rows, before=()):
    specs, spans = piece_specs(pieces, TILE)
    tiles, skip = spans[-1][1], first // TILE
    q_width = kv_local * GROUP * HEAD_DIM
    by_row = lambda width: pl.BlockSpec((TILE, width), lambda i: (skip + i, 0))
    by_head = pl.BlockSpec((kv_local, TILE, HEAD_DIM), lambda i: (0, skip + i, 0))
    heads = shape_of((kv_local, rows, HEAD_DIM))
    count = len(pieces) + 4
    return call(
        functools.partial(enter_kernel, kv_local, spans, len(before)), (tiles,),
        specs
        + [fixed((1, D)), fixed(weight.shape), by_row(LANES), by_row(LANES)]
        + [pl.BlockSpec(memory_space=pl.ANY)] * len(before),
        [by_row(D), by_row(D), by_row(q_width), by_head, by_head],
        [shape_of((rows, D)), shape_of((rows, D)), shape_of((rows, q_width)), heads, heads],
        (*pieces, gain_row, weight, cosine, sine, *before), "enter",
        flops=2 * tiles * TILE * D * weight.shape[1], moved=tiles * TILE * D * 8,
        aliases={count + k: k for k in range(len(before))},
    )


def allowed_bias(rows, size, first, query_row, key_col, diagonal):
    allowed = key_col == query_row
    if diagonal:
        key_pos = lax.broadcasted_iota(jnp.int32, (size, rows - first), 0)
        query_pos = lax.broadcasted_iota(jnp.int32, (size, rows - first), 1)
        allowed = (allowed & (key_pos <= query_pos)) | (key_pos == query_pos)
    return jnp.where(allowed, 0.0, NEGATIVE)


def attend_one_kernel(rows, me_ref, q_ref, k_ref, v_ref, query_row_ref, key_col_ref, out_ref, total_ref, v_t, peak, total, acc):
    index = pl.program_id(1)
    me = me_ref[0]
    half = rows // 2

    @pl.when(index == 0)
    def _():
        v_t[...] = v_ref[0].astype(F32).T.astype(BF)

    peak[...] = jnp.full(peak.shape, NEGATIVE, F32)
    total[...] = jnp.zeros(total.shape, F32)
    acc[...] = jnp.zeros(acc.shape, F32)

    def visit(at, size, first, diagonal):
        keys = k_ref[0, pl.ds(at, size), :]
        values_t = v_t[:, pl.ds(at, size)]
        bias = allowed_bias(rows, size, first, query_row_ref[:, first:], key_col_ref[pl.ds(at, size), :], diagonal)
        for head in range(GROUP):
            query = q_ref[first:, head * HEAD_DIM : (head + 1) * HEAD_DIM]
            scores = dot(keys, query, NT) + bias
            old = peak[head : head + 1, first:]
            new = jnp.maximum(old, jnp.max(scores, axis=0, keepdims=True))
            expo = jnp.exp(scores - new)
            fade = jnp.exp(old - new)
            peak[head : head + 1, first:] = new
            total[head : head + 1, first:] = total[head : head + 1, first:] * fade + jnp.sum(expo, axis=0, keepdims=True)
            acc[head, :, first:] = acc[head, :, first:] * fade + dot(values_t, expo.astype(BF))

    here = pl.multiple_of((index ^ me) * rows, rows)
    visit(here, half, 0, True)
    visit(pl.multiple_of(here + half, half), half, half, True)

    def step(j, _):
        visit(pl.multiple_of((j ^ me) * rows, rows), rows, 0, False)
        return 0

    lax.fori_loop(0, index, step, 0)
    for head in range(GROUP):
        out = acc[head] / total[head : head + 1, :]
        out_ref[:, head * HEAD_DIM : (head + 1) * HEAD_DIM] = out.T.astype(BF)
    total_ref[0] = peak[...] + jnp.log(total[...])


def attend_one(me_row, q, k, v, query_row, key_col, rows, group):
    length = k.shape[1]
    width = GROUP * HEAD_DIM
    head = pl.BlockSpec((1, length, HEAD_DIM), lambda g, i, me: (group, 0, 0))
    return call(
        functools.partial(attend_one_kernel, rows), (1, length // rows),
        [
            pl.BlockSpec((rows, width), lambda g, i, me: (i ^ me[0], group)),
            head,
            head,
            pl.BlockSpec((1, rows), lambda g, i, me: (0, i ^ me[0])),
            fixed((length, 1)),
        ],
        [
            pl.BlockSpec((rows, width), lambda g, i, me: (i ^ me[0], 0)),
            pl.BlockSpec((1, GROUP, rows), lambda g, i, me: (0, 0, i ^ me[0])),
        ],
        [shape_of((length, width)), shape_of((1, GROUP, length), F32)],
        (me_row, q, k, v, query_row, key_col), "attend", flops=2.6e10, moved=1 << 22, prefetch=1,
        scratch=[
            pltpu.VMEM((HEAD_DIM, length), BF),
            pltpu.VMEM((GROUP, rows), F32),
            pltpu.VMEM((GROUP, rows), F32),
            pltpu.VMEM((GROUP, HEAD_DIM, rows), F32),
        ],
    )


def leave_kernel(groups, per, tiles, core_ref, x_ref, gain_ref, *refs):
    heads, weights, (normed_ref, attn_ref) = refs[: 5 * groups], refs[5 * groups : 5 * groups + 7], refs[5 * groups + 7 :]
    index = pl.program_id(0)
    stored = ((index // per) ^ 3) * per + index % per
    is_low = stored < tiles // 2
    attn, mine, other = None, 0.0, 0.0
    for k in range(4):
        parts = [
            heads[5 * g + k][...] if k < 3 else jnp.where(is_low, heads[5 * g + 3][...], heads[5 * g + 4][...])
            for g in range(groups)
        ]
        part = jnp.concatenate(parts, axis=1)
        if k == 0:
            attn = dot(part, weights[0][...], NT)
        else:
            mine = mine + dot(part, weights[k][...], NT)
            other = other + dot(part, weights[3 + k][...], NT)
    attn = attn + in_order(core_ref[0], mine, other)
    middle = x_ref[...].astype(F32) + attn
    inv = lax.rsqrt(jnp.mean(middle * middle, axis=-1, keepdims=True) + EPSILON)
    normed_ref[...] = (middle * inv * gain_ref[...]).astype(BF)

    @pl.when(index < per)
    def _():
        attn_ref[...] = attn


def weight_specs(weights):
    plain = [fixed(w.shape, 1) for w in weights if len(w.shape) == 2]
    stacked = [w.shape[1:] for w in weights if len(w.shape) == 3]
    return plain + [
        pl.BlockSpec((None,) + shape, lambda *_, k=k: (k, 0, 0), pipeline_mode=pl.Buffered(1))
        for shape in stacked
        for k in range(3)
    ]


def weight_args(weights):
    return [w for w in weights for _ in range(3 if len(w.shape) == 3 else 1)]


def leave(core_row, x_all, gain_row, heads, weights, rows):
    length = x_all.shape[0]
    per, tiles = rows // TILE, length // TILE
    by_row = pl.BlockSpec((TILE, D), lambda i, core: (i, 0))

    def head_spec(k, low, high, width):
        return pl.BlockSpec(
            (TILE, width), lambda i, core: (jnp.clip(((i // per) ^ k) * per + i % per - low, 0, high - low - 1), 0)
        )

    specs = []
    for pieces in heads:
        width = pieces[0].shape[1]
        for k in range(3):
            specs.append(head_spec(k, 0, tiles, width))
        specs += [head_spec(3, 0, tiles // 2, width), head_spec(3, tiles // 2, tiles, width)]
    return call(
        functools.partial(leave_kernel, len(heads), per, tiles), (tiles,),
        [by_row, fixed((1, D))] + specs + weight_specs(weights),
        [by_row, pl.BlockSpec((TILE, D), lambda i, core: (jnp.minimum(i, per - 1), 0))],
        [shape_of((length, D)), shape_of((rows, D), F32)],
        (core_row, x_all, gain_row, *[p for pieces in heads for p in pieces], *weight_args(weights)), "leave",
        flops=2 * length * D * D, moved=length * D * 8, prefetch=1,
    )


def up_kernel(normed_ref, gate_ref, up_ref, grad_ref, act_ref, grad_gate_ref, grad_up_ref):
    normed = normed_ref[...]
    for start in range(0, act_ref.shape[1], 256):
        part = slice(start, start + 256)
        gate = dot(normed, gate_ref[:, part])
        up = dot(normed, up_ref[:, part])
        grad = grad_ref[:, part].astype(F32)
        sigmoid = jax.nn.sigmoid(gate)
        silu = gate * sigmoid
        act_ref[:, part] = (silu * up).astype(BF)
        grad_gate_ref[:, part] = (grad * up * (sigmoid + silu * (1.0 - sigmoid))).astype(BF)
        grad_up_ref[:, part] = (grad * silu).astype(BF)


def up_project(normed, gate_up, grad_act, chunk):
    length, width = normed.shape[0], gate_up.shape[1] // 2
    tall, wide = 1024, 512
    across = width // wide
    out = pl.BlockSpec((tall, wide), lambda i, j: (i, j))
    return call(
        up_kernel, (length // tall, across),
        [
            pl.BlockSpec((tall, D), lambda i, j: (i, 0)),
            pl.BlockSpec((D, wide), lambda i, j: (0, j)),
            pl.BlockSpec((D, wide), lambda i, j: (0, across + j)),
            pl.BlockSpec((tall, wide), lambda i, j: (i, chunk * across + j)),
        ],
        [out] * 3, [shape_of((length, width))] * 3, (normed, gate_up, gate_up, grad_act), "up_project",
        flops=4 * length * D * width, moved=length * (D + 4 * width) * 2 + 8 * D * width,
    )


def sum_kernel(places, count, *refs):
    total = None
    for i in range(0, 2 * count, 2):
        part = dot(refs[i][...], refs[i + 1][...], NT)
        total = part if total is None else total + part
    total = total.astype(BF)
    for (tile, start, size), ref in zip(places, refs[2 * count :]):

        @pl.when(pl.program_id(0) == tile)
        def _(start=start, size=size, ref=ref):
            ref[...] = total[start : start + size]


def sum_of(terms, first, rows, halves):
    tall, wide = 512, 512
    specs, args = [], []
    for left, right, column in terms:
        width = left.shape[1]
        specs.append(pl.BlockSpec((tall, width), lambda i, j: (first // tall + i, 0)))
        specs.append(pl.BlockSpec((wide, width), lambda i, j, column=column: (j, column)))
        args += [left, right]
    size = tall // 2 if halves else tall
    places = [(i, start, size) for i in range(rows // tall) for start in range(0, tall, size)]
    last = D // wide - 1
    depth = sum(left.shape[1] for left, _, _ in terms)

    def out_spec(tile):
        return pl.BlockSpec((size, wide), lambda i, j: (0, jnp.where(i == tile, j, jnp.where(i < tile, 0, last))))

    return call(
        functools.partial(sum_kernel, places, len(terms)), (rows // tall, D // wide), specs,
        [out_spec(tile) for tile, _, _ in places], [shape_of((size, D))] * len(places), args, "sum_of",
        flops=2 * rows * D * depth, moved=2 * depth * (rows + D) + 2 * rows * D,
    )


def outer_kernel(across, count, left_ref, *refs):
    for k in range(count):

        @pl.when(pl.program_id(1) // across == k)
        def _(k=k):
            refs[-1][...] = dot(left_ref[...], refs[k][...], TN).astype(BF)


def outer(left, rights, wide, total=None):
    length, tall, width = left.shape[0], 1024, rights[0].shape[1]
    across, count = width // wide, len(rights)
    right_spec = lambda k: pl.BlockSpec((length, wide), lambda i, j: (0, jnp.clip(j - k * across, 0, across - 1)))
    return call(
        functools.partial(outer_kernel, across, count), (left.shape[1] // tall, across * count),
        [pl.BlockSpec((length, tall), lambda i, j: (0, i))] + [right_spec(k) for k in range(count)],
        pl.BlockSpec((tall, wide), lambda i, j: (i, j)), shape_of((left.shape[1], total or width * count)),
        (left, *rights), "outer", flops=2 * length * left.shape[1] * width * count,
        moved=2 * (length + left.shape[1]) * (left.shape[1] + width * count),
    )


def outer_local_kernel(groups, left_ref, *refs):
    for k in range(4):

        @pl.when(pl.program_id(1) == k)
        def _(k=k):
            right = jnp.concatenate([refs[4 * g + k][...] for g in range(groups)], axis=1)
            refs[-1][...] = dot(left_ref[...], right, TN).astype(BF)


def outer_local(left, heads):
    rows, width, tall = left.shape[0], heads[0][0].shape[1], 1024
    specs, args = [], []
    for pieces in heads:
        for k, piece, block in ((0, pieces[0], 0), (1, pieces[1], 1), (2, pieces[2], 2), (3, pieces[4], 1)):
            specs.append(pl.BlockSpec((rows, width), lambda i, k, block=block: (block, 0)))
            args.append(piece)
    across = width * len(heads)
    return call(
        functools.partial(outer_local_kernel, len(heads)), (D // tall, 4),
        [pl.BlockSpec((rows, tall), lambda i, k: (0, i))] + specs, pl.BlockSpec((tall, across), lambda i, k: (i, k)),
        shape_of((D, 4 * across)), (left, *args), "outer_local", flops=8 * rows * D * across,
        moved=2 * D * (rows + 4 * across),
    )


def outer_rows_kernel(count, *refs):
    for k in range(count):

        @pl.when(pl.program_id(0) == k)
        def _(k=k):
            refs[-1][...] = dot(refs[k][...], refs[count][...], TN).astype(BF)


def outer_rows(lefts, right, shard):
    length, width = lefts[0].shape
    count, shards = len(lefts), right.shape[1] // shard
    return call(
        functools.partial(outer_rows_kernel, count), (count, shards),
        [pl.BlockSpec((length, width), lambda f, s: (0, 0))] * count + [pl.BlockSpec((length, shard), lambda f, s: (0, s))],
        pl.BlockSpec((width, shard), lambda f, s: (s * count + f, 0)), shape_of((shards * count * width, shard)),
        (*lefts, right), "outer_rows", flops=2 * length * right.shape[1] * width * count,
        moved=2 * (length + right.shape[1]) * width * count,
    )


def two_halves(refs):
    return jnp.where(pl.program_id(0) == 0, refs[0][...], refs[1][...]).astype(F32)


def turn_back_kernel(core_ref, own_ref, x_low, x_high, y_low, y_high, x_ref, attn_ref, cot_ref, valid_ref, gain_ref, *refs):
    weights, (middle_ref, low_ref, heads_ref) = refs[:7], refs[7:]
    grad = own_ref[...].astype(F32) + two_halves((x_low, x_high)) + two_halves((y_low, y_high))
    middle = x_ref[...].astype(F32) + attn_ref[...]
    inv = lax.rsqrt(jnp.mean(middle * middle, axis=-1, keepdims=True) + EPSILON)
    grad_middle = cot_ref[...].astype(F32) * valid_ref[...] + norm_back(grad, middle, inv, gain_ref[...])
    middle_ref[...] = grad_middle
    low = grad_middle.astype(BF)
    low_ref[...] = low
    first, second = low[:, : D // 2], low[:, D // 2 :]
    mine = jnp.where(core_ref[0] == 0, first, second)
    other = jnp.where(core_ref[0] == 0, second, first)
    heads_ref[0] = dot(low, weights[0][...]).astype(BF)
    for k in range(1, 4):
        heads_ref[k] = (dot(mine, weights[k][...]) + dot(other, weights[3 + k][...])).astype(BF)


def turn_back(core_row, own, terms, x, attn, cot, valid_col, gain_row, weights):
    rows, width = x.shape[0], weights[0].shape[1]
    by_row = lambda w: pl.BlockSpec((TILE, w), lambda i, core: (i, 0))
    return call(
        turn_back_kernel, (rows // TILE,),
        [by_row(D)] + [fixed((TILE, D))] * 4 + [by_row(D)] * 3 + [by_row(1), fixed((1, D))] + weight_specs(weights),
        [by_row(D), by_row(D), pl.BlockSpec((4, TILE, width), lambda i, core: (0, i, 0))],
        [shape_of((rows, D), F32), shape_of((rows, D)), shape_of((4, rows, width))],
        (core_row, own, *terms, x, attn, cot, valid_col, gain_row, *weight_args(weights)), "turn_back",
        flops=8 * rows * D * width, moved=rows * D * 20, prefetch=1,
    )


def last_kernel(own_ref, by_x_ref, by_y_ref, x_ref, attn_ref, valid_ref, out_ref, stats_ref):
    mlp = own_ref[...].astype(F32) + by_x_ref[...].astype(F32) + by_y_ref[...].astype(F32)
    x, attn, valid = x_ref[...].astype(F32), attn_ref[...], valid_ref[...]
    middle = x + attn
    final = middle + mlp
    out_ref[...] = final.astype(BF)

    @pl.when(pl.program_id(0) == 0)
    def _():
        stats_ref[...] = jnp.zeros(stats_ref.shape, F32)

    for row, part in enumerate((x, middle, final, attn, mlp)):
        stats_ref[row : row + 1, :] += fold(jnp.sum(valid * part * part, axis=0, keepdims=True))


def last(own, by_x, by_y, x, attn, valid_col):
    rows = x.shape[0]
    by_row = lambda w: pl.BlockSpec((TILE, w), lambda i: (i, 0))
    return call(
        last_kernel, (rows // TILE,), [by_row(D)] * 5 + [by_row(1)], [by_row(D), fixed((8, LANES))],
        [shape_of((rows, D)), shape_of((8, LANES), F32)], (own, by_x, by_y, x, attn, valid_col), "last",
        moved=rows * D * 20,
    )


def attend_back_one_kernel(rows, count, me_ref, *refs):
    q_ref, k_ref, v_ref, out_ref, own, by_x, by_y, by_xy, total_ref, query_row_ref, key_col_ref = refs[:11]
    cos_ref, sin_ref, cos_t_ref, sin_t_ref, dqkv_ref, grad_ref, k_t, inner, dq_t, dk_acc, dv_acc = refs[11:]
    me = me_ref[0]
    half, width = HEAD_DIM // 2, GROUP * HEAD_DIM
    for block, ref in enumerate((own, by_x, by_y, by_xy)):
        grad_ref[block * rows : (block + 1) * rows, :] = ref[...] if len(ref.shape) == 2 else ref[0]
    k_t[...] = k_ref[0].astype(F32).T.astype(BF)
    dq_t[...] = jnp.zeros(dq_t.shape, F32)

    def prepare(i, _):
        here = pl.ds(pl.multiple_of(i * rows, rows), rows)
        for head in range(GROUP):
            cols = slice(head * HEAD_DIM, (head + 1) * HEAD_DIM)
            both = out_ref[here, cols].astype(F32) * grad_ref[here, cols].astype(F32)
            inner[head : head + 1, here] = jnp.sum(both.T, axis=0, keepdims=True)
        return 0

    lax.fori_loop(0, count, prepare, 0)

    def visit(key_at, size, local, query_at, first, diagonal):
        keys_here = pl.ds(key_at, size)
        here = pl.ds(pl.multiple_of(query_at + first, rows // 2), rows - first)
        keys, values, keys_t = k_ref[0, keys_here, :], v_ref[0, keys_here, :], k_t[:, keys_here]
        bias = allowed_bias(rows, size, first, query_row_ref[:, here], key_col_ref[keys_here, :], diagonal)
        for head in range(GROUP):
            cols = slice(head * HEAD_DIM, (head + 1) * HEAD_DIM)
            query, grad = q_ref[here, cols], grad_ref[here, cols]
            probs = jnp.exp(dot(keys, query, NT) + bias - total_ref[0, head : head + 1, here])
            dv_acc[local : local + size, :] += dot(probs.astype(BF), grad)
            grad_probs = dot(values, grad, NT)
            grad_scores = (probs * (grad_probs - inner[head : head + 1, here])).astype(BF)
            dk_acc[local : local + size, :] += dot(grad_scores, query)
            dq_t[head, :, here] += dot(keys_t, grad_scores)

    def key_step(j, _):
        key_start = pl.multiple_of((j ^ me) * rows, rows)
        key_at = pl.ds(key_start, rows)
        dk_acc[...] = jnp.zeros(dk_acc.shape, F32)
        dv_acc[...] = jnp.zeros(dv_acc.shape, F32)
        visit(key_start, rows // 2, 0, key_start, 0, True)
        visit(pl.multiple_of(key_start + rows // 2, rows // 2), rows // 2, rows // 2, key_start, rows // 2, True)

        def query_step(i, _):
            visit(key_start, rows, 0, pl.multiple_of((i ^ me) * rows, rows), 0, False)
            return 0

        lax.fori_loop(j + 1, count, query_step, 0)
        dk = dk_acc[...]
        low, high = dk[:, :half], dk[:, half:]
        cosine, sine = cos_ref[key_at, :half], sin_ref[key_at, half:HEAD_DIM]
        turned = jnp.concatenate([low * cosine + high * sine, high * cosine - low * sine], axis=1)
        dqkv_ref[key_at, width : width + HEAD_DIM] = turned.astype(BF)
        dqkv_ref[key_at, width + HEAD_DIM :] = dv_acc[...].astype(BF)
        return 0

    lax.fori_loop(0, count, key_step, 0)

    def finish_queries(i, _):
        here = pl.ds(pl.multiple_of(i * rows, rows), rows)
        cosine, sine = cos_t_ref[:, here], sin_t_ref[:, here]
        for head in range(GROUP):
            low, high = dq_t[head, :half, here], dq_t[head, half:, here]
            turned = jnp.concatenate([low * cosine + high * sine, high * cosine - low * sine], axis=0) * SCALE
            dqkv_ref[here, head * HEAD_DIM : (head + 1) * HEAD_DIM] = turned.T.astype(BF)
        return 0

    lax.fori_loop(0, count, finish_queries, 0)


def attend_back_one(me_row, q, k, v, out, grads, totals, query_row, key_col, tables, rows, group):
    length = k.shape[1]
    width = GROUP * HEAD_DIM
    whole = lambda shape: fixed(shape, 1)
    head = pl.BlockSpec((1, length, HEAD_DIM), lambda i, me: (group, 0, 0), pipeline_mode=pl.Buffered(1))
    part = pl.BlockSpec((rows, width), lambda i, me: (0, group))
    own = pl.BlockSpec((1, rows, width), lambda i, me: (0, 0, group))
    out_width = width + 2 * HEAD_DIM
    return call(
        functools.partial(attend_back_one_kernel, rows, length // rows), (1,),
        [
            pl.BlockSpec((length, width), lambda i, me: (0, group)), head, head, whole((length, width)),
            own, part, part, part, whole((1, GROUP, length)), whole((1, length)), whole((length, 1)),
            whole((length, LANES)), whole((length, LANES)),
            whole((HEAD_DIM // 2, length)), whole((HEAD_DIM // 2, length)),
        ],
        whole((length, out_width)), shape_of((length, out_width)),
        (me_row, q, k, v, out, *grads, totals, query_row, key_col, *tables), "attend_back",
        flops=3.4e10, moved=1 << 22, prefetch=1,
        scratch=[
            pltpu.VMEM((length, width), BF),
            pltpu.VMEM((HEAD_DIM, length), BF),
            pltpu.VMEM((GROUP, length), F32),
            pltpu.VMEM((GROUP, HEAD_DIM, length), F32),
            pltpu.VMEM((rows, HEAD_DIM), F32),
            pltpu.VMEM((rows, HEAD_DIM), F32),
        ],
    )


def finish_kernel(groups, step, core_ref, x_ref, middle_ref, gain_ref, *refs):
    grads, weights, out_ref = refs[: 4 * groups], refs[4 * groups : 4 * groups + 7], refs[-1]
    grad, mine, other = None, 0.0, 0.0
    for k in range(4):
        low = jnp.concatenate([grads[4 * g + k][...] for g in range(groups)], axis=1)
        if k == 0:
            grad = dot(low, weights[0][:, : groups * step], NT)
        else:
            mine = mine + dot(low, weights[k][...], NT)
            other = other + dot(low, weights[3 + k][...], NT)
    grad = grad + in_order(core_ref[0], mine, other)
    x = x_ref[...].astype(F32)
    inv = lax.rsqrt(jnp.mean(x * x, axis=-1, keepdims=True) + EPSILON)
    out_ref[...] = (middle_ref[...] + norm_back(grad, x, inv, gain_ref[...])).astype(BF)


def finish(core_row, x, grad_middle, gain_row, grads, weights):
    rows, step = x.shape[0], grads[0][0].shape[1]
    by_row = lambda w: pl.BlockSpec((TILE, w), lambda i, core: (i, 0))
    return call(
        functools.partial(finish_kernel, len(grads), step), (rows // TILE,),
        [by_row(D), by_row(D), fixed((1, D))] + [by_row(step)] * (4 * len(grads)) + weight_specs(weights),
        by_row(D), shape_of((rows, D)),
        (core_row, x, grad_middle, gain_row, *[p for parts in grads for p in parts], *weight_args(weights)), "finish",
        flops=8 * rows * D * step * len(grads), moved=rows * D * 8 + 4 * D * step * 4, prefetch=1,
    )


def each_piece(refs, emit):
    block = pl.program_id(0)
    for k in range(3):

        @pl.when(block == k)
        def _(k=k):
            emit(refs[k][...])

    @pl.when(block == 3)
    def _():
        emit(jnp.concatenate([refs[3][...], refs[4][...]], axis=0))


def fold(values):
    return sum(values[:, at : at + LANES] for at in range(0, values.shape[1], LANES))


def place_pair_kernel(first, me_ref, *refs):
    pieces, weight_a, weight_b = refs[:5], refs[5], refs[6]
    out_a, out_b, dot_ref = refs[-3:]
    width = out_a.shape[1]

    @pl.when(pl.program_id(0) == 0)
    def _():
        dot_ref[...] = jnp.zeros(dot_ref.shape, F32) if first else refs[9][...]

    def emit(values):
        a, b = values[:, :width].astype(F32), values[:, width:].astype(F32)
        out_a[...], out_b[...] = a, b
        dot_ref[...] += fold(a * weight_a[...].astype(F32)) + fold(b * weight_b[...].astype(F32))

    each_piece(pieces, emit)


def place_pair(me_row, pieces, weight_a, weight_b, chunks, chunk, before):
    rows, total = weight_a.shape
    width = pieces[0].shape[1] // 2
    column = pl.BlockSpec((rows, width), lambda i, me: (0, (i ^ me[0]) * chunks + chunk))
    any_spec = pl.BlockSpec(memory_space=pl.ANY)
    specs = [fixed(p.shape) for p in pieces] + [column, column]
    args = [me_row, *pieces, weight_a, weight_b]
    aliases = {}
    if before is not None:
        specs += [any_spec, any_spec, fixed((rows, LANES))]
        args += before
        aliases = {8: 0, 9: 1}
    return call(
        functools.partial(place_pair_kernel, before is None), (4,), specs, [column, column, fixed((rows, LANES))],
        [shape_of((rows, total), F32)] * 2 + [shape_of((rows, LANES), F32)], args, "place_pair",
        moved=rows * width * 64, prefetch=1, aliases=aliases,
    )


def place_rows_kernel(half, me_ref, *refs):
    block, tile = pl.program_id(0), pl.program_id(1)
    for k in range(5):
        first = jnp.minimum(block, 3) == min(k, 3)

        @pl.when(first if k < 3 else first & ((tile < half) == (k == 3)))
        def _(k=k):
            refs[5][...] = refs[k][...].astype(F32)


def place_rows(me_row, pieces, tall):
    rows, columns = pieces[0].shape
    across = rows // tall
    half = across // 2

    def spec(k):
        if k < 3:
            return pl.BlockSpec((tall, columns), lambda i, j, me: (jnp.where(i == k, j, 0), 0))
        low = (k - 3) * half
        return pl.BlockSpec((tall, columns), lambda i, j, me: (jnp.where(i == 3, jnp.clip(j - low, 0, half - 1), 0), 0))

    return call(
        functools.partial(place_rows_kernel, half), (4, across), [spec(k) for k in range(5)],
        pl.BlockSpec((tall, columns), lambda i, j, me: ((i ^ me[0]) * across + j, 0)),
        shape_of((4 * rows, columns), F32), (me_row, *pieces), "place_rows", moved=rows * columns * 24, prefetch=1,
    )


def place_attn_kernel(kv_local, me_ref, *refs):
    pieces, weights, outs, out_ref, dot_ref = refs[:5], refs[5:8], refs[8:11], refs[11], refs[12]
    width = GROUP * HEAD_DIM
    step = width + 2 * HEAD_DIM

    @pl.when(pl.program_id(0) == 0)
    def _():
        dot_ref[...] = jnp.zeros(dot_ref.shape, F32)

    def emit(values):
        values = values.astype(F32)
        take = lambda start, size: jnp.concatenate(
            [values[:, g * step + start : g * step + start + size] for g in range(kv_local)], axis=1
        )
        parts = (take(0, width), take(width, HEAD_DIM), take(width + HEAD_DIM, HEAD_DIM))
        for part, weight, out in zip(parts, weights, outs):
            out[...] = part
            dot_ref[...] += fold(part * weight[...].astype(F32))
        out_ref[...] = values[:, kv_local * step :].T

    each_piece(pieces, emit)


def place_attn(me_row, pieces, query_weight, key_weight, value_weight, kv_local):
    rows = query_weight.shape[0]
    q_width = kv_local * GROUP * HEAD_DIM
    column = lambda width: pl.BlockSpec((rows, width), lambda i, me: (0, i ^ me[0]))
    columns = [column(q_width), column(kv_local * HEAD_DIM), column(kv_local * HEAD_DIM)]
    weights = (query_weight, key_weight, value_weight)
    return call(
        functools.partial(place_attn_kernel, kv_local), (4,), [fixed(p.shape) for p in pieces] + columns,
        columns + [pl.BlockSpec((q_width, rows), lambda i, me: (i ^ me[0], 0)), fixed((rows, LANES))],
        [shape_of(w.shape, F32) for w in weights] + [shape_of((4 * q_width, rows), F32), shape_of((rows, LANES), F32)],
        (me_row, *pieces, *weights), "place_attn", moved=rows * 5120 * 8, prefetch=1,
    )


CHUNKS = 2


def square_body(
    inputs, cotangent, segments, valid_mask, query_weight, key_weight, value_weight, out_weight,
    gate_weight, up_weight, down_weight, attn_gain, mlp_gain,
):
    count = 4
    me = lax.axis_index("seq")
    me_row = me.reshape(1).astype(jnp.int32)
    core = lax.axis_index("fsdp") % 2
    core_row = core.reshape(1).astype(jnp.int32)
    rows = inputs.shape[1]
    length = rows * count
    kv_local = KV_HEADS // count
    q_width = kv_local * GROUP * HEAD_DIM
    ff_local = FF // count
    ff_chunk = ff_local // CHUNKS
    shard_rows = gate_weight.shape[0]
    step = (GROUP + 2) * HEAD_DIM

    tokens_low, cot_low = inputs[0], cotangent[0]
    marks = jnp.stack([segments[0], valid_mask[0]])
    marks_all = jnp.stack([marks] + [swap(marks, k) for k in range(1, count)])
    x_own = after(tokens_low, marks_all)
    x_x, x_y = to_both(x_own)

    segment_all = marks_all[:, 0].reshape(length)
    valid_all = marks_all[:, 1].reshape(length)
    valid_col = valid_mask[0].astype(F32)[:, None]

    position = (
        (jnp.arange(count, dtype=jnp.int32) ^ me)[:, None] * rows + jnp.arange(rows, dtype=jnp.int32)[None, :]
    ).reshape(length)
    same = (segment_all[:, None] == segment_all[None, :]) & (position[None, :] < position[:, None])
    places = jnp.sum(same.astype(jnp.int32), axis=1).astype(F32)
    half = HEAD_DIM // 2
    frequency = ROPE_BASE ** (-2.0 * jnp.arange(half, dtype=F32) / HEAD_DIM)
    angles_t = frequency[:, None] * places[None, :]
    cosine_t, sine_t = jnp.cos(angles_t), jnp.sin(angles_t)
    cosine = jnp.tile(cosine_t.T, (1, LANES // half))
    sign = jnp.tile(jnp.repeat(jnp.array([-1.0, 1.0], F32), half), LANES // HEAD_DIM)
    sine = jnp.tile(sine_t.T, (1, LANES // half)) * sign[None, :]
    query_row = jnp.where(valid_all == 1, segment_all, -1).reshape(1, length)
    key_col = segment_all.reshape(length, 1)
    tables = (cosine, sine, cosine_t, sine_t)

    gains = jnp.pad(jnp.stack([attn_gain, mlp_gain], axis=1), ((0, 0), (0, LANES - 2)))
    qkv_full = gather_fsdp(pack_qkv(me_row, query_weight, key_weight, value_weight, gains, kv_local))
    out_slice = gather_fsdp(pack_rows(me_row, out_weight, q_width))
    gain_one = qkv_full[:, kv_local * step].astype(F32).reshape(1, D)
    gain_two = qkv_full[:, kv_local * step + 1].astype(F32).reshape(1, D)

    x_far = pass_on(x_x, x_y, cosine, sine)
    entered = enter([x_own, x_x, x_y], gain_one, qkv_full, cosine, sine, kv_local, 0, length)

    down_t = gather_fsdp(pack_rows(me_row, after(down_weight, x_x, x_y, cosine, sine), ff_local))
    later_gate = after(gate_weight, x_x, x_y, cosine, sine)
    gate_up = [
        gather_fsdp(pack_pair(me_row, later_gate, up_weight, CHUNKS, c, ff_chunk)) for c in range(CHUNKS)
    ]

    done = (*x_far, entered[0])
    o_mine = [swap(core_half(after(out_slice, *done), core), k) for k in range(1, count)]
    grad_low = (cot_low.astype(F32) * valid_col).astype(BF)
    x_all, normed_one, q, k, v = enter(
        list(x_far), gain_one, qkv_full, cosine, sine, kv_local, 3 * rows, length, tuple(entered)
    )
    out_0, total_0 = attend_one(me_row, q, k, v, query_row, key_col, rows, 0)

    done = (*o_mine, out_0)
    h_x, h_y = to_both(after(out_0, *done))
    o_other = swap_core(jnp.stack([after(w, *done) for w in o_mine]))
    out_pieces = [out_slice, *o_mine, o_other]
    out_1, total_1 = attend_one(me_row, after(q, *done), k, v, query_row, key_col, rows, 1)
    heads, totals = [out_0, out_1], [total_0, total_1]

    done = (h_x, h_y, out_1, o_other)
    h_far = pass_on(h_x, h_y, *done)
    heads_0 = [out_0, h_x, h_y, *h_far]
    h_x, h_y = to_both(after(out_1, *done))

    done = (*h_far, h_x, h_y)
    h_far = pass_on(h_x, h_y, *done)
    heads_1 = [out_1, h_x, h_y, *h_far]
    c_own = after(grad_low, *done)
    c_x, c_y = to_both(c_own)
    normed_two, attn_branch = leave(core_row, after(x_all, *h_far), gain_two, [heads_0, heads_1], out_pieces, rows)

    done = (c_x, c_y, normed_two, down_t)
    c_far = pass_on(c_x, c_y, *done)
    acted = act_back([after(c_own, *done), c_x, c_y], down_t, 0, length)

    done = (*c_far, acted[0])
    w_mine = [swap(core_half(after(qkv_full, *done)[:, : kv_local * step], core), k) for k in range(1, count)]
    grad_mlp, grad_act = act_back(list(c_far), down_t, 3 * rows, length, tuple(acted))
    act_0, gate_0, up_0 = up_project(normed_two, gate_up[0], grad_act, 0)
    grad_0 = outer(normed_two, [gate_0, up_0], 1024)

    done = (*w_mine, grad_0)
    gate_up_0 = scatter_fsdp(after(grad_0, *done))
    w_other = [swap_core(after(w, *done)) for w in w_mine]
    weight_pieces = [qkv_full, *w_mine, *w_other]
    act_1, gate_1, up_1 = up_project(after(normed_two, *done), gate_up[1], grad_act, 1)
    terms = [(gate_0, gate_up[0], 0), (up_0, gate_up[0], 1), (gate_1, gate_up[1], 0), (up_1, gate_up[1], 1)]

    def terms_after(*events):
        return [(after(terms[0][0], *events), *terms[0][1:])] + terms[1:]

    far = sum_of(terms, 3 * rows, rows, True)

    done = (*far, *w_other)
    g_far = send_far(*far)
    near = sum_of(terms_after(*done), rows, 2 * rows, True)
    near = add_far(near, *g_far)
    g_near = send_near(near)
    [own] = sum_of(terms_after(*near), 0, rows, False)
    grad_1 = outer(after(normed_two, own), [gate_1, up_1], 1024)
    gate_up_1 = scatter_fsdp(after(grad_1, *g_near))
    grad_middle, grad_attn, grad_heads = turn_back(
        core_row, after(own, grad_1), g_near, tokens_low, attn_branch, cot_low, valid_col, gain_two, out_pieces
    )

    head_grads = [grad_heads] + [swap(grad_heads[k], k) for k in range(1, count)]
    p_own = after(gate_up_0, grad_attn)
    p_x, p_y = to_both(p_own)
    grad_down = outer_rows([act_0, act_1], after(grad_mlp, grad_attn), shard_rows)
    grad_out = outer_local(after(grad_attn, grad_down), [heads_0, heads_1])

    def attention_back(queries, group):
        return attend_back_one(
            me_row, queries, k, v, heads[group], head_grads, totals[group], query_row, key_col, tables, rows, group
        )

    done = (*head_grads[1:], p_x, p_y, grad_out)
    out_sum = scatter_fsdp(after(grad_out, *done))
    p_far = pass_on(p_x, p_y, *done)
    p_pieces = [p_own, p_x, p_y, *p_far]
    dqkv_0 = attention_back(after(q, *done), 0)

    done = (*p_far, dqkv_0)
    down_sum = scatter_fsdp(after(grad_down, *done))
    p_own = after(gate_up_1, *done)
    p_x, p_y = to_both(p_own)
    parts_0 = exchange_seq(blocks_of(after(dqkv_0, *done), count))
    dqkv_1 = attention_back(after(q, *done), 1)

    done = (p_x, p_y, *parts_0[1:], dqkv_1)
    parts_1 = exchange_seq(blocks_of(after(dqkv_1, *done), count))
    terms = [(act_0, down_t, 0), (act_1, down_t, 1)]
    far = sum_of(terms_after(*done), 3 * rows, rows, True)
    m_far = send_far(*far)
    near = sum_of(terms_after(*far, *parts_1[1:]), rows, 2 * rows, True)

    near = add_far(near, *m_far)
    near = [jnp.concatenate(near[:2]), jnp.concatenate(near[2:])]
    done = (*near, *parts_1[1:])
    m_x, m_y = swap(near[0], 1), swap(near[1], 2)
    p_far = pass_on(p_x, p_y, *done)
    grad_qkv = outer(after(normed_one, *done), [dqkv_0, dqkv_1], step)
    [own] = sum_of(terms_after(grad_qkv), 0, rows, False)
    input_grad = finish(core_row, after(tokens_low, own), grad_middle, gain_one, [parts_0, parts_1], weight_pieces)

    done = (m_x, m_y, *p_far, input_grad)
    qkv_sum = scatter_fsdp(after(grad_qkv, *done))
    input_grad = input_grad[None]
    out_ready = after(out_sum, *done)
    out_terms = exchange_seq([out_ready[:, k * q_width : (k + 1) * q_width] for k in range(count)])
    d_x, d_y = to_both(after(down_sum, out_ready))
    outputs, stats = last(after(own, *done), m_x, m_y, tokens_low, attn_branch, valid_col)
    outputs = outputs[None]
    placed = place_pair(me_row, [after(p_pieces[0], stats)] + p_pieces[1:], gate_weight, up_weight, CHUNKS, 0, None)

    done = (*out_terms[1:], placed[2])
    out_sum = sum(term.astype(F32) for term in out_terms).astype(BF)
    gate_grad, up_grad, gate_up_dot = place_pair(
        me_row, [after(p_own, *done), p_x, p_y, *p_far], gate_weight, up_weight, CHUNKS, 1, placed
    )

    done = (d_x, d_y, gate_up_dot)
    d_far = pass_on(d_x, d_y, *done)

    t_own = jnp.concatenate([after(qkv_sum, *d_far), out_sum], axis=1)
    t_x, t_y = to_both(t_own)
    stats = after(stats, *d_far)
    stats = stats + swap(stats, 1)
    down_grad = place_rows(me_row, [after(down_sum, *d_far), d_x, d_y, *d_far], 1024)
    t_far = pass_on(t_x, t_y, t_x, t_y, down_grad)
    stats = after(stats, t_x, t_y, down_grad)
    stats = stats + swap(stats, 2)
    query_grad, key_grad, value_grad, out_grad, qkv_dot = place_attn(
        me_row, [after(t_own, down_grad), t_x, t_y, *t_far], query_weight, key_weight, value_weight, kv_local
    )
    attn_gain_grad = jnp.sum(qkv_dot, axis=1) / attn_gain.astype(F32)
    mlp_gain_grad = jnp.sum(gate_up_dot, axis=1) / mlp_gain.astype(F32)

    rms_stats = jnp.sqrt(jnp.sum(stats[:5], axis=1)[None, :] / (jnp.sum(valid_all).astype(F32) * D))
    return (
        outputs, input_grad, query_grad, key_grad, value_grad, out_grad, gate_grad, up_grad, down_grad,
        attn_gain_grad, mlp_gain_grad, rms_stats,
    )


def solution(mesh):
    rows_in = P("fsdp", None)
    columns_in = P(None, "fsdp")
    placed = (
        P("fsdp", "seq", None), P("fsdp", "seq", None), P("fsdp", "seq"), P("fsdp", "seq"),
        rows_in, rows_in, rows_in, columns_in, rows_in, rows_in, columns_in, P("fsdp"), P("fsdp"),
    )
    return jax.shard_map(
        square_body if mesh.shape["seq"] == 4 else general_body,
        mesh=mesh,
        in_specs=placed,
        out_specs=(
            P("fsdp", "seq", None), P("fsdp", "seq", None), rows_in, rows_in, rows_in, columns_in,
            rows_in, rows_in, columns_in, P("fsdp"), P("fsdp"), P("fsdp", None),
        ),
        check_vma=False,
    )
```

```python
import functools

import jax
import jax.numpy as jnp
from jax import lax
from jax.experimental import pallas as pl
from jax.experimental.pallas import tpu as pltpu
from jax.sharding import PartitionSpec as P

D = 2048
HEADS = 32
KV_HEADS = 8
HEAD_DIM = 64
GROUP = HEADS // KV_HEADS
FF = 8192
EPSILON = 1e-05
ROPE_BASE = 500000.0
NEGATIVE = -1e30
SCALE = HEAD_DIM**-0.5
BF = jnp.bfloat16
F32 = jnp.float32
LANES = 128
VMEM_LIMIT = 60 * 1024 * 1024
NT = (((1,), (1,)), ((), ()))
NN = (((1,), (0,)), ((), ()))
TN = (((0,), (0,)), ((), ()))


def dot(left, right, dims=NN):
    return lax.dot_general(left, right, dims, preferred_element_type=F32)


def params(grid_rank):
    return pltpu.CompilerParams(
        dimension_semantics=("arbitrary",) * grid_rank, vmem_limit_bytes=VMEM_LIMIT
    )


def swap(values, bit):
    count = lax.axis_size("seq")
    return lax.ppermute(values, "seq", [(i, i ^ bit) for i in range(count)])


def bit_orders():
    bits = [1 << b for b in range(lax.axis_size("seq").bit_length() - 1)]
    return bits, bits[::-1]


def gather_stream(block, order):
    held, owners = block[None], [0]
    for bit in order:
        held = jnp.concatenate([held, swap(held, bit)], axis=0)
        owners = owners + [k ^ bit for k in owners]
    return [held[owners.index(k)] for k in range(len(owners))]


def gather_seq(block):
    half = block.shape[-1] // 2
    low_order, high_order = bit_orders()
    low = gather_stream(block[..., :half], low_order)
    high = gather_stream(block[..., half:], high_order)
    return [jnp.concatenate(pair, axis=-1) for pair in zip(low, high)]


def reduce_stream(blocks, order):
    held = {k: b for k, b in enumerate(blocks)}
    for bit in order:
        away = sorted(k for k in held if k & bit)
        sent = swap(jnp.stack([held[k].astype(BF) for k in away]), bit)
        held = {
            k: held[k].astype(F32) + sent[away.index(k ^ bit)].astype(F32)
            for k in held
            if not k & bit
        }
    return held[0]


def reduce_seq(blocks):
    half = blocks[0].shape[-1] // 2
    low_order, high_order = bit_orders()
    low = reduce_stream([b[..., :half] for b in blocks], low_order)
    high = reduce_stream([b[..., half:] for b in blocks], high_order)
    return jnp.concatenate([low, high], axis=-1)


def exchange_seq(blocks):
    return [b if k == 0 else swap(b, k) for k, b in enumerate(blocks)]


def gather_fsdp(shard):
    return lax.all_gather(shard, "fsdp", axis=0, tiled=True)


def scatter_fsdp(values):
    return lax.psum_scatter(values, "fsdp", scatter_dimension=0, tiled=True)


def turn(values, cosine, sine):
    lane = lax.broadcasted_iota(jnp.int32, values.shape, 1)
    half = HEAD_DIM // 2
    ahead = pltpu.roll(values, LANES - half, 1)
    behind = pltpu.roll(values, half, 1)
    return values * cosine + jnp.where(lane % HEAD_DIM < half, ahead, behind) * sine


def project_kernel(kv_local, x_ref, gain_ref, w_ref, cos_ref, sin_ref, normed_ref, q_ref, k_ref, v_ref):
    x = x_ref[...].astype(F32)
    inv = lax.rsqrt(jnp.mean(x * x, axis=-1, keepdims=True) + EPSILON)
    normed = (x * inv * gain_ref[...]).astype(BF)
    normed_ref[...] = normed
    q_width = kv_local * GROUP * HEAD_DIM
    kv_width = kv_local * HEAD_DIM
    lin = dot(normed, w_ref[:, : q_width + 2 * kv_width])
    cosine, sine = cos_ref[...], sin_ref[...]
    for start in range(0, q_width, LANES):
        part = turn(lin[:, start : start + LANES], cosine, sine) * SCALE
        q_ref[:, start : start + LANES] = part.astype(BF)
    for start in range(0, kv_width, LANES):
        part = turn(lin[:, q_width + start : q_width + start + LANES], cosine, sine)
        for at in range(0, min(LANES, kv_width - start), HEAD_DIM):
            k_ref[(start + at) // HEAD_DIM] = part[:, at : at + HEAD_DIM].astype(BF)
    for head in range(kv_local):
        start = q_width + kv_width + head * HEAD_DIM
        v_ref[head] = lin[:, start : start + HEAD_DIM].astype(BF)


def project(x, gain_row, weight, cosine, sine, kv_local):
    rows = x.shape[0]
    block = 256
    q_width = kv_local * GROUP * HEAD_DIM
    by_row = lambda i: (i, 0)
    whole = lambda i: (0, 0)
    by_head = lambda i: (0, i, 0)
    return pl.pallas_call(
        functools.partial(project_kernel, kv_local),
        grid=(rows // block,),
        in_specs=[
            pl.BlockSpec((block, D), by_row),
            pl.BlockSpec((1, D), whole),
            pl.BlockSpec(weight.shape, whole),
            pl.BlockSpec((block, LANES), by_row),
            pl.BlockSpec((block, LANES), by_row),
        ],
        out_specs=[
            pl.BlockSpec((block, D), by_row),
            pl.BlockSpec((block, q_width), by_row),
            pl.BlockSpec((kv_local, block, HEAD_DIM), by_head),
            pl.BlockSpec((kv_local, block, HEAD_DIM), by_head),
        ],
        out_shape=[
            jax.ShapeDtypeStruct((rows, D), BF),
            jax.ShapeDtypeStruct((rows, q_width), BF),
            jax.ShapeDtypeStruct((kv_local, rows, HEAD_DIM), BF),
            jax.ShapeDtypeStruct((kv_local, rows, HEAD_DIM), BF),
        ],
        compiler_params=params(1),
        cost_estimate=pl.CostEstimate(
            flops=2 * rows * D * weight.shape[1], bytes_accessed=rows * D * 6, transcendentals=0
        ),
        name="project",
    )(x, gain_row, weight, cosine, sine)


def pair_bias(rows, query_index, key_index, query_row, key_col):
    key_pos = key_index * rows + lax.broadcasted_iota(jnp.int32, (rows, rows), 0)
    query_pos = query_index * rows + lax.broadcasted_iota(jnp.int32, (rows, rows), 1)
    allowed = ((key_col == query_row) & (key_pos <= query_pos)) | (key_pos == query_pos)
    return jnp.where(allowed, 0.0, NEGATIVE)


def attend_kernel(rows, me_ref, q_ref, k_ref, v_ref, query_row_ref, key_col_ref, out_ref, total_ref, v_t, peak, total, acc):
    index = pl.program_id(1)
    me = me_ref[0]

    @pl.when(index == 0)
    def _():
        v_t[...] = v_ref[0].astype(F32).T.astype(BF)

    peak[...] = jnp.full(peak.shape, NEGATIVE, F32)
    total[...] = jnp.zeros(total.shape, F32)
    acc[...] = jnp.zeros(acc.shape, F32)

    def step(j, _):
        at = pl.multiple_of((j ^ me) * rows, rows)
        keys = k_ref[0, pl.ds(at, rows), :]
        values_t = v_t[:, pl.ds(at, rows)]
        bias = pair_bias(rows, index, j, query_row_ref[...], key_col_ref[pl.ds(at, rows), :])
        for head in range(GROUP):
            query = q_ref[:, head * HEAD_DIM : (head + 1) * HEAD_DIM]
            scores = dot(keys, query, NT) + bias
            old = peak[head : head + 1, :]
            new = jnp.maximum(old, jnp.max(scores, axis=0, keepdims=True))
            expo = jnp.exp(scores - new)
            fade = jnp.exp(old - new)
            peak[head : head + 1, :] = new
            total[head : head + 1, :] = total[head : head + 1, :] * fade + jnp.sum(expo, axis=0, keepdims=True)
            acc[head] = acc[head] * fade + dot(values_t, expo.astype(BF))
        return 0

    lax.fori_loop(0, index + 1, step, 0)
    for head in range(GROUP):
        out = acc[head] / total[head : head + 1, :]
        out_ref[:, head * HEAD_DIM : (head + 1) * HEAD_DIM] = out.T.astype(BF)
    total_ref[0] = peak[...] + jnp.log(total[...])


def attend(me, q, k, v, query_row, key_col, rows):
    kv_local, length = k.shape[0], k.shape[1]
    count = length // rows
    width = GROUP * HEAD_DIM
    return pl.pallas_call(
        functools.partial(attend_kernel, rows),
        grid_spec=pltpu.PrefetchScalarGridSpec(
            num_scalar_prefetch=1,
            grid=(kv_local, count),
            in_specs=[
                pl.BlockSpec((rows, width), lambda g, i, me: (i ^ me[0], g)),
                pl.BlockSpec((1, length, HEAD_DIM), lambda g, i, me: (g, 0, 0)),
                pl.BlockSpec((1, length, HEAD_DIM), lambda g, i, me: (g, 0, 0)),
                pl.BlockSpec((1, rows), lambda g, i, me: (0, i ^ me[0])),
                pl.BlockSpec((length, 1), lambda g, i, me: (0, 0)),
            ],
            out_specs=[
                pl.BlockSpec((rows, width), lambda g, i, me: (i ^ me[0], g)),
                pl.BlockSpec((1, GROUP, rows), lambda g, i, me: (g, 0, i ^ me[0])),
            ],
            scratch_shapes=[
                pltpu.VMEM((HEAD_DIM, length), BF),
                pltpu.VMEM((GROUP, rows), F32),
                pltpu.VMEM((GROUP, rows), F32),
                pltpu.VMEM((GROUP, HEAD_DIM, rows), F32),
            ],
        ),
        out_shape=[
            jax.ShapeDtypeStruct((length, kv_local * width), BF),
            jax.ShapeDtypeStruct((kv_local, GROUP, length), F32),
        ],
        compiler_params=params(2),
        cost_estimate=pl.CostEstimate(
            flops=kv_local * GROUP * length * length * HEAD_DIM * 8, bytes_accessed=1 << 24, transcendentals=0
        ),
        name="attend",
    )(me, q, k, v, query_row, key_col)


def attend_back_kernel(
    rows, count, me_ref, q_ref, k_ref, v_ref, out_ref, grad_ref, total_ref, query_row_ref, key_col_ref,
    cos_ref, sin_ref, cos_t_ref, sin_t_ref, dq_ref, dk_ref, dv_ref, k_t, inner, dq_t, dk_acc, dv_acc,
):
    me = me_ref[0]
    half = HEAD_DIM // 2
    k_t[...] = k_ref[0].astype(F32).T.astype(BF)
    dq_t[...] = jnp.zeros(dq_t.shape, F32)

    def prepare(i, _):
        here = pl.ds(pl.multiple_of(i * rows, rows), rows)
        for head in range(GROUP):
            cols = slice(head * HEAD_DIM, (head + 1) * HEAD_DIM)
            both = out_ref[here, cols].astype(F32) * grad_ref[here, cols].astype(F32)
            inner[head : head + 1, here] = jnp.sum(both.T, axis=0, keepdims=True)
        return 0

    lax.fori_loop(0, count, prepare, 0)

    def key_step(j, _):
        key_at = pl.ds(pl.multiple_of((j ^ me) * rows, rows), rows)
        keys, values = k_ref[0, key_at, :], v_ref[0, key_at, :]
        keys_t = k_t[:, key_at]
        key_col = key_col_ref[key_at, :]
        dk_acc[...] = jnp.zeros(dk_acc.shape, F32)
        dv_acc[...] = jnp.zeros(dv_acc.shape, F32)

        def query_step(i, _):
            at = pl.ds(pl.multiple_of((i ^ me) * rows, rows), rows)
            bias = pair_bias(rows, i, j, query_row_ref[:, at], key_col)
            for head in range(GROUP):
                cols = slice(head * HEAD_DIM, (head + 1) * HEAD_DIM)
                query, grad = q_ref[at, cols], grad_ref[at, cols]
                probs = jnp.exp(dot(keys, query, NT) + bias - total_ref[0, head : head + 1, at])
                dv_acc[...] += dot(probs.astype(BF), grad)
                grad_probs = dot(values, grad, NT)
                grad_scores = (probs * (grad_probs - inner[head : head + 1, at])).astype(BF)
                dk_acc[...] += dot(grad_scores, query)
                dq_t[head, :, at] += dot(keys_t, grad_scores)
            return 0

        lax.fori_loop(j, count, query_step, 0)
        dk = dk_acc[...]
        low, high = dk[:, :half], dk[:, half:]
        cosine, sine = cos_ref[key_at, :half], sin_ref[key_at, half:HEAD_DIM]
        dk_ref[0, key_at, :] = jnp.concatenate(
            [low * cosine + high * sine, high * cosine - low * sine], axis=1
        ).astype(BF)
        dv_ref[0, key_at, :] = dv_acc[...].astype(BF)
        return 0

    lax.fori_loop(0, count, key_step, 0)

    def finish(i, _):
        here = pl.ds(pl.multiple_of(i * rows, rows), rows)
        cosine, sine = cos_t_ref[:, here], sin_t_ref[:, here]
        for head in range(GROUP):
            low, high = dq_t[head, :half, here], dq_t[head, half:, here]
            turned = jnp.concatenate([low * cosine + high * sine, high * cosine - low * sine], axis=0) * SCALE
            dq_ref[here, head * HEAD_DIM : (head + 1) * HEAD_DIM] = turned.T.astype(BF)
        return 0

    lax.fori_loop(0, count, finish, 0)


def attend_back(me, q, k, v, out, grad, totals, query_row, key_col, cosine, sine, cosine_t, sine_t, rows):
    kv_local, length = k.shape[0], k.shape[1]
    width = GROUP * HEAD_DIM
    by_group = pl.BlockSpec((length, width), lambda g, me: (0, g))
    by_head = pl.BlockSpec((1, length, HEAD_DIM), lambda g, me: (g, 0, 0))
    whole = lambda shape: pl.BlockSpec(shape, lambda g, me: (0, 0))
    return pl.pallas_call(
        functools.partial(attend_back_kernel, rows, length // rows),
        grid_spec=pltpu.PrefetchScalarGridSpec(
            num_scalar_prefetch=1,
            grid=(kv_local,),
            in_specs=[
                by_group,
                by_head,
                by_head,
                by_group,
                by_group,
                pl.BlockSpec((1, GROUP, length), lambda g, me: (g, 0, 0)),
                whole((1, length)),
                whole((length, 1)),
                whole((length, LANES)),
                whole((length, LANES)),
                whole((HEAD_DIM // 2, length)),
                whole((HEAD_DIM // 2, length)),
            ],
            out_specs=[by_group, by_head, by_head],
            scratch_shapes=[
                pltpu.VMEM((HEAD_DIM, length), BF),
                pltpu.VMEM((GROUP, length), F32),
                pltpu.VMEM((GROUP, HEAD_DIM, length), F32),
                pltpu.VMEM((rows, HEAD_DIM), F32),
                pltpu.VMEM((rows, HEAD_DIM), F32),
            ],
        ),
        out_shape=[
            jax.ShapeDtypeStruct((length, kv_local * width), BF),
            jax.ShapeDtypeStruct((kv_local, length, HEAD_DIM), BF),
            jax.ShapeDtypeStruct((kv_local, length, HEAD_DIM), BF),
        ],
        compiler_params=params(1),
        cost_estimate=pl.CostEstimate(
            flops=kv_local * GROUP * length * length * HEAD_DIM * 20, bytes_accessed=1 << 24, transcendentals=0
        ),
        name="attend_back",
    )(me, q, k, v, out, grad, totals, query_row, key_col, cosine, sine, cosine_t, sine_t)


def norm_scale(values):
    return lax.rsqrt(jnp.mean(values * values, axis=-1, keepdims=True) + EPSILON)


def norm_back(grad_normed, values, inv_rms, gain_row):
    unit_rows = values * inv_rms
    scaled = grad_normed * gain_row
    return inv_rms * (scaled - unit_rows * jnp.mean(scaled * unit_rows, axis=-1, keepdims=True))


def blocks_of(values, count):
    rows = values.shape[0] // count
    return [values[k * rows : (k + 1) * rows] for k in range(count)]


def whole_columns(blocks, me):
    stacked = jnp.stack(blocks)
    ordered = [
        lax.dynamic_index_in_dim(stacked, p ^ me, 0, keepdims=False) for p in range(len(blocks))
    ]
    return jnp.concatenate(ordered, axis=1).astype(F32)


def general_body(
    inputs, cotangent, segments, valid_mask, query_weight, key_weight, value_weight, out_weight,
    gate_weight, up_weight, down_weight, attn_gain, mlp_gain,
):
    count = lax.axis_size("seq")
    me = lax.axis_index("seq")
    me_row = me.reshape(1).astype(jnp.int32)
    rows = inputs.shape[1]
    length = rows * count
    kv_local = KV_HEADS // count
    q_width = kv_local * GROUP * HEAD_DIM
    kv_width = kv_local * HEAD_DIM
    ff_local = FF // count
    shard_rows = gate_weight.shape[0]

    def mine(weight, width, axis=1):
        return lax.dynamic_slice_in_dim(weight, me * width, width, axis)

    gains = jnp.pad(jnp.stack([attn_gain, mlp_gain], axis=1), ((0, 0), (0, LANES - 2)))
    qkv_shard = jnp.concatenate(
        [mine(query_weight, q_width), mine(key_weight, kv_width), mine(value_weight, kv_width), gains], axis=1
    )
    qkv_full = gather_fsdp(qkv_shard)
    out_slice = gather_fsdp(mine(out_weight, q_width, 0).T)
    down_t = gather_fsdp(mine(down_weight, ff_local, 0).T)
    gate_up = gather_fsdp(jnp.concatenate([mine(gate_weight, ff_local), mine(up_weight, ff_local)], axis=1))
    gain_one = qkv_full[:, q_width + 2 * kv_width].astype(F32).reshape(1, D)
    gain_two = qkv_full[:, q_width + 2 * kv_width + 1].astype(F32).reshape(1, D)
    qkv_weight = qkv_full[:, : q_width + 2 * kv_width]

    marks = jnp.stack([segments[0], valid_mask[0]])
    marks_all = jnp.stack(gather_stream(marks, bit_orders()[0]))
    segment_all = marks_all[:, 0].reshape(length)
    valid_all = marks_all[:, 1].reshape(length)
    x_all = jnp.concatenate(gather_seq(inputs[0]), axis=0)
    valid_col = valid_mask[0].astype(F32)[:, None]
    grad_final = cotangent[0].astype(F32) * valid_col
    grad_mlp = jnp.concatenate(gather_seq(grad_final.astype(BF)), axis=0)

    position = (
        (jnp.arange(count, dtype=jnp.int32) ^ me)[:, None] * rows + jnp.arange(rows, dtype=jnp.int32)[None, :]
    ).reshape(length)
    same = (segment_all[:, None] == segment_all[None, :]) & (position[None, :] < position[:, None])
    places = jnp.sum(same.astype(jnp.int32), axis=1).astype(F32)
    half = HEAD_DIM // 2
    frequency = ROPE_BASE ** (-2.0 * jnp.arange(half, dtype=F32) / HEAD_DIM)
    angles_t = frequency[:, None] * places[None, :]
    cosine_t, sine_t = jnp.cos(angles_t), jnp.sin(angles_t)
    cosine = jnp.tile(cosine_t.T, (1, LANES // half))
    sign = jnp.tile(jnp.repeat(jnp.array([-1.0, 1.0], F32), half), LANES // HEAD_DIM)
    sine = jnp.tile(sine_t.T, (1, LANES // half)) * sign[None, :]
    query_row = jnp.where(valid_all == 1, segment_all, -1).reshape(1, length)
    key_col = segment_all.reshape(length, 1)

    normed_one, q, k, v = project(x_all, gain_one, qkv_full, cosine, sine, kv_local)
    heads_own, totals = attend(me_row, q, k, v, query_row, key_col, rows)

    heads_blocks = gather_seq(heads_own)
    heads_all = jnp.concatenate(
        [
            jnp.concatenate([blocks_of(heads_blocks[k], count)[i ^ k] for i in range(count)], axis=0)
            for k in range(count)
        ],
        axis=1,
    )
    out_blocks = gather_seq(out_slice)
    out_t = jnp.concatenate(out_blocks, axis=1)
    attn_all = dot(heads_all, out_t, NT)
    middle_all = x_all.astype(F32) + attn_all
    normed_two = (middle_all * norm_scale(middle_all) * gain_two).astype(BF)
    tokens = inputs[0].astype(F32)
    attn_branch = attn_all[:rows]
    middle = tokens + attn_branch
    inv_two = norm_scale(middle)

    gate_full, up_full = gate_up[:, :ff_local], gate_up[:, ff_local:]
    gate_lin = dot(normed_two, gate_full)
    up_lin = dot(normed_two, up_full)
    sigmoid_gate = jax.nn.sigmoid(gate_lin)
    silu_gate = gate_lin * sigmoid_gate
    activated = (silu_gate * up_lin).astype(BF)
    grad_act = dot(grad_mlp, down_t)
    grad_gate = (grad_act * up_lin * sigmoid_gate * (1.0 + gate_lin * (1.0 - sigmoid_gate))).astype(BF)
    grad_up = (grad_act * silu_gate).astype(BF)
    mlp_part = dot(activated, down_t, NT).astype(BF)
    grad_both = jnp.concatenate([grad_gate, grad_up], axis=1)
    grad_two_part = dot(grad_both, gate_up, NT).astype(BF)
    grad_normed_two = reduce_seq(blocks_of(grad_two_part, count))
    mlp_branch = reduce_seq(blocks_of(mlp_part, count))
    final = middle + mlp_branch
    outputs = final.astype(BF)[None]

    gate_up_grad = scatter_fsdp(dot(normed_two, grad_both, TN).astype(BF))
    down_grad_t = scatter_fsdp(dot(grad_mlp, activated, TN).astype(BF))

    grad_middle = grad_final + norm_back(grad_normed_two, middle, inv_two, gain_two)
    grad_attn = grad_middle.astype(BF)
    grad_heads = jnp.concatenate(
        exchange_seq([dot(grad_attn, b).astype(BF) for b in out_blocks]), axis=0
    )
    grad_attn_all = jnp.concatenate(gather_seq(grad_attn), axis=0)
    out_grad_t = scatter_fsdp(dot(grad_attn_all, heads_own, TN).astype(BF))

    dq, dk, dv = attend_back(
        me_row, q, k, v, heads_own, grad_heads, totals, query_row, key_col, cosine, sine, cosine_t, sine_t, rows
    )
    dqkv = jnp.concatenate([dq] + [dk[g] for g in range(kv_local)] + [dv[g] for g in range(kv_local)], axis=1)
    qkv_grad = scatter_fsdp(dot(normed_one, dqkv, TN).astype(BF))
    weight_blocks = gather_seq(qkv_weight)
    parts = exchange_seq(blocks_of(dqkv, count))
    grad_normed_one = dot(jnp.concatenate(parts, axis=1), jnp.concatenate(weight_blocks, axis=1), NT)
    inv_one = norm_scale(tokens)
    input_grad = (grad_middle + norm_back(grad_normed_one, tokens, inv_one, gain_one)).astype(BF)[None]

    gate_up_blocks = gather_seq(gate_up_grad)
    gate_grad = whole_columns([b[:, :ff_local] for b in gate_up_blocks], me)
    up_grad = whole_columns([b[:, ff_local:] for b in gate_up_blocks], me)
    down_grad = whole_columns(gather_seq(down_grad_t), me).T
    out_grad = whole_columns(gather_seq(out_grad_t), me).T
    qkv_blocks = gather_seq(qkv_grad)
    query_grad = whole_columns([b[:, :q_width] for b in qkv_blocks], me)
    key_grad = whole_columns([b[:, q_width : q_width + kv_width] for b in qkv_blocks], me)
    value_grad = whole_columns([b[:, q_width + kv_width :] for b in qkv_blocks], me)

    def rows_dot(weight, grad):
        return jnp.sum(weight.astype(F32) * grad, axis=1)

    attn_gain_grad = (
        rows_dot(query_weight, query_grad) + rows_dot(key_weight, key_grad) + rows_dot(value_weight, value_grad)
    ) / attn_gain.astype(F32)
    mlp_gain_grad = (rows_dot(gate_weight, gate_grad) + rows_dot(up_weight, up_grad)) / mlp_gain.astype(F32)

    squares = [jnp.sum(valid_col * part * part) for part in (tokens, middle, final, attn_branch, mlp_branch)]
    stats = jnp.stack([jnp.sum(valid_col)] + squares)
    stats = jnp.broadcast_to(jnp.pad(stats, (0, LANES - 6))[None, :], (8, LANES))
    for bit in bit_orders()[0]:
        stats = stats + swap(stats, bit)
    rms_stats = jnp.sqrt(stats[:1, 1:6] / (stats[:1, :1] * D))
    return (
        outputs, input_grad, query_grad, key_grad, value_grad, out_grad, gate_grad, up_grad, down_grad,
        attn_gain_grad, mlp_gain_grad, rms_stats,
    )


TILE = 256

def after(value, *events):
    return lax.optimization_barrier((value,) + events)[0]


def to_both(block):
    return swap(block, 1), swap(block, 2)


def pass_on(by_x, by_y, *events):
    half = by_x.shape[0] // 2
    return swap(after(by_y[:half], *events), 1), swap(after(by_x[half:], *events), 2)


def swap_core(values):
    count = lax.axis_size("fsdp")
    return lax.ppermute(values, "fsdp", [(i, i ^ 1) for i in range(count)])


def core_half(weight, core):
    half = weight.shape[0] // 2
    return lax.dynamic_slice_in_dim(weight, core * half, half, 0)


def in_order(core, mine, other):
    return jnp.where(core == 0, jnp.concatenate([mine, other], axis=1), jnp.concatenate([other, mine], axis=1))


def add_low(a, b):
    return (a.astype(F32) + b.astype(F32)).astype(BF)


def send_far(low, high):
    return swap(low, 1), swap(high, 2)


def add_far(near, low, high):
    x_low, x_high, y_low, y_high = near
    return [x_low, add_low(x_high, high), add_low(y_low, low), y_high]


def send_near(near):
    return [swap(part, bit) for part, bit in zip(near, (1, 1, 2, 2))]


def call(kernel, grid, in_specs, out_specs, out_shape, args, name, flops=0, moved=0, scratch=(), prefetch=0, aliases=None):
    return pl.pallas_call(
        kernel,
        grid_spec=pltpu.PrefetchScalarGridSpec(
            num_scalar_prefetch=prefetch,
            grid=grid,
            in_specs=in_specs,
            out_specs=out_specs,
            scratch_shapes=list(scratch),
        ),
        out_shape=out_shape,
        input_output_aliases=aliases or {},
        compiler_params=pltpu.CompilerParams(
            dimension_semantics=("arbitrary",) * len(grid), vmem_limit_bytes=VMEM_LIMIT
        ),
        cost_estimate=pl.CostEstimate(flops=int(flops), bytes_accessed=int(moved), transcendentals=0),
        name=name,
    )(*args)


def shape_of(shape, dtype=BF):
    return jax.ShapeDtypeStruct(shape, dtype)


def fixed(shape, buffers=None):
    mode = {} if buffers is None else {"pipeline_mode": pl.Buffered(buffers)}
    return pl.BlockSpec(shape, lambda *_: (0,) * len(shape), **mode)


def piece_specs(pieces, tile):
    specs, spans, start = [], [], 0
    for piece in pieces:
        tiles = piece.shape[0] // tile
        specs.append(
            pl.BlockSpec(
                (tile, piece.shape[1]),
                lambda i, *_, start=start, tiles=tiles: (jnp.clip(i - start, 0, tiles - 1), 0),
            )
        )
        spans.append((start, start + tiles))
        start += tiles
    return specs, spans


def copy_piece(refs, spans, index, target):
    for ref, (first, last) in zip(refs, spans):

        @pl.when((index >= first) & (index < last))
        def _(ref=ref):
            target[...] = ref[...]


def act_back_kernel(spans, others, *refs):
    weight_ref = refs[len(spans)]
    whole_ref, out_ref = refs[len(spans) + 1 + others :]
    copy_piece(refs[: len(spans)], spans, pl.program_id(0), whole_ref)
    out_ref[...] = dot(whole_ref[...], weight_ref[...]).astype(BF)


def act_back(pieces, weight, first, rows, before=()):
    specs, spans = piece_specs(pieces, TILE)
    tiles, skip, width = spans[-1][1], first // TILE, weight.shape[1]
    by_row = lambda w: pl.BlockSpec((TILE, w), lambda i: (skip + i, 0))
    count = len(pieces) + 1
    return call(
        functools.partial(act_back_kernel, spans, len(before)), (tiles,),
        specs + [fixed(weight.shape)] + [pl.BlockSpec(memory_space=pl.ANY)] * len(before),
        [by_row(D), by_row(width)], [shape_of((rows, D)), shape_of((rows, width))],
        (*pieces, weight, *before), "act_back", flops=2 * tiles * TILE * D * width, moved=tiles * TILE * D * 6,
        aliases={count + k: k for k in range(len(before))},
    )


def pack_qkv_kernel(kv_local, me_ref, q_ref, k_ref, v_ref, gains_ref, out_ref):
    width = GROUP * HEAD_DIM
    parts = []
    for g in range(kv_local):
        head = slice(g * HEAD_DIM, (g + 1) * HEAD_DIM)
        parts += [q_ref[:, g * width : (g + 1) * width], jnp.concatenate([k_ref[:, head], v_ref[:, head]], axis=1)]
    out_ref[...] = jnp.concatenate(parts + [gains_ref[...]], axis=1)


def pack_qkv(me_row, query_weight, key_weight, value_weight, gains, kv_local):
    rows = query_weight.shape[0]
    q_width, kv_width = kv_local * GROUP * HEAD_DIM, kv_local * HEAD_DIM
    total = q_width + 2 * kv_width + LANES
    mine = lambda width: pl.BlockSpec((rows, width), lambda i, me: (0, me[0]))
    return call(
        functools.partial(pack_qkv_kernel, kv_local), (1,),
        [mine(q_width), mine(kv_width), mine(kv_width), fixed((rows, LANES))],
        fixed((rows, total)), shape_of((rows, total)),
        (me_row, query_weight, key_weight, value_weight, gains), "pack_qkv", moved=4 * rows * total, prefetch=1,
    )


def pack_rows_kernel(me_ref, in_ref, out_ref):
    out_ref[...] = in_ref[...].astype(F32).T.astype(BF)


def pack_rows(me_row, weight, rows, owners=(0,)):
    tile = 512
    tiles, columns = rows // tile, weight.shape[1]

    def index(i, me):
        owner = sum(jnp.where(i // tiles == k, owner, 0) for k, owner in enumerate(owners))
        return ((me[0] ^ owner) * tiles + i % tiles, 0)

    return call(
        pack_rows_kernel, (tiles * len(owners),), [pl.BlockSpec((tile, columns), index)],
        pl.BlockSpec((columns, tile), lambda i, me: (0, i)), shape_of((columns, rows * len(owners))), (me_row, weight),
        "pack_rows", moved=4 * rows * columns, prefetch=1,
    )


def pack_pair_kernel(me_ref, a_ref, b_ref, out_ref):
    width = a_ref.shape[1]
    out_ref[:, :width] = a_ref[...]
    out_ref[:, width:] = b_ref[...]


def pack_pair(me_row, a, b, chunks, chunk, width):
    rows = a.shape[0]
    spec = pl.BlockSpec((rows, width), lambda i, me: (0, me[0] * chunks + chunk))
    return call(
        pack_pair_kernel, (1,), [spec, spec], fixed((rows, 2 * width)), shape_of((rows, 2 * width)), (me_row, a, b),
        "pack_pair", moved=8 * rows * width, prefetch=1,
    )


def enter_kernel(kv_local, spans, others, *refs):
    pieces = refs[: len(spans)]
    gain_ref, w_ref, cos_ref, sin_ref = refs[len(spans) : len(spans) + 4]
    x_ref, normed_ref, q_ref, k_ref, v_ref = refs[len(spans) + 4 + others :]
    copy_piece(pieces, spans, pl.program_id(0), x_ref)
    x = x_ref[...].astype(F32)
    inv = lax.rsqrt(jnp.mean(x * x, axis=-1, keepdims=True) + EPSILON)
    normed = (x * inv * gain_ref[...]).astype(BF)
    normed_ref[...] = normed
    width = GROUP * HEAD_DIM
    step = width + 2 * HEAD_DIM
    lin = dot(normed, w_ref[:, : kv_local * step])
    cosine, sine = cos_ref[...], sin_ref[...]
    for g in range(kv_local):
        for start in range(0, width, LANES):
            part = turn(lin[:, g * step + start : g * step + start + LANES], cosine, sine) * SCALE
            q_ref[:, g * width + start : g * width + start + LANES] = part.astype(BF)
        pair = lin[:, g * step + width : (g + 1) * step]
        k_ref[g] = turn(pair, cosine, sine)[:, :HEAD_DIM].astype(BF)
        v_ref[g] = pair[:, HEAD_DIM:].astype(BF)


def enter(pieces, gain_row, weight, cosine, sine, kv_local, first, rows, before=()):
    specs, spans = piece_specs(pieces, TILE)
    tiles, skip = spans[-1][1], first // TILE
    q_width = kv_local * GROUP * HEAD_DIM
    by_row = lambda width: pl.BlockSpec((TILE, width), lambda i: (skip + i, 0))
    by_head = pl.BlockSpec((kv_local, TILE, HEAD_DIM), lambda i: (0, skip + i, 0))
    heads = shape_of((kv_local, rows, HEAD_DIM))
    count = len(pieces) + 4
    return call(
        functools.partial(enter_kernel, kv_local, spans, len(before)), (tiles,),
        specs
        + [fixed((1, D)), fixed(weight.shape), by_row(LANES), by_row(LANES)]
        + [pl.BlockSpec(memory_space=pl.ANY)] * len(before),
        [by_row(D), by_row(D), by_row(q_width), by_head, by_head],
        [shape_of((rows, D)), shape_of((rows, D)), shape_of((rows, q_width)), heads, heads],
        (*pieces, gain_row, weight, cosine, sine, *before), "enter",
        flops=2 * tiles * TILE * D * weight.shape[1], moved=tiles * TILE * D * 8,
        aliases={count + k: k for k in range(len(before))},
    )


def allowed_bias(rows, size, first, query_row, key_col, diagonal):
    allowed = key_col == query_row
    if diagonal:
        key_pos = lax.broadcasted_iota(jnp.int32, (size, rows - first), 0)
        query_pos = lax.broadcasted_iota(jnp.int32, (size, rows - first), 1)
        allowed = (allowed & (key_pos <= query_pos)) | (key_pos == query_pos)
    return jnp.where(allowed, 0.0, NEGATIVE)


def attend_one_kernel(rows, me_ref, q_ref, k_ref, v_ref, query_row_ref, key_col_ref, out_ref, total_ref, v_t, peak, total, acc):
    index = pl.program_id(1)
    me = me_ref[0]
    half = rows // 2

    @pl.when(index == 0)
    def _():
        v_t[...] = v_ref[0].astype(F32).T.astype(BF)

    peak[...] = jnp.full(peak.shape, NEGATIVE, F32)
    total[...] = jnp.zeros(total.shape, F32)
    acc[...] = jnp.zeros(acc.shape, F32)

    def visit(at, size, first, diagonal):
        keys = k_ref[0, pl.ds(at, size), :]
        values_t = v_t[:, pl.ds(at, size)]
        bias = allowed_bias(rows, size, first, query_row_ref[:, first:], key_col_ref[pl.ds(at, size), :], diagonal)
        for head in range(GROUP):
            query = q_ref[first:, head * HEAD_DIM : (head + 1) * HEAD_DIM]
            scores = dot(keys, query, NT) + bias
            old = peak[head : head + 1, first:]
            new = jnp.maximum(old, jnp.max(scores, axis=0, keepdims=True))
            expo = jnp.exp(scores - new)
            fade = jnp.exp(old - new)
            peak[head : head + 1, first:] = new
            total[head : head + 1, first:] = total[head : head + 1, first:] * fade + jnp.sum(expo, axis=0, keepdims=True)
            acc[head, :, first:] = acc[head, :, first:] * fade + dot(values_t, expo.astype(BF))

    here = pl.multiple_of((index ^ me) * rows, rows)
    visit(here, half, 0, True)
    visit(pl.multiple_of(here + half, half), half, half, True)

    def step(j, _):
        visit(pl.multiple_of((j ^ me) * rows, rows), rows, 0, False)
        return 0

    lax.fori_loop(0, index, step, 0)
    for head in range(GROUP):
        out = acc[head] / total[head : head + 1, :]
        out_ref[:, head * HEAD_DIM : (head + 1) * HEAD_DIM] = out.T.astype(BF)
    total_ref[0] = peak[...] + jnp.log(total[...])


def attend_one(me_row, q, k, v, query_row, key_col, rows, group):
    length = k.shape[1]
    width = GROUP * HEAD_DIM
    head = pl.BlockSpec((1, length, HEAD_DIM), lambda g, i, me: (group, 0, 0))
    return call(
        functools.partial(attend_one_kernel, rows), (1, length // rows),
        [
            pl.BlockSpec((rows, width), lambda g, i, me: (i ^ me[0], group)),
            head,
            head,
            pl.BlockSpec((1, rows), lambda g, i, me: (0, i ^ me[0])),
            fixed((length, 1)),
        ],
        [
            pl.BlockSpec((rows, width), lambda g, i, me: (i ^ me[0], 0)),
            pl.BlockSpec((1, GROUP, rows), lambda g, i, me: (0, 0, i ^ me[0])),
        ],
        [shape_of((length, width)), shape_of((1, GROUP, length), F32)],
        (me_row, q, k, v, query_row, key_col), "attend", flops=2.6e10, moved=1 << 22, prefetch=1,
        scratch=[
            pltpu.VMEM((HEAD_DIM, length), BF),
            pltpu.VMEM((GROUP, rows), F32),
            pltpu.VMEM((GROUP, rows), F32),
            pltpu.VMEM((GROUP, HEAD_DIM, rows), F32),
        ],
    )


def leave_kernel(groups, per, tiles, core_ref, x_ref, gain_ref, *refs):
    heads, weights, (normed_ref, attn_ref) = refs[: 5 * groups], refs[5 * groups : 5 * groups + 7], refs[5 * groups + 7 :]
    index = pl.program_id(0)
    stored = ((index // per) ^ 3) * per + index % per
    is_low = stored < tiles // 2
    attn, mine, other = None, 0.0, 0.0
    for k in range(4):
        parts = [
            heads[5 * g + k][...] if k < 3 else jnp.where(is_low, heads[5 * g + 3][...], heads[5 * g + 4][...])
            for g in range(groups)
        ]
        part = jnp.concatenate(parts, axis=1)
        if k == 0:
            attn = dot(part, weights[0][...], NT)
        else:
            mine = mine + dot(part, weights[k][...], NT)
            other = other + dot(part, weights[3 + k][...], NT)
    attn = attn + in_order(core_ref[0], mine, other)
    middle = x_ref[...].astype(F32) + attn
    inv = lax.rsqrt(jnp.mean(middle * middle, axis=-1, keepdims=True) + EPSILON)
    normed_ref[...] = (middle * inv * gain_ref[...]).astype(BF)

    @pl.when(index < per)
    def _():
        attn_ref[...] = attn


def weight_specs(weights):
    plain = [fixed(w.shape, 1) for w in weights if len(w.shape) == 2]
    stacked = [w.shape[1:] for w in weights if len(w.shape) == 3]
    return plain + [
        pl.BlockSpec((None,) + shape, lambda *_, k=k: (k, 0, 0), pipeline_mode=pl.Buffered(1))
        for shape in stacked
        for k in range(3)
    ]


def weight_args(weights):
    return [w for w in weights for _ in range(3 if len(w.shape) == 3 else 1)]


def leave(core_row, x_all, gain_row, heads, weights, rows):
    length = x_all.shape[0]
    per, tiles = rows // TILE, length // TILE
    by_row = pl.BlockSpec((TILE, D), lambda i, core: (i, 0))

    def head_spec(k, low, high, width):
        return pl.BlockSpec(
            (TILE, width), lambda i, core: (jnp.clip(((i // per) ^ k) * per + i % per - low, 0, high - low - 1), 0)
        )

    specs = []
    for pieces in heads:
        width = pieces[0].shape[1]
        for k in range(3):
            specs.append(head_spec(k, 0, tiles, width))
        specs += [head_spec(3, 0, tiles // 2, width), head_spec(3, tiles // 2, tiles, width)]
    return call(
        functools.partial(leave_kernel, len(heads), per, tiles), (tiles,),
        [by_row, fixed((1, D))] + specs + weight_specs(weights),
        [by_row, pl.BlockSpec((TILE, D), lambda i, core: (jnp.minimum(i, per - 1), 0))],
        [shape_of((length, D)), shape_of((rows, D), F32)],
        (core_row, x_all, gain_row, *[p for pieces in heads for p in pieces], *weight_args(weights)), "leave",
        flops=2 * length * D * D, moved=length * D * 8, prefetch=1,
    )


def up_kernel(normed_ref, gate_ref, up_ref, grad_ref, act_ref, grad_gate_ref, grad_up_ref):
    normed = normed_ref[...]
    for start in range(0, act_ref.shape[1], 256):
        part = slice(start, start + 256)
        gate = dot(normed, gate_ref[:, part])
        up = dot(normed, up_ref[:, part])
        grad = grad_ref[:, part].astype(F32)
        sigmoid = jax.nn.sigmoid(gate)
        silu = gate * sigmoid
        act_ref[:, part] = (silu * up).astype(BF)
        grad_gate_ref[:, part] = (grad * up * (sigmoid + silu * (1.0 - sigmoid))).astype(BF)
        grad_up_ref[:, part] = (grad * silu).astype(BF)


def up_project(normed, gate_up, grad_act, chunk):
    length, width = normed.shape[0], gate_up.shape[1] // 2
    tall, wide = 1024, 512
    across = width // wide
    out = pl.BlockSpec((tall, wide), lambda i, j: (i, j))
    return call(
        up_kernel, (length // tall, across),
        [
            pl.BlockSpec((tall, D), lambda i, j: (i, 0)),
            pl.BlockSpec((D, wide), lambda i, j: (0, j)),
            pl.BlockSpec((D, wide), lambda i, j: (0, across + j)),
            pl.BlockSpec((tall, wide), lambda i, j: (i, chunk * across + j)),
        ],
        [out] * 3, [shape_of((length, width))] * 3, (normed, gate_up, gate_up, grad_act), "up_project",
        flops=4 * length * D * width, moved=length * (D + 4 * width) * 2 + 8 * D * width,
    )


def sum_kernel(places, count, *refs):
    total = None
    for i in range(0, 2 * count, 2):
        part = dot(refs[i][...], refs[i + 1][...], NT)
        total = part if total is None else total + part
    total = total.astype(BF)
    for (tile, start, size), ref in zip(places, refs[2 * count :]):

        @pl.when(pl.program_id(0) == tile)
        def _(start=start, size=size, ref=ref):
            ref[...] = total[start : start + size]


def sum_of(terms, first, rows, halves):
    tall, wide = 512, 512
    specs, args = [], []
    for left, right, column in terms:
        width = left.shape[1]
        specs.append(pl.BlockSpec((tall, width), lambda i, j: (first // tall + i, 0)))
        specs.append(pl.BlockSpec((wide, width), lambda i, j, column=column: (j, column)))
        args += [left, right]
    size = tall // 2 if halves else tall
    places = [(i, start, size) for i in range(rows // tall) for start in range(0, tall, size)]
    last = D // wide - 1
    depth = sum(left.shape[1] for left, _, _ in terms)

    def out_spec(tile):
        return pl.BlockSpec((size, wide), lambda i, j: (0, jnp.where(i == tile, j, jnp.where(i < tile, 0, last))))

    return call(
        functools.partial(sum_kernel, places, len(terms)), (rows // tall, D // wide), specs,
        [out_spec(tile) for tile, _, _ in places], [shape_of((size, D))] * len(places), args, "sum_of",
        flops=2 * rows * D * depth, moved=2 * depth * (rows + D) + 2 * rows * D,
    )


def outer_kernel(across, count, left_ref, *refs):
    for k in range(count):

        @pl.when(pl.program_id(1) // across == k)
        def _(k=k):
            refs[-1][...] = dot(left_ref[...], refs[k][...], TN).astype(BF)


def outer(left, rights, wide, total=None):
    length, tall, width = left.shape[0], left.shape[1], rights[0].shape[1]
    across, count = width // wide, len(rights)
    right_spec = lambda k: pl.BlockSpec((length, wide), lambda i, j: (0, jnp.clip(j - k * across, 0, across - 1)))
    return call(
        functools.partial(outer_kernel, across, count), (left.shape[1] // tall, across * count),
        [pl.BlockSpec((length, tall), lambda i, j: (0, i))] + [right_spec(k) for k in range(count)],
        pl.BlockSpec((tall, wide), lambda i, j: (i, j)), shape_of((left.shape[1], total or width * count)),
        (left, *rights), "outer", flops=2 * length * left.shape[1] * width * count,
        moved=2 * (length + left.shape[1]) * (left.shape[1] + width * count),
    )


def outer_local_kernel(groups, left_ref, *refs):
    for k in range(4):

        @pl.when(pl.program_id(1) == k)
        def _(k=k):
            right = jnp.concatenate([refs[4 * g + k][...] for g in range(groups)], axis=1)
            refs[-1][...] = dot(left_ref[...], right, TN).astype(BF)


def outer_local(left, heads):
    rows, width, tall = left.shape[0], heads[0][0].shape[1], 1024
    specs, args = [], []
    for pieces in heads:
        for k, piece, block in ((0, pieces[0], 0), (1, pieces[1], 1), (2, pieces[2], 2), (3, pieces[4], 1)):
            specs.append(pl.BlockSpec((rows, width), lambda i, k, block=block: (block, 0)))
            args.append(piece)
    across = width * len(heads)
    return call(
        functools.partial(outer_local_kernel, len(heads)), (D // tall, 4),
        [pl.BlockSpec((rows, tall), lambda i, k: (0, i))] + specs, pl.BlockSpec((tall, across), lambda i, k: (i, k)),
        shape_of((D, 4 * across)), (left, *args), "outer_local", flops=8 * rows * D * across,
        moved=2 * D * (rows + 4 * across),
    )


def outer_rows_kernel(count, *refs):
    for k in range(count):

        @pl.when(pl.program_id(0) == k)
        def _(k=k):
            refs[-1][...] = dot(refs[k][...], refs[count][...], TN).astype(BF)


def outer_rows(lefts, right, shard):
    length, width = lefts[0].shape
    count, shards = len(lefts), right.shape[1] // shard
    return call(
        functools.partial(outer_rows_kernel, count), (count, shards),
        [pl.BlockSpec((length, width), lambda f, s: (0, 0))] * count + [pl.BlockSpec((length, shard), lambda f, s: (0, s))],
        pl.BlockSpec((width, shard), lambda f, s: (s * count + f, 0)), shape_of((shards * count * width, shard)),
        (*lefts, right), "outer_rows", flops=2 * length * right.shape[1] * width * count,
        moved=2 * (length + right.shape[1]) * width * count,
    )


def two_halves(refs):
    return jnp.where(pl.program_id(0) == 0, refs[0][...], refs[1][...]).astype(F32)


def turn_back_kernel(core_ref, own_ref, x_low, x_high, y_low, y_high, x_ref, attn_ref, cot_ref, valid_ref, gain_ref, *refs):
    weights, (middle_ref, low_ref, heads_ref) = refs[:7], refs[7:]
    grad = own_ref[...].astype(F32) + two_halves((x_low, x_high)) + two_halves((y_low, y_high))
    middle = x_ref[...].astype(F32) + attn_ref[...]
    inv = lax.rsqrt(jnp.mean(middle * middle, axis=-1, keepdims=True) + EPSILON)
    grad_middle = cot_ref[...].astype(F32) * valid_ref[...] + norm_back(grad, middle, inv, gain_ref[...])
    middle_ref[...] = grad_middle
    low = grad_middle.astype(BF)
    low_ref[...] = low
    first, second = low[:, : D // 2], low[:, D // 2 :]
    mine = jnp.where(core_ref[0] == 0, first, second)
    other = jnp.where(core_ref[0] == 0, second, first)
    heads_ref[0] = dot(low, weights[0][...]).astype(BF)
    for k in range(1, 4):
        heads_ref[k] = (dot(mine, weights[k][...]) + dot(other, weights[3 + k][...])).astype(BF)


def turn_back(core_row, own, terms, x, attn, cot, valid_col, gain_row, weights):
    rows, width = x.shape[0], weights[0].shape[1]
    by_row = lambda w: pl.BlockSpec((TILE, w), lambda i, core: (i, 0))
    return call(
        turn_back_kernel, (rows // TILE,),
        [by_row(D)] + [fixed((TILE, D))] * 4 + [by_row(D)] * 3 + [by_row(1), fixed((1, D))] + weight_specs(weights),
        [by_row(D), by_row(D), pl.BlockSpec((4, TILE, width), lambda i, core: (0, i, 0))],
        [shape_of((rows, D), F32), shape_of((rows, D)), shape_of((4, rows, width))],
        (core_row, own, *terms, x, attn, cot, valid_col, gain_row, *weight_args(weights)), "turn_back",
        flops=8 * rows * D * width, moved=rows * D * 20, prefetch=1,
    )


def last_kernel(own_ref, by_x_ref, by_y_ref, x_ref, attn_ref, valid_ref, out_ref, stats_ref):
    mlp = own_ref[...].astype(F32) + by_x_ref[...].astype(F32) + by_y_ref[...].astype(F32)
    x, attn, valid = x_ref[...].astype(F32), attn_ref[...], valid_ref[...]
    middle = x + attn
    final = middle + mlp
    out_ref[...] = final.astype(BF)

    @pl.when(pl.program_id(0) == 0)
    def _():
        stats_ref[...] = jnp.zeros(stats_ref.shape, F32)

    for row, part in enumerate((x, middle, final, attn, mlp)):
        stats_ref[row : row + 1, :] += fold(jnp.sum(valid * part * part, axis=0, keepdims=True))


def last(own, by_x, by_y, x, attn, valid_col):
    rows = x.shape[0]
    by_row = lambda w: pl.BlockSpec((TILE, w), lambda i: (i, 0))
    return call(
        last_kernel, (rows // TILE,), [by_row(D)] * 5 + [by_row(1)], [by_row(D), fixed((8, LANES))],
        [shape_of((rows, D)), shape_of((8, LANES), F32)], (own, by_x, by_y, x, attn, valid_col), "last",
        moved=rows * D * 20,
    )


def attend_back_one_kernel(rows, count, me_ref, *refs):
    q_ref, k_ref, v_ref, out_ref, own, by_x, by_y, by_xy, total_ref, query_row_ref, key_col_ref = refs[:11]
    cos_ref, sin_ref, cos_t_ref, sin_t_ref, dqkv_ref, grad_ref, k_t, inner, dq_t, dk_acc, dv_acc = refs[11:]
    me = me_ref[0]
    half, width = HEAD_DIM // 2, GROUP * HEAD_DIM
    for block, ref in enumerate((own, by_x, by_y, by_xy)):
        grad_ref[block * rows : (block + 1) * rows, :] = ref[...] if len(ref.shape) == 2 else ref[0]
    k_t[...] = k_ref[0].astype(F32).T.astype(BF)
    dq_t[...] = jnp.zeros(dq_t.shape, F32)

    def prepare(i, _):
        here = pl.ds(pl.multiple_of(i * rows, rows), rows)
        for head in range(GROUP):
            cols = slice(head * HEAD_DIM, (head + 1) * HEAD_DIM)
            both = out_ref[here, cols].astype(F32) * grad_ref[here, cols].astype(F32)
            inner[head : head + 1, here] = jnp.sum(both.T, axis=0, keepdims=True)
        return 0

    lax.fori_loop(0, count, prepare, 0)

    def visit(key_at, size, local, query_at, first, diagonal):
        keys_here = pl.ds(key_at, size)
        here = pl.ds(pl.multiple_of(query_at + first, rows // 2), rows - first)
        keys, values, keys_t = k_ref[0, keys_here, :], v_ref[0, keys_here, :], k_t[:, keys_here]
        bias = allowed_bias(rows, size, first, query_row_ref[:, here], key_col_ref[keys_here, :], diagonal)
        for head in range(GROUP):
            cols = slice(head * HEAD_DIM, (head + 1) * HEAD_DIM)
            query, grad = q_ref[here, cols], grad_ref[here, cols]
            probs = jnp.exp(dot(keys, query, NT) + bias - total_ref[0, head : head + 1, here])
            dv_acc[local : local + size, :] += dot(probs.astype(BF), grad)
            grad_probs = dot(values, grad, NT)
            grad_scores = (probs * (grad_probs - inner[head : head + 1, here])).astype(BF)
            dk_acc[local : local + size, :] += dot(grad_scores, query)
            dq_t[head, :, here] += dot(keys_t, grad_scores)

    def key_step(j, _):
        key_start = pl.multiple_of((j ^ me) * rows, rows)
        key_at = pl.ds(key_start, rows)
        dk_acc[...] = jnp.zeros(dk_acc.shape, F32)
        dv_acc[...] = jnp.zeros(dv_acc.shape, F32)
        visit(key_start, rows // 2, 0, key_start, 0, True)
        visit(pl.multiple_of(key_start + rows // 2, rows // 2), rows // 2, rows // 2, key_start, rows // 2, True)

        def query_step(i, _):
            visit(key_start, rows, 0, pl.multiple_of((i ^ me) * rows, rows), 0, False)
            return 0

        lax.fori_loop(j + 1, count, query_step, 0)
        dk = dk_acc[...]
        low, high = dk[:, :half], dk[:, half:]
        cosine, sine = cos_ref[key_at, :half], sin_ref[key_at, half:HEAD_DIM]
        turned = jnp.concatenate([low * cosine + high * sine, high * cosine - low * sine], axis=1)
        dqkv_ref[key_at, width : width + HEAD_DIM] = turned.astype(BF)
        dqkv_ref[key_at, width + HEAD_DIM :] = dv_acc[...].astype(BF)
        return 0

    lax.fori_loop(0, count, key_step, 0)

    def finish_queries(i, _):
        here = pl.ds(pl.multiple_of(i * rows, rows), rows)
        cosine, sine = cos_t_ref[:, here], sin_t_ref[:, here]
        for head in range(GROUP):
            low, high = dq_t[head, :half, here], dq_t[head, half:, here]
            turned = jnp.concatenate([low * cosine + high * sine, high * cosine - low * sine], axis=0) * SCALE
            dqkv_ref[here, head * HEAD_DIM : (head + 1) * HEAD_DIM] = turned.T.astype(BF)
        return 0

    lax.fori_loop(0, count, finish_queries, 0)


def attend_back_one(me_row, q, k, v, out, grads, totals, query_row, key_col, tables, rows, group):
    length = k.shape[1]
    width = GROUP * HEAD_DIM
    whole = lambda shape: fixed(shape, 1)
    head = pl.BlockSpec((1, length, HEAD_DIM), lambda i, me: (group, 0, 0), pipeline_mode=pl.Buffered(1))
    part = pl.BlockSpec((rows, width), lambda i, me: (0, group))
    own = pl.BlockSpec((1, rows, width), lambda i, me: (0, 0, group))
    out_width = width + 2 * HEAD_DIM
    return call(
        functools.partial(attend_back_one_kernel, rows, length // rows), (1,),
        [
            pl.BlockSpec((length, width), lambda i, me: (0, group)), head, head, whole((length, width)),
            own, part, part, part, whole((1, GROUP, length)), whole((1, length)), whole((length, 1)),
            whole((length, LANES)), whole((length, LANES)),
            whole((HEAD_DIM // 2, length)), whole((HEAD_DIM // 2, length)),
        ],
        whole((length, out_width)), shape_of((length, out_width)),
        (me_row, q, k, v, out, *grads, totals, query_row, key_col, *tables), "attend_back",
        flops=3.4e10, moved=1 << 22, prefetch=1,
        scratch=[
            pltpu.VMEM((length, width), BF),
            pltpu.VMEM((HEAD_DIM, length), BF),
            pltpu.VMEM((GROUP, length), F32),
            pltpu.VMEM((GROUP, HEAD_DIM, length), F32),
            pltpu.VMEM((rows, HEAD_DIM), F32),
            pltpu.VMEM((rows, HEAD_DIM), F32),
        ],
    )


def finish_kernel(groups, step, core_ref, x_ref, middle_ref, gain_ref, *refs):
    grads, weights, out_ref = refs[: 4 * groups], refs[4 * groups : 4 * groups + 7], refs[-1]
    grad, mine, other = None, 0.0, 0.0
    for k in range(4):
        low = jnp.concatenate([grads[4 * g + k][...] for g in range(groups)], axis=1)
        if k == 0:
            grad = dot(low, weights[0][:, : groups * step], NT)
        else:
            mine = mine + dot(low, weights[k][...], NT)
            other = other + dot(low, weights[3 + k][...], NT)
    grad = grad + in_order(core_ref[0], mine, other)
    x = x_ref[...].astype(F32)
    inv = lax.rsqrt(jnp.mean(x * x, axis=-1, keepdims=True) + EPSILON)
    out_ref[...] = (middle_ref[...] + norm_back(grad, x, inv, gain_ref[...])).astype(BF)


def finish(core_row, x, grad_middle, gain_row, grads, weights):
    rows, step = x.shape[0], grads[0][0].shape[1]
    by_row = lambda w: pl.BlockSpec((TILE, w), lambda i, core: (i, 0))
    return call(
        functools.partial(finish_kernel, len(grads), step), (rows // TILE,),
        [by_row(D), by_row(D), fixed((1, D))] + [by_row(step)] * (4 * len(grads)) + weight_specs(weights),
        by_row(D), shape_of((rows, D)),
        (core_row, x, grad_middle, gain_row, *[p for parts in grads for p in parts], *weight_args(weights)), "finish",
        flops=8 * rows * D * step * len(grads), moved=rows * D * 8 + 4 * D * step * 4, prefetch=1,
    )


def each_piece(refs, emit):
    block = pl.program_id(0)
    for k in range(3):

        @pl.when(block == k)
        def _(k=k):
            emit(refs[k][...])

    @pl.when(block == 3)
    def _():
        emit(jnp.concatenate([refs[3][...], refs[4][...]], axis=0))


def fold(values):
    return sum(values[:, at : at + LANES] for at in range(0, values.shape[1], LANES))


def place_pair_kernel(first, me_ref, *refs):
    pieces, weight_a, weight_b = refs[:5], refs[5], refs[6]
    out_a, out_b, dot_ref = refs[-3:]
    width = out_a.shape[1]

    @pl.when(pl.program_id(0) == 0)
    def _():
        dot_ref[...] = jnp.zeros(dot_ref.shape, F32) if first else refs[9][...]

    def emit(values):
        a, b = values[:, :width].astype(F32), values[:, width:].astype(F32)
        out_a[...], out_b[...] = a, b
        dot_ref[...] += fold(a * weight_a[...].astype(F32)) + fold(b * weight_b[...].astype(F32))

    each_piece(pieces, emit)


def place_pair(me_row, pieces, weight_a, weight_b, chunks, chunk, before):
    rows, total = weight_a.shape
    width = pieces[0].shape[1] // 2
    column = pl.BlockSpec((rows, width), lambda i, me: (0, (i ^ me[0]) * chunks + chunk))
    any_spec = pl.BlockSpec(memory_space=pl.ANY)
    specs = [fixed(p.shape) for p in pieces] + [column, column]
    args = [me_row, *pieces, weight_a, weight_b]
    aliases = {}
    if before is not None:
        specs += [any_spec, any_spec, fixed((rows, LANES))]
        args += before
        aliases = {8: 0, 9: 1}
    return call(
        functools.partial(place_pair_kernel, before is None), (4,), specs, [column, column, fixed((rows, LANES))],
        [shape_of((rows, total), F32)] * 2 + [shape_of((rows, LANES), F32)], args, "place_pair",
        moved=rows * width * 64, prefetch=1, aliases=aliases,
    )


def place_rows_kernel(half, me_ref, *refs):
    block, tile = pl.program_id(0), pl.program_id(1)
    for k in range(5):
        first = jnp.minimum(block, 3) == min(k, 3)

        @pl.when(first if k < 3 else first & ((tile < half) == (k == 3)))
        def _(k=k):
            refs[5][...] = refs[k][...].astype(F32)


def place_rows(me_row, pieces, tall):
    rows, columns = pieces[0].shape
    across = rows // tall
    half = across // 2

    def spec(k):
        if k < 3:
            return pl.BlockSpec((tall, columns), lambda i, j, me: (jnp.where(i == k, j, 0), 0))
        low = (k - 3) * half
        return pl.BlockSpec((tall, columns), lambda i, j, me: (jnp.where(i == 3, jnp.clip(j - low, 0, half - 1), 0), 0))

    return call(
        functools.partial(place_rows_kernel, half), (4, across), [spec(k) for k in range(5)],
        pl.BlockSpec((tall, columns), lambda i, j, me: ((i ^ me[0]) * across + j, 0)),
        shape_of((4 * rows, columns), F32), (me_row, *pieces), "place_rows", moved=rows * columns * 24, prefetch=1,
    )


def place_attn_kernel(kv_local, me_ref, *refs):
    pieces, weights, outs, out_ref, dot_ref = refs[:5], refs[5:8], refs[8:11], refs[11], refs[12]
    width = GROUP * HEAD_DIM
    step = width + 2 * HEAD_DIM

    @pl.when(pl.program_id(0) == 0)
    def _():
        dot_ref[...] = jnp.zeros(dot_ref.shape, F32)

    def emit(values):
        values = values.astype(F32)
        take = lambda start, size: jnp.concatenate(
            [values[:, g * step + start : g * step + start + size] for g in range(kv_local)], axis=1
        )
        parts = (take(0, width), take(width, HEAD_DIM), take(width + HEAD_DIM, HEAD_DIM))
        for part, weight, out in zip(parts, weights, outs):
            out[...] = part
            dot_ref[...] += fold(part * weight[...].astype(F32))
        out_ref[...] = values[:, kv_local * step :].T

    each_piece(pieces, emit)


def place_attn(me_row, pieces, query_weight, key_weight, value_weight, kv_local):
    rows = query_weight.shape[0]
    q_width = kv_local * GROUP * HEAD_DIM
    column = lambda width: pl.BlockSpec((rows, width), lambda i, me: (0, i ^ me[0]))
    columns = [column(q_width), column(kv_local * HEAD_DIM), column(kv_local * HEAD_DIM)]
    weights = (query_weight, key_weight, value_weight)
    return call(
        functools.partial(place_attn_kernel, kv_local), (4,), [fixed(p.shape) for p in pieces] + columns,
        columns + [pl.BlockSpec((q_width, rows), lambda i, me: (i ^ me[0], 0)), fixed((rows, LANES))],
        [shape_of(w.shape, F32) for w in weights] + [shape_of((4 * q_width, rows), F32), shape_of((rows, LANES), F32)],
        (me_row, *pieces, *weights), "place_attn", moved=rows * 5120 * 8, prefetch=1,
    )


CHUNKS = 2


def square_body(
    inputs, cotangent, segments, valid_mask, query_weight, key_weight, value_weight, out_weight,
    gate_weight, up_weight, down_weight, attn_gain, mlp_gain,
):
    count = 4
    me = lax.axis_index("seq")
    me_row = me.reshape(1).astype(jnp.int32)
    core = lax.axis_index("fsdp") % 2
    core_row = core.reshape(1).astype(jnp.int32)
    rows = inputs.shape[1]
    length = rows * count
    kv_local = KV_HEADS // count
    q_width = kv_local * GROUP * HEAD_DIM
    ff_local = FF // count
    ff_chunk = ff_local // CHUNKS
    shard_rows = gate_weight.shape[0]
    step = (GROUP + 2) * HEAD_DIM

    tokens_low, cot_low = inputs[0], cotangent[0]
    marks = jnp.stack([segments[0], valid_mask[0]])
    marks_all = jnp.stack([marks] + [swap(marks, k) for k in range(1, count)])
    x_own = after(tokens_low, marks_all)
    x_x, x_y = to_both(x_own)

    segment_all = marks_all[:, 0].reshape(length)
    valid_all = marks_all[:, 1].reshape(length)
    valid_col = valid_mask[0].astype(F32)[:, None]

    position = (
        (jnp.arange(count, dtype=jnp.int32) ^ me)[:, None] * rows + jnp.arange(rows, dtype=jnp.int32)[None, :]
    ).reshape(length)
    same = (segment_all[:, None] == segment_all[None, :]) & (position[None, :] < position[:, None])
    places = jnp.sum(same.astype(jnp.int32), axis=1).astype(F32)
    half = HEAD_DIM // 2
    frequency = ROPE_BASE ** (-2.0 * jnp.arange(half, dtype=F32) / HEAD_DIM)
    angles_t = frequency[:, None] * places[None, :]
    cosine_t, sine_t = jnp.cos(angles_t), jnp.sin(angles_t)
    cosine = jnp.tile(cosine_t.T, (1, LANES // half))
    sign = jnp.tile(jnp.repeat(jnp.array([-1.0, 1.0], F32), half), LANES // HEAD_DIM)
    sine = jnp.tile(sine_t.T, (1, LANES // half)) * sign[None, :]
    query_row = jnp.where(valid_all == 1, segment_all, -1).reshape(1, length)
    key_col = segment_all.reshape(length, 1)
    tables = (cosine, sine, cosine_t, sine_t)

    gains = jnp.pad(jnp.stack([attn_gain, mlp_gain], axis=1), ((0, 0), (0, LANES - 2)))
    qkv_full = gather_fsdp(pack_qkv(me_row, query_weight, key_weight, value_weight, gains, kv_local))
    out_slice = gather_fsdp(pack_rows(me_row, out_weight, q_width))
    gain_one = qkv_full[:, kv_local * step].astype(F32).reshape(1, D)
    gain_two = qkv_full[:, kv_local * step + 1].astype(F32).reshape(1, D)

    x_far = pass_on(x_x, x_y, cosine, sine)
    entered = enter([x_own, x_x, x_y], gain_one, qkv_full, cosine, sine, kv_local, 0, length)

    down_t = gather_fsdp(pack_rows(me_row, after(down_weight, x_x, x_y, cosine, sine), ff_local))
    later_gate = after(gate_weight, x_x, x_y, cosine, sine)
    gate_up = [
        gather_fsdp(pack_pair(me_row, later_gate, up_weight, CHUNKS, c, ff_chunk)) for c in range(CHUNKS)
    ]

    done = (*x_far, entered[0])
    o_mine = [swap(core_half(after(out_slice, *done), core), k) for k in range(1, count)]
    grad_low = (cot_low.astype(F32) * valid_col).astype(BF)
    x_all, normed_one, q, k, v = enter(
        list(x_far), gain_one, qkv_full, cosine, sine, kv_local, 3 * rows, length, tuple(entered)
    )
    out_0, total_0 = attend_one(me_row, q, k, v, query_row, key_col, rows, 0)

    done = (*o_mine, out_0)
    h_x, h_y = to_both(after(out_0, *done))
    o_other = swap_core(jnp.stack([after(w, *done) for w in o_mine]))
    out_pieces = [out_slice, *o_mine, o_other]
    out_1, total_1 = attend_one(me_row, after(q, *done), k, v, query_row, key_col, rows, 1)
    heads, totals = [out_0, out_1], [total_0, total_1]

    done = (h_x, h_y, out_1, o_other)
    h_far = pass_on(h_x, h_y, *done)
    heads_0 = [out_0, h_x, h_y, *h_far]
    h_x, h_y = to_both(after(out_1, *done))

    done = (*h_far, h_x, h_y)
    h_far = pass_on(h_x, h_y, *done)
    heads_1 = [out_1, h_x, h_y, *h_far]
    c_own = after(grad_low, *done)
    c_x, c_y = to_both(c_own)
    normed_two, attn_branch = leave(core_row, after(x_all, *h_far), gain_two, [heads_0, heads_1], out_pieces, rows)

    done = (c_x, c_y, normed_two, down_t)
    c_far = pass_on(c_x, c_y, *done)
    acted = act_back([after(c_own, *done), c_x, c_y], down_t, 0, length)

    done = (*c_far, acted[0])
    w_mine = [swap(core_half(after(qkv_full, *done)[:, : kv_local * step], core), k) for k in range(1, count)]
    grad_mlp, grad_act = act_back(list(c_far), down_t, 3 * rows, length, tuple(acted))
    act_0, gate_0, up_0 = up_project(normed_two, gate_up[0], grad_act, 0)
    grad_0 = outer(normed_two, [gate_0, up_0], 512)

    done = (*w_mine, grad_0)
    gate_up_0 = scatter_fsdp(after(grad_0, *done))
    w_other = [swap_core(after(w, *done)) for w in w_mine]
    weight_pieces = [qkv_full, *w_mine, *w_other]
    act_1, gate_1, up_1 = up_project(after(normed_two, *done), gate_up[1], grad_act, 1)
    terms = [(gate_0, gate_up[0], 0), (up_0, gate_up[0], 1), (gate_1, gate_up[1], 0), (up_1, gate_up[1], 1)]

    def terms_after(*events):
        return [(after(terms[0][0], *events), *terms[0][1:])] + terms[1:]

    far = sum_of(terms, 3 * rows, rows, True)

    done = (*far, *w_other)
    g_far = send_far(*far)
    near = sum_of(terms_after(*done), rows, 2 * rows, True)
    near = add_far(near, *g_far)
    g_near = send_near(near)
    [own] = sum_of(terms_after(*near), 0, rows, False)
    grad_1 = outer(after(normed_two, own), [gate_1, up_1], 512)
    gate_up_1 = scatter_fsdp(after(grad_1, *g_near))
    grad_middle, grad_attn, grad_heads = turn_back(
        core_row, after(own, grad_1), g_near, tokens_low, attn_branch, cot_low, valid_col, gain_two, out_pieces
    )

    head_grads = [grad_heads] + [swap(grad_heads[k], k) for k in range(1, count)]
    p_own = after(gate_up_0, grad_attn)
    p_x, p_y = to_both(p_own)
    grad_down = outer_rows([act_0, act_1], after(grad_mlp, grad_attn), shard_rows)
    grad_out = outer_local(after(grad_attn, grad_down), [heads_0, heads_1])

    def attention_back(queries, group):
        return attend_back_one(
            me_row, queries, k, v, heads[group], head_grads, totals[group], query_row, key_col, tables, rows, group
        )

    done = (*head_grads[1:], p_x, p_y, grad_out)
    out_sum = scatter_fsdp(after(grad_out, *done))
    p_far = pass_on(p_x, p_y, *done)
    p_pieces = [p_own, p_x, p_y, *p_far]
    dqkv_0 = attention_back(after(q, *done), 0)

    done = (*p_far, dqkv_0)
    down_sum = scatter_fsdp(after(grad_down, *done))
    p_own = after(gate_up_1, *done)
    p_x, p_y = to_both(p_own)
    parts_0 = exchange_seq(blocks_of(after(dqkv_0, *done), count))
    dqkv_1 = attention_back(after(q, *done), 1)

    done = (p_x, p_y, *parts_0[1:], dqkv_1)
    parts_1 = exchange_seq(blocks_of(after(dqkv_1, *done), count))
    terms = [(act_0, down_t, 0), (act_1, down_t, 1)]
    far = sum_of(terms_after(*done), 3 * rows, rows, True)
    m_far = send_far(*far)
    near = sum_of(terms_after(*far, *parts_1[1:]), rows, 2 * rows, True)

    near = add_far(near, *m_far)
    near = [jnp.concatenate(near[:2]), jnp.concatenate(near[2:])]
    done = (*near, *parts_1[1:])
    m_x, m_y = swap(near[0], 1), swap(near[1], 2)
    p_far = pass_on(p_x, p_y, *done)
    grad_qkv = outer(after(normed_one, *done), [dqkv_0, dqkv_1], step)
    [own] = sum_of(terms_after(grad_qkv), 0, rows, False)
    input_grad = finish(core_row, after(tokens_low, own), grad_middle, gain_one, [parts_0, parts_1], weight_pieces)

    done = (m_x, m_y, *p_far, input_grad)
    qkv_sum = scatter_fsdp(after(grad_qkv, *done))
    input_grad = input_grad[None]
    out_ready = after(out_sum, *done)
    out_terms = exchange_seq([out_ready[:, k * q_width : (k + 1) * q_width] for k in range(count)])
    outputs, stats = last(after(own, *done), m_x, m_y, tokens_low, attn_branch, valid_col)
    outputs = outputs[None]
    placed = place_pair(me_row, [after(p_pieces[0], stats)] + p_pieces[1:], gate_weight, up_weight, CHUNKS, 0, None)

    done = (*out_terms[1:], placed[2])
    out_sum = sum(term.astype(F32) for term in out_terms).astype(BF)
    d_own = after(down_sum, *done)
    d_x, d_y = to_both(d_own)
    gate_grad, up_grad, gate_up_dot = place_pair(
        me_row, [after(p_own, *done), p_x, p_y, *p_far], gate_weight, up_weight, CHUNKS, 1, placed
    )

    done = (d_x, d_y, gate_up_dot)
    d_far = pass_on(d_x, d_y, *done)

    t_own = jnp.concatenate([after(qkv_sum, *d_far), out_sum], axis=1)
    t_x, t_y = to_both(t_own)
    stats = after(stats, *d_far)
    down_grad = place_rows(me_row, [after(down_sum, *d_far), d_x, d_y, *d_far], 1024)
    t_far = pass_on(t_x, t_y, t_x, t_y)
    query_grad, key_grad, value_grad, out_grad, qkv_dot = place_attn(
        me_row, [after(t_own, down_grad), t_x, t_y, *t_far], query_weight, key_weight, value_weight, kv_local
    )
    attn_gain_grad = jnp.sum(qkv_dot, axis=1) / attn_gain.astype(F32)
    mlp_gain_grad = jnp.sum(gate_up_dot, axis=1) / mlp_gain.astype(F32)

    for bit in bit_orders()[0]:
        stats = stats + swap(stats, bit)
    rms_stats = jnp.sqrt(jnp.sum(stats[:5], axis=1)[None, :] / (jnp.sum(valid_all).astype(F32) * D))
    return (
        outputs, input_grad, query_grad, key_grad, value_grad, out_grad, gate_grad, up_grad, down_grad,
        attn_gain_grad, mlp_gain_grad, rms_stats,
    )


def solution(mesh):
    rows_in = P("fsdp", None)
    columns_in = P(None, "fsdp")
    placed = (
        P("fsdp", "seq", None), P("fsdp", "seq", None), P("fsdp", "seq"), P("fsdp", "seq"),
        rows_in, rows_in, rows_in, columns_in, rows_in, rows_in, columns_in, P("fsdp"), P("fsdp"),
    )
    return jax.shard_map(
        square_body if mesh.shape["seq"] == 4 else general_body,
        mesh=mesh,
        in_specs=placed,
        out_specs=(
            P("fsdp", "seq", None), P("fsdp", "seq", None), rows_in, rows_in, rows_in, columns_in,
            rows_in, rows_in, columns_in, P("fsdp"), P("fsdp"), P("fsdp", None),
        ),
        check_vma=False,
    )
```
